32 devices in a mesh: dp: 8 (over z, x), tensor: 4 (over y, core).
Axes of the slice: x: 2, y: 2, z: 4, core: 2. Of those that a mesh axis runs over, the one named last changes fastest.
Arguments:
- tokens: bfloat16 [8, 2048, 1280], P('dp', 'tensor'), may hold values from -6 to 6
- segment_ids: int32 [8, 2048], P('dp'), may hold values from 0 to 2047, as said below
- adapter_choice: int32 [8], P('dp'), may hold values from 0 to 7, as said below
- cotangent: bfloat16 [8, 2048, 1280], P('dp', 'tensor'), may hold values from -6 to 6
- weight_query: bfloat16 [1280, 1280], P(None, 'tensor'), may hold values from -0.15625 to 0.15625
- weight_key: bfloat16 [1280, 1280], P(None, 'tensor'), may hold values from -0.15625 to 0.15625
- weight_value: bfloat16 [1280, 1280], P(None, 'tensor'), may hold values from -0.15625 to 0.15625
- weight_output: bfloat16 [1280, 1280], P(None, 'tensor'), may hold values from -0.625 to 0.625
- weight_upward: bfloat16 [1280, 1280], P(None, 'tensor'), may hold values from -0.15625 to 0.15625
- weight_downward: bfloat16 [1280, 1280], P(None, 'tensor'), may hold values from -0.15625 to 0.15625
- query_lower: bfloat16 [8, 16, 1280], replicated, may hold values from -0.15625 to 0.15625
- query_raise: bfloat16 [8, 16, 1280], P(None, None, 'tensor'), may hold values from -1.5 to 1.5
- key_lower: bfloat16 [8, 16, 1280], replicated, may hold values from -0.15625 to 0.15625
- key_raise: bfloat16 [8, 16, 1280], P(None, None, 'tensor'), may hold values from -1.5 to 1.5
- value_lower: bfloat16 [8, 16, 1280], replicated, may hold values from -0.15625 to 0.15625
- value_raise: bfloat16 [8, 16, 1280], P(None, None, 'tensor'), may hold values from -1.5 to 1.5
- output_lower: bfloat16 [8, 16, 1280], P(None, None, 'tensor'), may hold values from -0.625 to 0.625
- output_raise: bfloat16 [8, 16, 1280], replicated, may hold values from -1.5 to 1.5
- upward_lower: bfloat16 [8, 16, 1280], replicated, may hold values from -0.15625 to 0.15625
- upward_raise: bfloat16 [8, 16, 1280], P(None, None, 'tensor'), may hold values from -1.5 to 1.5
- downward_lower: bfloat16 [8, 16, 1280], P(None, None, 'tensor'), may hold values from -0.15625 to 0.15625
- downward_raise: bfloat16 [8, 16, 1280], replicated, may hold values from -1.5 to 1.5
Outputs:
- activations: bfloat16 [8, 2048, 1280], P('dp', 'tensor')
- input_grad: bfloat16 [8, 2048, 1280], P('dp', 'tensor')
- grad_query_lower: float32 [8, 16, 1280], replicated
- grad_query_raise: float32 [8, 16, 1280], P(None, None, 'tensor')
- grad_key_lower: float32 [8, 16, 1280], replicated
- grad_key_raise: float32 [8, 16, 1280], P(None, None, 'tensor')
- grad_value_lower: float32 [8, 16, 1280], replicated
- grad_value_raise: float32 [8, 16, 1280], P(None, None, 'tensor')
- grad_output_lower: float32 [8, 16, 1280], P(None, None, 'tensor')
- grad_output_raise: float32 [8, 16, 1280], replicated
- grad_upward_lower: float32 [8, 16, 1280], replicated
- grad_upward_raise: float32 [8, 16, 1280], P(None, None, 'tensor')
- grad_downward_lower: float32 [8, 16, 1280], P(None, None, 'tensor')
- grad_downward_raise: float32 [8, 16, 1280], replicated
The draws below stay inside these ranges and needn't reach their ends.
Inputs may be any that keep to these rules, and one draw needn't show every extreme that they name: `segment_ids`: in each row the document numbers start at 0 and never fall, and may skip values; the last document of each row is numbered 2048 - 1; one document of each row begins before position 512 and covers position 1536. `adapter_choice`: set 0 and set 8 - 1 are each picked by some sequence; one set among 1 to 6 is picked by no sequence.
All inputs are finite; a program needn't handle non-finite values.
Results may differ from the reference program's by a relative error of at most 0.019.
Values may be sent and summed in bfloat16 or wider, within the bound.
A program may use at most 192 MiB of HBM per device.

```python
import jax
import jax.numpy as jnp
from jax import lax

D = 1280
H = 16
HD = 80
FF = 1280
RANK = 16
SETS = 8
SEQ = 2048
SEQS = 8


def draw_segment_ids(key, part):
    key = jax.random.fold_in(key, 7)

    def one_row(row_key):
        row_keys = jax.random.split(row_key, 3)
        long_first = jax.random.randint(row_keys[0], (), 1, SEQ // 4)
        long_end = jax.random.randint(row_keys[1], (), 3 * SEQ // 4 + 1, SEQ + 1)
        places = jnp.arange(SEQ, dtype=jnp.int32)
        coin_draws = jax.random.randint(row_keys[2], (SEQ,), 0, 5)
        inside = (places > long_first) & (places < long_end)
        breaks = (coin_draws == 0) & jnp.logical_not(inside) | (places == long_first) | (places == long_end)
        breaks = breaks & (places > 0)
        counted = jnp.cumsum(breaks.astype(jnp.int32)).astype(jnp.int32)
        last_doc = counted[SEQ - 1]
        return jnp.where(counted == last_doc, SEQ - 1, counted).astype(jnp.int32)
    return jax.vmap(one_row)(jax.random.split(key, SEQS))


def draw_adapter_choice(key, part):
    key = jax.random.fold_in(key, 11)
    pick_keys = jax.random.split(key, 3)
    missing = jax.random.randint(pick_keys[0], (), 1, SETS - 1)
    raw_picks = jax.random.randint(pick_keys[1], (SEQS,), 0, SETS - 1)
    picks = raw_picks + (raw_picks >= missing).astype(jnp.int32)
    order = jax.random.permutation(pick_keys[2], SEQS)
    picks = picks.at[order[0]].set(0)
    picks = picks.at[order[1]].set(SETS - 1)
    return picks.astype(jnp.int32)


def steps_of(rng, shape, cuts, smallest, largest):
    gain, own = 1.0, jax.random.fold_in(rng, 6)
    for dim, shards_of in cuts:
        steps = jnp.exp(jax.random.uniform(jax.random.fold_in(own, dim), (shards_of,), jnp.float32, smallest / len(cuts), largest / len(cuts)))
        gain = gain * jnp.repeat(steps, shape[dim] // shards_of).reshape([-1 if axis == dim else 1 for axis in range(len(shape))])
    return gain


def gaussian(stream_key, dims, spread, reach, cuts=(), kind=jnp.bfloat16):
    gain = steps_of(stream_key, dims, cuts, -0.22, 0.18) if cuts else 1.0
    drawn = jax.random.normal(stream_key, dims, jnp.float32) * spread * gain
    return jnp.minimum(jnp.maximum(drawn, -reach), reach).astype(kind)


def setup_inputs(seed: int = 0) -> dict:
    streams_of = jax.random.split(jax.random.key(seed), 23)
    tokens = gaussian(streams_of[0], (SEQS, SEQ, D), 1.0, 6.0, ((0, 8), (1, 4)))
    segment_ids = draw_segment_ids(jax.random.fold_in(streams_of[22], 71), 0)
    adapter_choice = draw_adapter_choice(jax.random.fold_in(streams_of[22], 71), 0)
    cotangent = gaussian(streams_of[3], (SEQS, SEQ, D), 1.0, 6.0, ((0, 8), (1, 4)))
    weight_query = gaussian(streams_of[4], (D, D), D ** -0.5, 0.15625, ((1, 4),))
    weight_key = gaussian(streams_of[5], (D, D), D ** -0.5, 0.15625, ((1, 4),))
    weight_value = gaussian(streams_of[6], (D, D), D ** -0.5, 0.15625, ((1, 4),))
    weight_output = gaussian(streams_of[7], (D, D), (D // 16) ** -0.5, 0.625, ((1, 4),))
    weight_upward = gaussian(streams_of[8], (D, FF), D ** -0.5, 0.15625, ((1, 4),))
    weight_downward = gaussian(streams_of[9], (D, FF), FF ** -0.5, 0.15625, ((1, 4),))
    query_lower = gaussian(streams_of[10], (SETS, RANK, D), D ** -0.5, 0.15625)
    query_raise = gaussian(streams_of[11], (SETS, RANK, D), RANK ** -0.5, 1.5, ((2, 4),))
    key_lower = gaussian(streams_of[12], (SETS, RANK, D), D ** -0.5, 0.15625)
    key_raise = gaussian(streams_of[13], (SETS, RANK, D), RANK ** -0.5, 1.5, ((2, 4),))
    value_lower = gaussian(streams_of[14], (SETS, RANK, D), D ** -0.5, 0.15625)
    value_raise = gaussian(streams_of[15], (SETS, RANK, D), RANK ** -0.5, 1.5, ((2, 4),))
    output_lower = gaussian(streams_of[16], (SETS, RANK, D), (D // 16) ** -0.5, 0.625, ((2, 4),))
    output_raise = gaussian(streams_of[17], (SETS, RANK, D), RANK ** -0.5, 1.5)
    upward_lower = gaussian(streams_of[18], (SETS, RANK, D), D ** -0.5, 0.15625)
    upward_raise = gaussian(streams_of[19], (SETS, RANK, FF), RANK ** -0.5, 1.5, ((2, 4),))
    downward_lower = gaussian(streams_of[20], (SETS, RANK, FF), FF ** -0.5, 0.15625, ((2, 4),))
    downward_raise = gaussian(streams_of[21], (SETS, RANK, D), RANK ** -0.5, 1.5)
    return {"tokens": tokens, "segment_ids": segment_ids, "adapter_choice": adapter_choice, "cotangent": cotangent, "weight_query": weight_query, "weight_key": weight_key, "weight_value": weight_value, "weight_output": weight_output, "weight_upward": weight_upward, "weight_downward": weight_downward, "query_lower": query_lower, "query_raise": query_raise, "key_lower": key_lower, "key_raise": key_raise, "value_lower": value_lower, "value_raise": value_raise, "output_lower": output_lower, "output_raise": output_raise, "upward_lower": upward_lower, "upward_raise": upward_raise, "downward_lower": downward_lower, "downward_raise": downward_raise}


EPS = 1e-06
NEG = -1e+30
FULL_PRECISION = lax.Precision.HIGHEST

@jax.custom_vjp
def low(v):
    return lax.optimization_barrier(v.astype(jnp.bfloat16)).astype(jnp.float32)

@jax.custom_vjp
def low_back(v):
    return v

def low_keep(v):
    return (low(v), None)

def low_pass(kept, grad):
    return (grad,)

def back_keep(v):
    return (v, None)

def back_low(kept, grad):
    return (low(grad),)
low.defvjp(low_keep, low_pass)
low_back.defvjp(back_keep, back_low)

def matmul(left, right):
    return jnp.dot(left, right, precision=FULL_PRECISION)

def matmul_flip(left, right):
    return jnp.dot(left, right.T, precision=FULL_PRECISION)

def rms_unit(values):
    return values * lax.rsqrt(lax.optimization_barrier(jnp.mean(values * values, axis=-1, keepdims=True)) + EPS)

def attention(queries, keys_all, values_all, segments):
    length = queries.shape[0]
    block_rows = min(512, length)
    count = length // block_rows
    query_blocks = queries.reshape(count, block_rows, H, HD)
    keys_heads = keys_all.reshape(length, H, HD)
    values_heads = values_all.reshape(length, H, HD)
    positions = jnp.arange(length, dtype=jnp.int32)
    segment_blocks = segments.reshape(count, block_rows)
    position_blocks = positions.reshape(count, block_rows)

    def one_block(pieces):
        query_piece, segment_piece, position_piece = pieces
        products = low_back(jnp.einsum('qhd,khd->hqk', query_piece, keys_heads, precision=FULL_PRECISION))
        allowed = (segment_piece[:, None] == segments[None, :]) & (positions[None, :] <= position_piece[:, None])
        scores = jnp.where(allowed[None], products * HD ** (-0.5), NEG)
        row_max = lax.optimization_barrier(jnp.max(scores, axis=-1, keepdims=True))
        exponent = jnp.exp(scores - row_max)
        probabilities = exponent / lax.optimization_barrier(jnp.sum(exponent, axis=-1, keepdims=True))
        return jnp.einsum('hqk,khd->qhd', low(probabilities), values_heads, precision=FULL_PRECISION)
    attended = lax.map(jax.checkpoint(one_block), (query_blocks, segment_blocks, position_blocks))
    return attended.reshape(length, D)

def layer_forward(inputs, adapters, chosen, weights, segments):
    picked = [jnp.einsum('s,srd->rd', chosen, stacked, precision=FULL_PRECISION) for stacked in adapters]
    query_lower, query_raise, key_lower, key_raise, value_lower, value_raise = picked[:6]
    output_lower, output_raise, upward_lower, upward_raise, downward_lower, downward_raise = picked[6:]
    weight_query, weight_key, weight_value, weight_output, weight_upward, weight_downward = weights
    normed_in = low(rms_unit(inputs))
    queries = low(low_back(matmul(normed_in, weight_query) + matmul(low(matmul_flip(normed_in, query_lower)), query_raise)))
    keys_all = low(low_back(matmul(normed_in, weight_key) + matmul(low(matmul_flip(normed_in, key_lower)), key_raise)))
    values_all = low(low_back(matmul(normed_in, weight_value) + matmul(low(matmul_flip(normed_in, value_lower)), value_raise)))
    attended = low(low_back(attention(queries, keys_all, values_all, segments)))
    low_out = low_back(matmul_flip(attended, output_lower))
    branch = low_back(matmul_flip(attended, weight_output) + matmul(low_out, output_raise))
    middle = inputs + branch
    normed_mid = low(rms_unit(middle))
    preact = low_back(matmul(normed_mid, weight_upward) + matmul(low(matmul_flip(normed_mid, upward_lower)), upward_raise))
    activated = low(jax.nn.silu(preact))
    low_down = low_back(matmul_flip(activated, downward_lower))
    return middle + matmul_flip(activated, weight_downward) + matmul(low_down, downward_raise)

def reference(tokens, segment_ids, adapter_choice, cotangent, weight_query, weight_key, weight_value, weight_output, weight_upward, weight_downward, query_lower, query_raise, key_lower, key_raise, value_lower, value_raise, output_lower, output_raise, upward_lower, upward_raise, downward_lower, downward_raise):
    weights = tuple((matrix.astype(jnp.float32) for matrix in (weight_query, weight_key, weight_value, weight_output, weight_upward, weight_downward)))
    adapters = tuple((stacked.astype(jnp.float32) for stacked in (query_lower, query_raise, key_lower, key_raise, value_lower, value_raise, output_lower, output_raise, upward_lower, upward_raise, downward_lower, downward_raise)))

    def sequence_step(totals, sequence_items):
        inputs, segments, which, grad_out = sequence_items
        chosen = (jnp.arange(SETS, dtype=jnp.int32) == which).astype(jnp.float32)

        def forward_fn(input_rows, adapter_list):
            return layer_forward(input_rows, adapter_list, chosen, weights, segments)
        outputs, pullback = jax.vjp(forward_fn, inputs.astype(jnp.float32), adapters)
        grad_inputs, grad_adapters = pullback(grad_out.astype(jnp.float32))
        totals = tuple((running + update for running, update in zip(totals, grad_adapters)))
        return (totals, (outputs.astype(jnp.bfloat16), grad_inputs.astype(jnp.bfloat16)))
    initial = tuple((jnp.zeros(stacked.shape, jnp.float32) for stacked in adapters))
    grads, (activations, input_grad) = lax.scan(sequence_step, initial, (tokens, segment_ids, adapter_choice, cotangent))
    return (activations, input_grad, grads[0], grads[1], grads[2], grads[3], grads[4], grads[5], grads[6], grads[7], grads[8], grads[9], grads[10], grads[11])
```

```python
import functools
import math

import jax
import jax.numpy as jnp
from jax import lax
from jax.experimental import pallas as pl
from jax.experimental.pallas import tpu as pltpu
from jax.sharding import PartitionSpec as P

HD = 80
LANES = 128
EPS = 1e-06
NEG = -1e30
F32 = jnp.float32
BF16 = jnp.bfloat16
VMEM_BYTES = 60 * 2**20
SCORE_SCALE = HD ** (-0.5)
LOG2E = math.log2(math.e)
SLOT = 384

NT = (((1,), (1,)), ((), ()))
TN = (((0,), (0,)), ((), ()))


def nn(left, right):
    return jnp.dot(left, right, preferred_element_type=F32)


def nt(left, right):
    return lax.dot_general(left, right, NT, preferred_element_type=F32)


def tn(left, right):
    return lax.dot_general(left, right, TN, preferred_element_type=F32)


def params(**more):
    return pltpu.CompilerParams(vmem_limit_bytes=VMEM_BYTES, **more)


def cost(flops, nbytes):
    return pl.CostEstimate(flops=int(flops), bytes_accessed=int(nbytes), transcendentals=0)


def whole(shape):
    return pl.BlockSpec(shape, lambda *_: (0,) * len(shape))


def swap(array, axis_name, count, bit):
    return lax.ppermute(array, axis_name, [(i, i ^ bit) for i in range(count)])


def norm_kernel(choice, x_ref, ol_ref, ur_ref, dl_ref, out_ref):
    rows = x_ref.shape[0]
    x = x_ref[...].astype(F32)
    factor = lax.rsqrt(jnp.mean(x * x, axis=-1, keepdims=True) + EPS)
    out_ref[:rows] = (x * factor).astype(BF16)
    out_ref[rows:] = jnp.zeros_like(out_ref[rows:])
    width = ol_ref.shape[2]
    for slot, ref in enumerate((ol_ref, ur_ref, dl_ref)):
        out_ref[rows:, slot * SLOT : slot * SLOT + width] = ref[0]


def norm_call(x, choice, ol, ur, dl):
    rows, width = x.shape
    rank, local = ol.shape[1:]
    pick = pl.BlockSpec((1, rank, local), lambda g, c: (c[0], 0, 0))
    return pl.pallas_call(
        norm_kernel,
        grid_spec=pltpu.PrefetchScalarGridSpec(
            num_scalar_prefetch=1,
            grid=(1,),
            in_specs=[whole((rows, width)), pick, pick, pick],
            out_specs=whole((rows + rank, width)),
        ),
        out_shape=jax.ShapeDtypeStruct((rows + rank, width), BF16),
        compiler_params=params(),
        name="norm_in",
    )(choice, x, ol, ur, dl)


def prep_kernel(heads, wq, wk, wv, wo, wu, wd, pq, pk, pv, wt):
    for src, dst in ((wq, pq), (wk, pk), (wv, pv)):
        value = src[...].astype(F32)
        for h in range(heads):
            piece = value[:, h * HD : (h + 1) * HD]
            piece = jnp.concatenate(
                [piece, jnp.zeros((piece.shape[0], LANES - HD), F32)], axis=1
            )
            dst[:, h * LANES : (h + 1) * LANES] = piece.astype(BF16)
    width = wo.shape[1]
    for n, src in enumerate((wo, wu, wd)):
        wt[n * width : (n + 1) * width] = src[...].astype(F32).T.astype(BF16)


def prep_call(wq, wk, wv, wo, wu, wd):
    depth, width = wq.shape
    heads = width // HD
    step = 256
    src = pl.BlockSpec((step, width), lambda g: (g, 0))
    dst = pl.BlockSpec((step, heads * LANES), lambda g: (g, 0))
    padded = jax.ShapeDtypeStruct((depth, heads * LANES), BF16)
    return pl.pallas_call(
        functools.partial(prep_kernel, heads),
        grid=(depth // step,),
        in_specs=[src] * 6,
        out_specs=[dst, dst, dst, pl.BlockSpec((3 * width, step), lambda g: (0, g))],
        out_shape=[padded, padded, padded, jax.ShapeDtypeStruct((3 * width, depth), BF16)],
        compiler_params=params(),
        name="weight_layouts",
    )(wq, wk, wv, wo, wu, wd)


def pad_heads(value, heads):
    parts = []
    for h in range(heads):
        parts.append(value[:, h * HD : (h + 1) * HD])
        parts.append(jnp.zeros((value.shape[0], LANES - HD), value.dtype))
    return jnp.concatenate(parts, axis=1)


def qkv_kernel(
    heads, scal, p0, p1, p2, p3, wq, wk, wv, lq, lk, lv, rq, rk, rv,
    q_ref, k_ref, v_ref, kt_ref, vt_ref, low_ref, buf, sems,
):
    x = pl.program_id(0)
    rows = buf.shape[1]
    pieces = (p0, p1, p2, p3)
    copies = [
        pltpu.make_async_copy(pieces[n].at[pl.ds(0, rows)], buf.at[n], sems.at[n])
        for n in range(4)
    ]

    @pl.when(x == 0)
    def _():
        for c in copies:
            c.start()

    for n in range(4):

        @pl.when(x == n)
        def _(n=n):
            copies[n].wait()

    block = buf[x]
    lower = jnp.concatenate([lq[0], lk[0], lv[0]], axis=0)
    low = nt(block, lower).astype(BF16)
    low_ref[...] = low
    rank = lq.shape[1]
    for n, (w, r, row_ref, col_ref) in enumerate(
        ((wq, rq, q_ref, None), (wk, rk, k_ref, kt_ref), (wv, rv, v_ref, vt_ref))
    ):
        raise_pad = pad_heads(r[0].astype(F32), heads).astype(BF16)
        out = nn(block, w[...]) + nn(low[:, n * rank : (n + 1) * rank], raise_pad)
        if n == 0:
            out = out * (SCORE_SCALE * LOG2E)
        row_ref[...] = out.astype(BF16)
        if col_ref is not None:
            col_ref[...] = out.T.astype(BF16)


def qkv_call(scal, pieces, padded, lowers, raises, rows, length):
    depth, wide = padded[0].shape
    heads = wide // LANES
    rank = lowers[0].shape[1]
    width = raises[0].shape[2]
    any_spec = pl.BlockSpec(memory_space=pl.ANY)
    lower = pl.BlockSpec((1, rank, depth), lambda g, s: (s[0], 0, 0))
    raise_ = pl.BlockSpec((1, rank, width), lambda g, s: (s[0], 0, 0))
    row = pl.BlockSpec((rows, wide), lambda g, s: (s[1] ^ g, 0))
    col = pl.BlockSpec((wide, rows), lambda g, s: (0, s[1] ^ g))
    low = pl.BlockSpec((rows, 3 * rank), lambda g, s: (s[1] ^ g, 0))
    row_t = jax.ShapeDtypeStruct((length, wide), BF16)
    col_t = jax.ShapeDtypeStruct((wide, length), BF16)
    return pl.pallas_call(
        functools.partial(qkv_kernel, heads),
        grid_spec=pltpu.PrefetchScalarGridSpec(
            num_scalar_prefetch=1,
            grid=(4,),
            in_specs=[any_spec] * 4 + [whole((depth, wide))] * 3 + [lower] * 3 + [raise_] * 3,
            out_specs=[row, row, row, col, col, low],
            scratch_shapes=[
                pltpu.VMEM((4, rows, depth), BF16),
                pltpu.SemaphoreType.DMA((4,)),
            ],
        ),
        out_shape=[
            row_t, row_t, row_t, col_t, col_t,
            jax.ShapeDtypeStruct((length, 3 * rank), BF16),
        ],
        compiler_params=params(),
        cost_estimate=cost(2 * length * depth * wide * 3, 12 * length * wide),
        name="project",
    )(scal, *pieces, *padded, *lowers, *raises)


def allowed_mask(seg_row, seg_col, first, last, start, size):
    ok = seg_col[first:last, :] == seg_row[:, start : start + size]
    if last > start:
        key = lax.broadcasted_iota(jnp.int32, (last - first, size), 0) + first
        query = lax.broadcasted_iota(jnp.int32, (last - first, size), 1) + start
        ok = ok & (key <= query)
    return ok


def attend_kernel(
    step, scal, seg_row, seg_col, q_ref, k_ref, vt_ref,
    ot_ref, lse_ref, o0, o1, o2, o3, wide,
):
    h = pl.program_id(0)
    length = q_ref.shape[0]
    for i in range(length // step):
        start, last = i * step, (i + 1) * step
        s = nt(k_ref[:last], q_ref[start:last])
        s = jnp.where(allowed_mask(seg_row, seg_col, 0, last, start, step), s, NEG)
        top = jnp.max(s, axis=0, keepdims=True)
        p = jnp.exp2(s - top)
        total = jnp.sum(p, axis=0, keepdims=True)
        out = nn(vt_ref[:HD, :last], p.astype(BF16)) / total
        ot_ref[:, start:last] = out.astype(BF16)
        wide[pl.ds(pl.multiple_of(h * HD, 16), HD), start:last] = out
        lse_ref[0, :, start:last] = top + jnp.log2(total)

    @pl.when(h == pl.num_programs(0) - 1)
    def _():
        rows = o0.shape[0]
        for x, ref in enumerate((o0, o1, o2, o3)):
            at = pl.multiple_of((scal[1] ^ x) * rows, rows)
            ref[...] = wide[:, pl.ds(at, rows)].T.astype(BF16)


def attend_call(scal, seg_row, seg_col, q, k, vt, rows):
    length, wide = q.shape
    heads = wide // LANES
    width = heads * HD
    row = pl.BlockSpec((length, LANES), lambda h, s: (0, h))
    out = whole((rows, width))
    out_t = jax.ShapeDtypeStruct((rows, width), BF16)
    return pl.pallas_call(
        functools.partial(attend_kernel, 512),
        grid_spec=pltpu.PrefetchScalarGridSpec(
            num_scalar_prefetch=1,
            grid=(heads,),
            in_specs=[
                whole((1, length)), whole((length, 1)), row, row,
                pl.BlockSpec((LANES, length), lambda h, s: (h, 0)),
            ],
            out_specs=[
                pl.BlockSpec((HD, length), lambda h, s: (h, 0)),
                pl.BlockSpec((1, 1, length), lambda h, s: (h, 0, 0)),
                out, out, out, out,
            ],
            scratch_shapes=[pltpu.VMEM((width, length), F32)],
        ),
        out_shape=[
            jax.ShapeDtypeStruct((width, length), BF16),
            jax.ShapeDtypeStruct((heads, 1, length), F32),
            out_t, out_t, out_t, out_t,
        ],
        compiler_params=params(),
        cost_estimate=cost(heads * 4 * length * length * LANES, 8 * length * wide),
        name="attend",
    )(scal, seg_row, seg_col, q, k, vt)


def attend_back_kernel(
    step, scal, seg_row, seg_col, q_ref, k_ref, v_ref, kt_ref, ot_ref, lse_ref,
    d0, d1, d2, d3, dq_ref, dk_ref, dv_ref, grad_t, dk_sum, dv_sum,
):
    h = pl.program_id(0)
    length = q_ref.shape[0]

    @pl.when(h == 0)
    def _():
        rows = d0.shape[0]
        for x, ref in enumerate((d0, d1, d2, d3)):
            at = pl.multiple_of((scal[1] ^ x) * rows, rows)
            grad_t[:, pl.ds(at, rows)] = ref[...].astype(F32).T.astype(BF16)

    mine = grad_t[pl.ds(pl.multiple_of(h * HD, 16), HD), :]
    row_dot = jnp.sum(mine.astype(F32) * ot_ref[...].astype(F32), axis=0, keepdims=True)
    dv_sum[:, HD:] = jnp.zeros((length, LANES - HD), F32)
    for i in range(length // step):
        start, last = i * step, (i + 1) * step
        grad = mine[:, start:last]
        s = nt(k_ref[:last], q_ref[start:last])
        dp = nn(v_ref[:last, :HD], grad)
        s = jnp.where(allowed_mask(seg_row, seg_col, 0, last, start, step), s, NEG)
        p = jnp.exp2(s - lse_ref[0, :, start:last])
        ds = (p * (dp - row_dot[:, start:last])).astype(BF16)
        dv = nt(p.astype(BF16), grad)
        dk = nn(ds, q_ref[start:last])
        dqt = nn(kt_ref[:HD, :last], ds)
        if start:
            dv_sum[:start, :HD] += dv[:start]
            dk_sum[:start] += dk[:start]
        dv_sum[start:last, :HD] = dv[start:]
        dk_sum[start:last] = dk[start:]
        dq_ref[start:last, :HD] = (dqt * SCORE_SCALE).T.astype(BF16)
        dq_ref[start:last, HD:] = jnp.zeros((step, LANES - HD), BF16)
    dk_ref[...] = (dk_sum[...] * (1.0 / LOG2E)).astype(BF16)
    dv_ref[...] = dv_sum[...].astype(BF16)


def attend_back_call(scal, seg_row, seg_col, q, k, v, kt, ot, lse, grads):
    length, wide = q.shape
    heads = wide // LANES
    width = heads * HD
    rows = grads[0].shape[0]
    row = pl.BlockSpec((length, LANES), lambda h, s: (0, h))
    row_t = jax.ShapeDtypeStruct((length, wide), BF16)
    return pl.pallas_call(
        functools.partial(attend_back_kernel, 256),
        grid_spec=pltpu.PrefetchScalarGridSpec(
            num_scalar_prefetch=1,
            grid=(heads,),
            in_specs=[
                whole((1, length)), whole((length, 1)), row, row, row,
                pl.BlockSpec((LANES, length), lambda h, s: (h, 0)),
                pl.BlockSpec((HD, length), lambda h, s: (h, 0)),
                pl.BlockSpec((1, 1, length), lambda h, s: (h, 0, 0)),
            ]
            + [whole((rows, width))] * 4,
            out_specs=[row, row, row],
            scratch_shapes=[
                pltpu.VMEM((width, length), BF16),
                pltpu.VMEM((length, LANES), F32),
                pltpu.VMEM((length, LANES), F32),
            ],
        ),
        out_shape=[row_t, row_t, row_t],
        compiler_params=params(),
        cost_estimate=cost(heads * 8 * length * length * LANES, 16 * length * wide),
        name="attend_back",
    )(scal, seg_row, seg_col, q, k, v, kt, ot, lse, *grads)


def middle_kernel(
    scal, x_ref, g_ref, a0, a1, a2, a3, s0, s1, s2, s3, w0, w1, w2, w3,
    orr, ulr, drr,
    act_ref, gm_ref, o0, o1, o2, o3, e0, e1, e2, e3,
    wo, wu, wd, ol, ur, dl, sems, e_sum,
):
    c = pl.program_id(0)
    width = a0.shape[1]
    rank = orr.shape[1]
    copies = []
    for n, dst in enumerate((wo, wu, wd)):
        for x, src in enumerate((w0, w1, w2, w3)):
            copies.append(
                pltpu.make_async_copy(
                    src.at[pl.ds(n * width, width)],
                    dst.at[pl.ds(x * width, width)],
                    sems.at[n * 4 + x],
                )
            )

    @pl.when(c == 0)
    def _():
        for copy in copies:
            copy.start()
        for x, src in enumerate((s0, s1, s2, s3)):
            for slot, dst in enumerate((ol, ur, dl)):
                dst[:, x * width : (x + 1) * width] = src[:, slot * SLOT : slot * SLOT + width].astype(F32)
        e_sum[...] = jnp.zeros_like(e_sum)
        for copy in copies:
            copy.wait()

    out_lower, up_raise, down_lower = (r[...].astype(BF16) for r in (ol, ur, dl))
    out_raise, up_lower, down_raise = orr[0], ulr[0], drr[0]
    att = jnp.concatenate([a[...].astype(F32) for a in (a0, a1, a2, a3)], axis=1).astype(BF16)
    low_out = nt(att, out_lower).astype(BF16)
    middle = x_ref[...].astype(F32) + nn(att, wo[...]) + nn(low_out, out_raise)
    factor = lax.rsqrt(jnp.mean(middle * middle, axis=-1, keepdims=True) + EPS)
    unit = middle * factor
    normed = unit.astype(BF16)
    low_up = nt(normed, up_lower).astype(BF16)
    preact = nt(normed, wu[...]) + nn(low_up, up_raise)
    sigma = 1.0 / (1.0 + jnp.exp(-preact))
    active = (preact * sigma).astype(BF16)
    low_down = nt(active, down_lower).astype(BF16)
    act_ref[...] = (middle + (nn(active, wd[...]) + nn(low_down, down_raise))).astype(BF16)

    grad = g_ref[...]
    grad_low_down = nt(grad, down_raise).astype(BF16)
    grad_act = nt(grad, wd[...]) + nn(grad_low_down, down_lower)
    grad_pre = (grad_act * (sigma * (1.0 + preact * (1.0 - sigma)))).astype(BF16)
    grad_low_up = nt(grad_pre, up_raise).astype(BF16)
    grad_mid = nn(grad_pre, wu[...]) + nn(grad_low_up, up_lower)
    dot = jnp.mean(grad_mid * unit, axis=-1, keepdims=True)
    grad_middle = grad.astype(F32) + factor * (grad_mid - unit * dot)
    gm_ref[...] = grad_middle
    grad_attn = grad_middle.astype(BF16)
    grad_low_out = nt(grad_attn, out_raise).astype(BF16)
    grad_att = nt(grad_attn, wo[...]) + nn(grad_low_out, out_lower)
    for x, ref in enumerate((o0, o1, o2, o3)):
        ref[...] = grad_att[:, x * width : (x + 1) * width].astype(BF16)

    e_sum[0:rank] += tn(low_out, grad_attn)
    e_sum[rank : 2 * rank] += tn(grad_low_up, normed)
    e_sum[2 * rank : 3 * rank] += tn(low_down, grad)
    e_sum[3 * rank : 4 * rank] += tn(grad_low_out, att)
    e_sum[4 * rank : 5 * rank] += tn(low_up, grad_pre)
    e_sum[5 * rank : 6 * rank] += tn(grad_low_down, active)

    @pl.when(c == pl.num_programs(0) - 1)
    def _():
        shared = e_sum[: 3 * rank].astype(BF16)
        for x, ref in enumerate((e0, e1, e2, e3)):
            ref[: 3 * rank] = shared
            mark = jnp.full((rank, ref.shape[1]), scal[0], jnp.int32).astype(F32)
            if x:
                mark = jnp.zeros_like(mark)
            ref[3 * rank :] = mark.astype(BF16)
            for slot in range(3):
                part = e_sum[(3 + slot) * rank : (4 + slot) * rank, x * width : (x + 1) * width]
                ref[3 * rank :, slot * SLOT : slot * SLOT + width] = part.astype(BF16)


def middle_call(scal, x, g, att, pieces, weights, out_raise, up_lower, down_raise):
    rows, depth = x.shape
    width = att[0].shape[1]
    rank = out_raise.shape[1]
    step = 256
    wide = pl.BlockSpec((step, depth), lambda c, s: (c, 0))
    part = pl.BlockSpec((step, width), lambda c, s: (c, 0))
    small = pl.BlockSpec((rank, depth), lambda c, s: (rows // rank, 0))
    pick = pl.BlockSpec((1, rank, depth), lambda c, s: (s[0], 0, 0))
    any_spec = pl.BlockSpec(memory_space=pl.ANY)
    part_t = jax.ShapeDtypeStruct((rows, width), BF16)
    pack_t = jax.ShapeDtypeStruct((4 * rank, depth), BF16)
    square = pltpu.VMEM((4 * width, depth), BF16)
    thin = pltpu.VMEM((rank, depth), F32)
    return pl.pallas_call(
        middle_kernel,
        grid_spec=pltpu.PrefetchScalarGridSpec(
            num_scalar_prefetch=1,
            grid=(rows // step,),
            in_specs=[wide, wide] + [part] * 4 + [small] * 4 + [any_spec] * 4 + [pick] * 3,
            out_specs=[wide, wide] + [part] * 4 + [whole((4 * rank, depth))] * 4,
            scratch_shapes=[
                square, square, square, thin, thin, thin,
                pltpu.SemaphoreType.DMA((12,)),
                pltpu.VMEM((6 * rank, depth), F32),
            ],
        ),
        out_shape=[
            jax.ShapeDtypeStruct((rows, depth), BF16),
            jax.ShapeDtypeStruct((rows, depth), F32),
        ]
        + [part_t] * 4
        + [pack_t] * 4,
        compiler_params=params(),
        cost_estimate=cost(12 * rows * depth * depth, 6 * depth * depth + 12 * rows * depth),
        name="feed_forward",
    )(scal, x, g, *att, *pieces, *weights, out_raise, up_lower, down_raise)


def grad_in_kernel(
    heads, scal, dq, dk, dv, low, p0, p1, p2, p3, wq, wk, wv, lq, lk, lv, rq, rk, rv,
    out_ref, pack_ref, buf, sems, lower_sum, raise_sum,
):
    x = pl.program_id(0)
    rows = buf.shape[1]
    rank = lq.shape[1]
    pieces = (p0, p1, p2, p3)
    copies = [
        pltpu.make_async_copy(pieces[n].at[pl.ds(0, rows)], buf.at[n], sems.at[n])
        for n in range(4)
    ]

    @pl.when(x == 0)
    def _():
        for c in copies:
            c.start()
        lower_sum[...] = jnp.zeros_like(lower_sum)
        raise_sum[...] = jnp.zeros_like(raise_sum)

    for n in range(4):

        @pl.when(x == n)
        def _(n=n):
            copies[n].wait()

    block = buf[x]
    total = None
    low_grads = []
    for n, (d, w, r) in enumerate(((dq, wq, rq), (dk, wk, rk), (dv, wv, rv))):
        value = d[...]
        raise_pad = pad_heads(r[0].astype(F32), heads).astype(BF16)
        low_grads.append(nt(value, raise_pad))
        term = nt(value, w[...])
        total = term if total is None else total + term
        raise_sum[n * rank : (n + 1) * rank] += tn(low[:, n * rank : (n + 1) * rank], value)
    grad_low = jnp.concatenate(low_grads, axis=1).astype(BF16)
    lower = jnp.concatenate([lq[0], lk[0], lv[0]], axis=0)
    out_ref[0] = (total + nn(grad_low, lower)).astype(BF16)
    lower_sum[...] += tn(grad_low, block)

    @pl.when(x == pl.num_programs(0) - 1)
    def _():
        pack_ref[: 3 * rank] = lower_sum[...].astype(BF16)
        pack_ref[3 * rank :] = jnp.zeros((rank, pack_ref.shape[1]), BF16)
        for n in range(3):
            for h in range(heads):
                part = raise_sum[n * rank : (n + 1) * rank, h * LANES : h * LANES + HD]
                at = n * SLOT + h * HD
                pack_ref[3 * rank :, at : at + HD] = part.astype(BF16)


def grad_in_call(scal, grads, low, pieces, padded, lowers, raises, rows):
    depth, wide = padded[0].shape
    heads = wide // LANES
    rank = lowers[0].shape[1]
    width = raises[0].shape[2]
    any_spec = pl.BlockSpec(memory_space=pl.ANY)
    lower = pl.BlockSpec((1, rank, depth), lambda g, s: (s[0], 0, 0))
    raise_ = pl.BlockSpec((1, rank, width), lambda g, s: (s[0], 0, 0))
    row = pl.BlockSpec((rows, wide), lambda g, s: (s[1] ^ g, 0))
    low_spec = pl.BlockSpec((rows, 3 * rank), lambda g, s: (s[1] ^ g, 0))
    return pl.pallas_call(
        functools.partial(grad_in_kernel, heads),
        grid_spec=pltpu.PrefetchScalarGridSpec(
            num_scalar_prefetch=1,
            grid=(4,),
            in_specs=[row] * 3 + [low_spec] + [any_spec] * 4 + [whole((depth, wide))] * 3
            + [lower] * 3 + [raise_] * 3,
            out_specs=[
                pl.BlockSpec((1, rows, depth), lambda g, s: (g, 0, 0)),
                whole((4 * rank, depth)),
            ],
            scratch_shapes=[
                pltpu.VMEM((4, rows, depth), BF16),
                pltpu.SemaphoreType.DMA((4,)),
                pltpu.VMEM((3 * rank, depth), F32),
                pltpu.VMEM((3 * rank, wide), F32),
            ],
        ),
        out_shape=[
            jax.ShapeDtypeStruct((4, rows, depth), BF16),
            jax.ShapeDtypeStruct((4 * rank, depth), BF16),
        ],
        compiler_params=params(),
        cost_estimate=cost(8 * rows * depth * wide * 3, 16 * rows * depth),
        name="grad_input",
    )(scal, *grads, low, *pieces, *padded, *lowers, *raises)


def last_kernel(x_ref, gm_ref, a_ref, b_ref, c_ref, out_ref):
    x = x_ref[...].astype(F32)
    factor = lax.rsqrt(jnp.mean(x * x, axis=-1, keepdims=True) + EPS)
    unit = x * factor
    grad = a_ref[0].astype(F32) + b_ref[...].astype(F32) + c_ref[...].astype(F32)
    dot = jnp.mean(grad * unit, axis=-1, keepdims=True)
    out_ref[...] = (gm_ref[...] + factor * (grad - unit * dot)).astype(BF16)


def last_call(x, gm, a, b, c):
    rows, depth = x.shape
    step = 128
    wide = pl.BlockSpec((step, depth), lambda g: (g, 0))
    return pl.pallas_call(
        last_kernel,
        grid=(rows // step,),
        in_specs=[wide, wide, pl.BlockSpec((1, step, depth), lambda g: (0, g, 0)), wide, wide],
        out_specs=wide,
        out_shape=jax.ShapeDtypeStruct((rows, depth), BF16),
        compiler_params=params(),
        name="input_gradient",
    )(x, gm, a, b, c)


def sets_kernel(first_ref, second_ref, *outs):
    j = pl.program_id(0)
    rank = outs[0].shape[1]
    depth = first_ref.shape[2]
    sums = [jnp.zeros(first_ref.shape[1:], F32) for _ in range(2)]
    for n in range(first_ref.shape[0]):
        chosen = first_ref[n, 3 * rank : 3 * rank + 1, depth - 1 : depth].astype(F32)
        pick = (chosen == j.astype(F32)).astype(F32)
        for m, ref in enumerate((first_ref, second_ref)):
            sums[m] = sums[m] + ref[n].astype(F32) * pick
    for m, total in enumerate(sums):
        for k in range(3):
            outs[6 * m + k][0] = total[k * rank : (k + 1) * rank]
            width = outs[6 * m + 3 + k].shape[2]
            outs[6 * m + 3 + k][0] = total[3 * rank :, k * SLOT : k * SLOT + width]


def sets_call(first, second, sets, width):
    parts, four, depth = first.shape
    rank = four // 4
    full = pl.BlockSpec((1, rank, depth), lambda j: (j, 0, 0))
    thin = pl.BlockSpec((1, rank, width), lambda j: (j, 0, 0))
    full_t = jax.ShapeDtypeStruct((sets, rank, depth), F32)
    thin_t = jax.ShapeDtypeStruct((sets, rank, width), F32)
    return pl.pallas_call(
        sets_kernel,
        grid=(sets,),
        in_specs=[whole(first.shape), whole(second.shape)],
        out_specs=[full, full, full, thin, thin, thin] * 2,
        out_shape=[full_t, full_t, full_t, thin_t, thin_t, thin_t] * 2,
        compiler_params=params(),
        name="set_sums",
    )(first, second)


def on_device(
    dp_count,
    tensor_count,
    tokens,
    segment_ids,
    adapter_choice,
    cotangent,
    weight_query,
    weight_key,
    weight_value,
    weight_output,
    weight_upward,
    weight_downward,
    query_lower,
    query_raise,
    key_lower,
    key_raise,
    value_lower,
    value_raise,
    output_lower,
    output_raise,
    upward_lower,
    upward_raise,
    downward_lower,
    downward_raise,
):
    across = functools.partial(swap, axis_name="tensor", count=tensor_count)
    x, g = tokens[0], cotangent[0]
    rows = x.shape[0]
    length = segment_ids.shape[1]
    sets, rank = query_lower.shape[:2]
    me = lax.axis_index("tensor").astype(jnp.int32)
    scal = jnp.stack([adapter_choice[0], me])
    seg_row = segment_ids
    seg_col = segment_ids.reshape(length, 1)

    own = norm_call(x, adapter_choice, output_lower, upward_raise, downward_lower)
    far = across(own, bit=2)
    near = across(own, bit=1)
    pq, pk, pv, wt = prep_call(
        weight_query, weight_key, weight_value, weight_output, weight_upward, weight_downward
    )
    share = wt.shape[0] // dp_count
    mine = lax.dynamic_slice_in_dim(wt, lax.axis_index("dp") * share, share, 0)
    fetched = across(mine, bit=2)
    wt_far = lax.all_gather(fetched, "dp", axis=0, tiled=True)
    wt_near = across(wt, bit=1)
    wt_cross = across(wt_far, bit=1)

    cross = across(far, bit=1)
    pieces = (own, near, far, cross)
    lowers = (query_lower, key_lower, value_lower)
    raises = (query_raise, key_raise, value_raise)
    padded = (pq, pk, pv)
    q, k, v, kt, vt, low = qkv_call(scal, pieces, padded, lowers, raises, rows, length)
    ot, lse, *att = attend_call(scal, seg_row, seg_col, q, k, vt, rows)
    att = [att[0]] + [across(att[n], bit=n) for n in (1, 2, 3)]
    act, grad_middle, *more = middle_call(
        scal, x, g, att, pieces, (wt, wt_near, wt_far, wt_cross),
        output_raise, upward_lower, downward_raise,
    )
    grads, packs = more[:4], more[4:]
    grads = [grads[0]] + [across(grads[n], bit=n) for n in (1, 2, 3)]
    packs = [packs[0]] + [across(packs[n], bit=n) for n in (1, 2, 3)]
    packs = [p.astype(F32) for p in packs]
    first = ((packs[0] + packs[1]) + (packs[2] + packs[3])).astype(BF16)
    first_all = lax.all_gather(first, "dp", axis=0)

    back = attend_back_call(scal, seg_row, seg_col, q, k, v, kt, ot, lse, grads)
    partial, pack = grad_in_call(scal, back, low, pieces, padded, lowers, raises, rows)

    lower_part = pack[: 3 * rank]
    others = [across(lower_part, bit=n).astype(F32) for n in (1, 2, 3)]
    lower_sum = (lower_part.astype(F32) + others[0]) + (others[1] + others[2])
    second = jnp.concatenate([lower_sum.astype(BF16), pack[3 * rank :]], axis=0)
    second_all = lax.all_gather(second, "dp", axis=0)

    near_mine = across(partial[1], bit=1)
    near_far = across(partial[3], bit=1)
    to_far = (partial[2].astype(F32) + near_far.astype(F32)).astype(BF16)
    from_far = across(to_far, bit=2)
    input_grad = last_call(x, grad_middle, partial, near_mine, from_far)

    out = sets_call(first_all, second_all, sets, query_raise.shape[2])
    (out_raise_g, up_lower_g, down_raise_g, out_lower_g, up_raise_g, down_lower_g) = out[:6]
    (q_lower_g, k_lower_g, v_lower_g, q_raise_g, k_raise_g, v_raise_g) = out[6:]
    return (
        act[None],
        input_grad[None],
        q_lower_g,
        q_raise_g,
        k_lower_g,
        k_raise_g,
        v_lower_g,
        v_raise_g,
        out_lower_g,
        out_raise_g,
        up_lower_g,
        up_raise_g,
        down_lower_g,
        down_raise_g,
    )


def solution(mesh):
    split = P(None, None, "tensor")
    return jax.shard_map(
        functools.partial(on_device, mesh.shape["dp"], mesh.shape["tensor"]),
        mesh=mesh,
        in_specs=(
            P("dp", "tensor", None),
            P("dp", None),
            P("dp"),
            P("dp", "tensor", None),
            P(None, "tensor"),
            P(None, "tensor"),
            P(None, "tensor"),
            P(None, "tensor"),
            P(None, "tensor"),
            P(None, "tensor"),
            P(),
            split,
            P(),
            split,
            P(),
            split,
            split,
            P(),
            P(),
            split,
            split,
            P(),
        ),
        out_specs=(
            P("dp", "tensor", None),
            P("dp", "tensor", None),
            P(),
            split,
            P(),
            split,
            P(),
            split,
            split,
            P(),
            P(),
            split,
            split,
            P(),
        ),
        check_vma=False,
    )
```

```python
import functools
import math

import jax
import jax.numpy as jnp
from jax import lax
from jax.experimental import pallas as pl
from jax.experimental.pallas import tpu as pltpu
from jax.sharding import PartitionSpec as P

HD = 80
LANES = 128
EPS = 1e-06
NEG = -1e30
F32 = jnp.float32
BF16 = jnp.bfloat16
VMEM_BYTES = 60 * 2**20
SCORE_SCALE = HD ** (-0.5)
LOG2E = math.log2(math.e)
SLOT = 384

NT = (((1,), (1,)), ((), ()))
TN = (((0,), (0,)), ((), ()))


def nn(left, right):
    return jnp.dot(left, right, preferred_element_type=F32)


def nt(left, right):
    return lax.dot_general(left, right, NT, preferred_element_type=F32)


def tn(left, right):
    return lax.dot_general(left, right, TN, preferred_element_type=F32)


def params(**more):
    return pltpu.CompilerParams(vmem_limit_bytes=VMEM_BYTES, **more)


def cost(flops, nbytes):
    return pl.CostEstimate(flops=int(flops), bytes_accessed=int(nbytes), transcendentals=0)


def whole(shape):
    return pl.BlockSpec(shape, lambda *_: (0,) * len(shape))


def swap(array, axis_name, count, bit):
    return lax.ppermute(array, axis_name, [(i, i ^ bit) for i in range(count)])


def norm_kernel(choice, x_ref, ol_ref, ur_ref, dl_ref, out_ref):
    rows = x_ref.shape[0]
    x = x_ref[...].astype(F32)
    factor = lax.rsqrt(jnp.mean(x * x, axis=-1, keepdims=True) + EPS)
    out_ref[:rows] = (x * factor).astype(BF16)
    out_ref[rows:] = jnp.zeros_like(out_ref[rows:])
    width = ol_ref.shape[2]
    for slot, ref in enumerate((ol_ref, ur_ref, dl_ref)):
        out_ref[rows:, slot * SLOT : slot * SLOT + width] = ref[0]


def norm_call(x, choice, ol, ur, dl):
    rows, width = x.shape
    rank, local = ol.shape[1:]
    pick = pl.BlockSpec((1, rank, local), lambda g, c: (c[0], 0, 0))
    return pl.pallas_call(
        norm_kernel,
        grid_spec=pltpu.PrefetchScalarGridSpec(
            num_scalar_prefetch=1,
            grid=(1,),
            in_specs=[whole((rows, width)), pick, pick, pick],
            out_specs=whole((rows + rank, width)),
        ),
        out_shape=jax.ShapeDtypeStruct((rows + rank, width), BF16),
        compiler_params=params(),
        name="norm_in",
    )(choice, x, ol, ur, dl)


def copies_of(pieces, buf, sems):
    rows = buf.shape[1]
    return [
        pltpu.make_async_copy(piece.at[pl.ds(0, rows)], buf.at[n], sems.at[n])
        for n, piece in enumerate(pieces)
    ]


def bring(copies):
    step = pl.program_id(0)

    @pl.when(step == 0)
    def _():
        for c in copies:
            c.start()

    for n, c in enumerate(copies):

        @pl.when(step == n)
        def _(c=c):
            c.wait()


def project_step(heads, block, stack, raises, qt_ref, kt_ref, vt_ref, k_ref, v_ref, low_ref):
    width = heads * HD
    rank = raises[0].shape[1]
    out = nt(stack[...], block)
    low = out[3 * width :].astype(BF16)
    low_ref[...] = low
    for n, (r, col_ref, row_ref) in enumerate(
        zip(raises, (qt_ref, kt_ref, vt_ref), (None, k_ref, v_ref))
    ):
        part = out[n * width : (n + 1) * width] + tn(r[0], low[n * rank : (n + 1) * rank])
        if n == 0:
            part = part * (SCORE_SCALE * LOG2E)
        part = part.astype(BF16)
        col_ref[...] = part
        if row_ref is not None:
            for h in range(heads):
                at = h * LANES
                row_ref[:, at : at + HD] = part[h * HD : (h + 1) * HD].T


def project_near_kernel(
    heads, scal, p0, p1, wq, wk, wv, lq, lk, lv, rq, rk, rv,
    qt_ref, kt_ref, vt_ref, k_ref, v_ref, low_ref, stack, buf, sems,
):
    bring(copies_of((p0, p1), buf, sems))

    @pl.when(pl.program_id(0) == 0)
    def _():
        at = 0
        for part in (wq[...], wk[...], wv[...], lq[0], lk[0], lv[0]):
            stack[at : at + part.shape[0]] = part
            at += part.shape[0]

    project_step(
        heads, buf[pl.program_id(0)], stack, (rq, rk, rv),
        qt_ref, kt_ref, vt_ref, k_ref, v_ref, low_ref,
    )


def project_far_kernel(
    heads, scal, p0, p1, stack, rq, rk, rv, i0, i1, i2, i3, i4, i5,
    qt_ref, kt_ref, vt_ref, k_ref, v_ref, low_ref, buf, sems,
):
    bring(copies_of((p0, p1), buf, sems))
    project_step(
        heads, buf[pl.program_id(0)], stack, (rq, rk, rv),
        qt_ref, kt_ref, vt_ref, k_ref, v_ref, low_ref,
    )


def project_call(scal, first, pieces, weights, lowers, stack, raises, so_far, rows, length):
    depth = pieces[0].shape[1]
    rank, width = raises[0].shape[1:]
    heads = width // HD
    total = 3 * (width + rank)
    any_spec = pl.BlockSpec(memory_space=pl.ANY)
    lower = pl.BlockSpec((1, rank, depth), lambda g, s: (s[0], 0, 0))
    raise_ = pl.BlockSpec((1, rank, width), lambda g, s: (s[0], 0, 0))
    row = pl.BlockSpec((rows, heads * LANES), lambda g, s: (s[1] ^ (g + first), 0))
    col = pl.BlockSpec((width, rows), lambda g, s: (0, s[1] ^ (g + first)))
    low = pl.BlockSpec((3 * rank, rows), lambda g, s: (0, s[1] ^ (g + first)))
    col_t = jax.ShapeDtypeStruct((width, length), BF16)
    row_t = jax.ShapeDtypeStruct((length, heads * LANES), BF16)
    out_specs = [col, col, col, row, row, low]
    out_shape = [col_t, col_t, col_t, row_t, row_t, jax.ShapeDtypeStruct((3 * rank, length), BF16)]
    if so_far is None:
        body = project_near_kernel
        in_specs = [any_spec] * 2 + [whole((width, depth))] * 3 + [lower] * 3 + [raise_] * 3
        args = (*pieces, *weights, *lowers, *raises)
        out_specs = out_specs + [whole((total, depth))]
        out_shape = out_shape + [jax.ShapeDtypeStruct((total, depth), BF16)]
        alias = {}
    else:
        body = project_far_kernel
        in_specs = [any_spec] * 2 + [whole((total, depth))] + [raise_] * 3 + [any_spec] * 6
        args = (*pieces, stack, *raises, *so_far)
        alias = {7 + n: n for n in range(6)}
    return pl.pallas_call(
        functools.partial(body, heads),
        grid_spec=pltpu.PrefetchScalarGridSpec(
            num_scalar_prefetch=1,
            grid=(2,),
            in_specs=in_specs,
            out_specs=out_specs,
            scratch_shapes=[pltpu.VMEM((2, rows, depth), BF16), pltpu.SemaphoreType.DMA((2,))],
        ),
        out_shape=out_shape,
        input_output_aliases=alias,
        compiler_params=params(),
        cost_estimate=cost(2 * 2 * rows * depth * total, 16 * rows * depth),
        name="project",
    )(scal, *args)


def allowed_mask(seg_row, seg_col, last, start, size):
    key = lax.broadcasted_iota(jnp.int32, (last, size), 0)
    query = lax.broadcasted_iota(jnp.int32, (last, size), 1) + start
    return (seg_col[:last, :] == seg_row[:, start : start + size]) & (key <= query)


def attend_kernel(step, scal, seg_row, seg_col, qt_ref, k_ref, vt_ref, *rest):
    ot_ref, lse_ref, o0, o1, o2, o3, wide = rest[-7:]
    h = pl.program_id(0)
    length = qt_ref.shape[1]
    for i in range(length // step):
        start, last = i * step, (i + 1) * step
        s = nn(k_ref[:last, :HD], qt_ref[:, start:last])
        s = jnp.where(allowed_mask(seg_row, seg_col, last, start, step), s, NEG)
        top = jnp.max(s, axis=0, keepdims=True)
        p = jnp.exp2(s - top)
        total = jnp.sum(p, axis=0, keepdims=True)
        out = nn(vt_ref[:, :last], p.astype(BF16)) / total
        ot_ref[:, start:last] = out.astype(BF16)
        wide[pl.ds(pl.multiple_of(h * HD, 16), HD), start:last] = out
        lse_ref[0, :, start:last] = top + jnp.log2(total)

    @pl.when(h == pl.num_programs(0) - 1)
    def _():
        rows = o0.shape[0]
        for x, ref in enumerate((o0, o1, o2, o3)):
            at = pl.multiple_of((scal[1] ^ x) * rows, rows)
            ref[...] = wide[:, pl.ds(at, rows)].T.astype(BF16)


def attend_call(scal, seg_row, seg_col, qt, k, vt, first, count, so_far, rows):
    width, length = qt.shape
    heads = width // HD
    col = pl.BlockSpec((HD, length), lambda h, s: (h + first, 0))
    out = whole((rows, count * HD))
    out_t = jax.ShapeDtypeStruct((rows, count * HD), BF16)
    kept = [] if so_far is None else list(so_far)
    return pl.pallas_call(
        functools.partial(attend_kernel, 512),
        grid_spec=pltpu.PrefetchScalarGridSpec(
            num_scalar_prefetch=1,
            grid=(count,),
            in_specs=[
                whole((1, length)), whole((length, 1)), col,
                pl.BlockSpec((length, LANES), lambda h, s: (0, h + first)), col,
            ]
            + [pl.BlockSpec(memory_space=pl.ANY)] * len(kept),
            out_specs=[
                col,
                pl.BlockSpec((1, 1, length), lambda h, s: (h + first, 0, 0)),
                out, out, out, out,
            ],
            scratch_shapes=[pltpu.VMEM((count * HD, length), F32)],
        ),
        out_shape=[
            jax.ShapeDtypeStruct((width, length), BF16),
            jax.ShapeDtypeStruct((heads, 1, length), F32),
            out_t, out_t, out_t, out_t,
        ],
        input_output_aliases={6 + n: n for n in range(len(kept))},
        compiler_params=params(),
        cost_estimate=cost(count * 4 * length * length * LANES, 8 * length * count * LANES),
        name="attend",
    )(scal, seg_row, seg_col, qt, k, vt, *kept)


def attend_back_kernel(
    step, scal, seg_row, seg_col, qt_ref, kt_ref, k_ref, v_ref, ot_ref, lse_ref,
    d0, d1, d2, d3, dq_ref, dk_ref, dv_ref, grad_t, dk_sum, dv_sum,
):
    h = pl.program_id(0)
    length = qt_ref.shape[1]

    @pl.when(h == 0)
    def _():
        rows = d0.shape[0]
        for x, ref in enumerate((d0, d1, d2, d3)):
            at = pl.multiple_of((scal[1] ^ x) * rows, rows)
            grad_t[:, pl.ds(at, rows)] = ref[...].astype(F32).T.astype(BF16)

    mine = grad_t[pl.ds(pl.multiple_of(h * HD, 16), HD), :]
    row_dot = jnp.sum(mine.astype(F32) * ot_ref[...].astype(F32), axis=0, keepdims=True)
    for i in range(length // step):
        start, last = i * step, (i + 1) * step
        grad, query = mine[:, start:last], qt_ref[:, start:last]
        s = nn(k_ref[:last, :HD], query)
        dp = nn(v_ref[:last, :HD], grad)
        s = jnp.where(allowed_mask(seg_row, seg_col, last, start, step), s, NEG)
        p = jnp.exp2(s - lse_ref[0, :, start:last])
        ds = (p * (dp - row_dot[:, start:last])).astype(BF16)
        dv = nt(grad, p.astype(BF16))
        dk = nt(query, ds)
        dq = nn(kt_ref[:, :last], ds)
        if start:
            dv_sum[:, :start] += dv[:, :start]
            dk_sum[:, :start] += dk[:, :start]
        dv_sum[:, start:last] = dv[:, start:]
        dk_sum[:, start:last] = dk[:, start:]
        dq_ref[:, start:last] = (dq * SCORE_SCALE).astype(BF16)
    dk_ref[...] = (dk_sum[...] * (1.0 / LOG2E)).astype(BF16)
    dv_ref[...] = dv_sum[...].astype(BF16)


def attend_back_call(scal, seg_row, seg_col, qt, kt, k, v, ot, lse, grads):
    width, length = qt.shape
    heads = width // HD
    rows = grads[0].shape[0]
    row = pl.BlockSpec((length, LANES), lambda h, s: (0, h))
    col = pl.BlockSpec((HD, length), lambda h, s: (h, 0))
    col_t = jax.ShapeDtypeStruct((width, length), BF16)
    return pl.pallas_call(
        functools.partial(attend_back_kernel, 256),
        grid_spec=pltpu.PrefetchScalarGridSpec(
            num_scalar_prefetch=1,
            grid=(heads,),
            in_specs=[
                whole((1, length)), whole((length, 1)), col, col, row, row, col,
                pl.BlockSpec((1, 1, length), lambda h, s: (h, 0, 0)),
            ]
            + [whole((rows, width))] * 4,
            out_specs=[col, col, col],
            scratch_shapes=[
                pltpu.VMEM((width, length), BF16),
                pltpu.VMEM((HD, length), F32),
                pltpu.VMEM((HD, length), F32),
            ],
        ),
        out_shape=[col_t, col_t, col_t],
        compiler_params=params(),
        cost_estimate=cost(heads * 8 * length * length * LANES, 16 * length * width),
        name="attend_back",
    )(scal, seg_row, seg_col, qt, kt, k, v, ot, lse, *grads)


def middle_kernel(
    scal, x_ref, g_ref, a0, a1, a2, a3, b0, b1, b2, b3, s0, s1, s2, s3, w0, w1, w2, w3,
    orr, ulr, drr,
    act_ref, gm_ref, o0, o1, o2, o3, e0, e1, e2, e3,
    wo, wu, wd, ol, ur, dl, sems,
):
    width = o0.shape[1]
    rank = orr.shape[1]
    copies = []
    for n, dst in enumerate((wo, wu, wd)):
        for x, src in enumerate((w0, w1, w2, w3)):
            copies.append(
                pltpu.make_async_copy(
                    src.at[pl.ds(n * width, width)],
                    dst.at[pl.ds(x * width, width)],
                    sems.at[n * 4 + x],
                )
            )
    for copy in copies:
        copy.start()

    def arrived(n):
        for copy in copies[4 * n : 4 * n + 4]:
            copy.wait()

    for x, src in enumerate((s0, s1, s2, s3)):
        for slot, dst in enumerate((ol, ur, dl)):
            dst[:, x * width : (x + 1) * width] = src[:, slot * SLOT : slot * SLOT + width].astype(F32)
    out_lower, up_raise, down_lower = (r[...].astype(BF16) for r in (ol, ur, dl))
    out_raise, up_lower, down_raise = orr[0], ulr[0], drr[0]
    grad = g_ref[...]
    parts = [r[...].astype(F32) for r in (a0, b0, a1, b1, a2, b2, a3, b3)]
    att = jnp.concatenate(parts, axis=1).astype(BF16)
    low_out = nt(att, out_lower).astype(BF16)
    grad_low_down = nt(grad, down_raise).astype(BF16)
    arrived(0)
    middle = x_ref[...].astype(F32) + (nn(att, wo[...]) + nn(low_out, out_raise))
    factor = lax.rsqrt(jnp.mean(middle * middle, axis=-1, keepdims=True) + EPS)
    unit = middle * factor
    normed = unit.astype(BF16)
    low_up = nt(normed, up_lower).astype(BF16)
    arrived(1)
    preact = nt(normed, wu[...]) + nn(low_up, up_raise)
    sigma = 1.0 / (1.0 + jnp.exp(-preact))
    active = (preact * sigma).astype(BF16)
    arrived(2)
    low_down = nt(active, down_lower).astype(BF16)
    grad_act = nt(grad, wd[...]) + nn(grad_low_down, down_lower)
    grad_pre = (grad_act * (sigma * (1.0 + preact * (1.0 - sigma)))).astype(BF16)
    grad_low_up = nt(grad_pre, up_raise).astype(BF16)
    grad_mid = nn(grad_pre, wu[...]) + nn(grad_low_up, up_lower)
    act_ref[...] = (middle + (nn(active, wd[...]) + nn(low_down, down_raise))).astype(BF16)
    dot = jnp.mean(grad_mid * unit, axis=-1, keepdims=True)
    grad_middle = grad.astype(F32) + factor * (grad_mid - unit * dot)
    gm_ref[...] = grad_middle
    grad_attn = grad_middle.astype(BF16)
    grad_low_out = nt(grad_attn, out_raise).astype(BF16)
    grad_att = nt(grad_attn, wo[...]) + nn(grad_low_out, out_lower)
    for x, ref in enumerate((o0, o1, o2, o3)):
        ref[...] = grad_att[:, x * width : (x + 1) * width].astype(BF16)

    packs = (e0, e1, e2, e3)
    for n, (low, value) in enumerate(
        ((low_out, grad_attn), (grad_low_up, normed), (low_down, grad))
    ):
        part = tn(low, value).astype(BF16)
        for ref in packs:
            ref[n * rank : (n + 1) * rank] = part
    for x, ref in enumerate(packs):
        mark = jnp.full((rank, ref.shape[1]), scal[0], jnp.int32).astype(F32)
        ref[3 * rank :] = (jnp.zeros_like(mark) if x else mark).astype(BF16)
    for slot, (low, value) in enumerate(
        ((grad_low_out, att), (low_up, grad_pre), (grad_low_down, active))
    ):
        part = tn(low, value)
        for x, ref in enumerate(packs):
            piece = part[:, x * width : (x + 1) * width].astype(BF16)
            ref[3 * rank :, slot * SLOT : slot * SLOT + width] = piece


def middle_call(scal, x, g, att, pieces, weights, out_raise, up_lower, down_raise):
    rows, depth = x.shape
    width = 2 * att[0].shape[1]
    rank = out_raise.shape[1]
    wide = whole((rows, depth))
    part = whole((rows, width))
    small = pl.BlockSpec((rank, depth), lambda c, s: (rows // rank, 0))
    pick = pl.BlockSpec((1, rank, depth), lambda c, s: (s[0], 0, 0))
    any_spec = pl.BlockSpec(memory_space=pl.ANY)
    part_t = jax.ShapeDtypeStruct((rows, width), BF16)
    pack_t = jax.ShapeDtypeStruct((4 * rank, depth), BF16)
    square = pltpu.VMEM((4 * width, depth), BF16)
    thin = pltpu.VMEM((rank, depth), F32)
    return pl.pallas_call(
        middle_kernel,
        grid_spec=pltpu.PrefetchScalarGridSpec(
            num_scalar_prefetch=1,
            grid=(1,),
            in_specs=[wide, wide] + [whole((rows, width // 2))] * 8 + [small] * 4
            + [any_spec] * 4 + [pick] * 3,
            out_specs=[wide, wide] + [part] * 4 + [whole((4 * rank, depth))] * 4,
            scratch_shapes=[
                square, square, square, thin, thin, thin,
                pltpu.SemaphoreType.DMA((12,)),
            ],
        ),
        out_shape=[
            jax.ShapeDtypeStruct((rows, depth), BF16),
            jax.ShapeDtypeStruct((rows, depth), F32),
        ]
        + [part_t] * 4
        + [pack_t] * 4,
        compiler_params=params(),
        cost_estimate=cost(12 * rows * depth * depth, 6 * depth * depth + 12 * rows * depth),
        name="feed_forward",
    )(scal, x, g, *att, *pieces, *weights, out_raise, up_lower, down_raise)


def adapter_kernel(
    scal, dq, dk, dv, low, p0, p1, p2, p3, rq, rk, rv,
    back_ref, pack_ref, buf, sems, lower_sum, raise_sum,
):
    step = pl.program_id(0)
    bring(copies_of((p0, p1, p2, p3), buf, sems))

    @pl.when(step == 0)
    def _():
        lower_sum[...] = jnp.zeros_like(lower_sum)
        raise_sum[...] = jnp.zeros_like(raise_sum)

    rank, width = rq.shape[1:]
    parts = []
    for n, (d, r) in enumerate(((dq, rq), (dk, rk), (dv, rv))):
        value = d[...]
        parts.append(nn(r[0], value))
        raise_sum[:, n * SLOT : n * SLOT + width] += nt(low[n * rank : (n + 1) * rank], value)
    back = jnp.concatenate(parts, axis=0).astype(BF16)
    back_ref[...] = back
    lower_sum[...] += nn(back, buf[step])

    @pl.when(step == pl.num_programs(0) - 1)
    def _():
        pack_ref[: 3 * rank] = lower_sum[...].astype(BF16)
        pack_ref[3 * rank :] = raise_sum[...].astype(BF16)


def adapter_call(scal, grads, low, pieces, raises, rows):
    depth = pieces[0].shape[1]
    width, length = grads[0].shape
    rank = raises[0].shape[1]
    any_spec = pl.BlockSpec(memory_space=pl.ANY)
    raise_ = pl.BlockSpec((1, rank, width), lambda g, s: (s[0], 0, 0))
    col = pl.BlockSpec((width, rows), lambda g, s: (0, s[1] ^ g))
    thin = pl.BlockSpec((3 * rank, rows), lambda g, s: (0, s[1] ^ g))
    return pl.pallas_call(
        adapter_kernel,
        grid_spec=pltpu.PrefetchScalarGridSpec(
            num_scalar_prefetch=1,
            grid=(4,),
            in_specs=[col] * 3 + [thin] + [any_spec] * 4 + [raise_] * 3,
            out_specs=[thin, whole((4 * rank, depth))],
            scratch_shapes=[
                pltpu.VMEM((4, rows, depth), BF16),
                pltpu.SemaphoreType.DMA((4,)),
                pltpu.VMEM((3 * rank, depth), F32),
                pltpu.VMEM((rank, depth), F32),
            ],
        ),
        out_shape=[
            jax.ShapeDtypeStruct((3 * rank, length), BF16),
            jax.ShapeDtypeStruct((4 * rank, depth), BF16),
        ],
        compiler_params=params(),
        cost_estimate=cost(8 * length * depth * 3 * rank, 4 * length * depth),
        name="adapter_gradients",
    )(scal, *grads, low, *pieces, *raises)


def grad_in_kernel(scal, dq, dk, dv, back, stack, out_ref):
    value = jnp.concatenate([dq[...], dk[...], dv[...], back[...]], axis=0)
    out_ref[0] = tn(value, stack[...]).astype(BF16)


def grad_in_call(scal, grads, back, stack, first, rows):
    width = grads[0].shape[0]
    total, depth = stack.shape
    col = pl.BlockSpec((width, rows), lambda g, s: (0, s[1] ^ (g + first)))
    thin = pl.BlockSpec((back.shape[0], rows), lambda g, s: (0, s[1] ^ (g + first)))
    return pl.pallas_call(
        grad_in_kernel,
        grid_spec=pltpu.PrefetchScalarGridSpec(
            num_scalar_prefetch=1,
            grid=(2,),
            in_specs=[col] * 3 + [thin, whole((total, depth))],
            out_specs=pl.BlockSpec((1, rows, depth), lambda g, s: (g, 0, 0)),
        ),
        out_shape=jax.ShapeDtypeStruct((2, rows, depth), BF16),
        compiler_params=params(),
        cost_estimate=cost(4 * rows * depth * total, 12 * rows * depth),
        name="grad_input",
    )(scal, *grads, back, stack)


def last_kernel(x_ref, gm_ref, a_ref, b_ref, c_ref, out_ref):
    x = x_ref[...].astype(F32)
    factor = lax.rsqrt(jnp.mean(x * x, axis=-1, keepdims=True) + EPS)
    unit = x * factor
    grad = a_ref[0].astype(F32) + b_ref[...].astype(F32) + c_ref[...].astype(F32)
    dot = jnp.mean(grad * unit, axis=-1, keepdims=True)
    out_ref[...] = (gm_ref[...] + factor * (grad - unit * dot)).astype(BF16)


def last_call(x, gm, a, b, c):
    rows, depth = x.shape
    step = 128
    wide = pl.BlockSpec((step, depth), lambda g: (g, 0))
    return pl.pallas_call(
        last_kernel,
        grid=(rows // step,),
        in_specs=[wide, wide, pl.BlockSpec((1, step, depth), lambda g: (0, g, 0)), wide, wide],
        out_specs=wide,
        out_shape=jax.ShapeDtypeStruct((rows, depth), BF16),
        compiler_params=params(),
        name="input_gradient",
    )(x, gm, a, b, c)


def sets_kernel(mark_ref, pack_ref, *outs):
    j = pl.program_id(0)
    rank = outs[0].shape[1]
    depth = mark_ref.shape[2]
    total = jnp.zeros(pack_ref.shape[1:], F32)
    for n in range(pack_ref.shape[0]):
        chosen = mark_ref[n, 3 * rank : 3 * rank + 1, depth - 1 : depth].astype(F32)
        pick = (chosen == j.astype(F32)).astype(F32)
        total = total + pack_ref[n].astype(F32) * pick
    for k in range(3):
        outs[k][0] = total[k * rank : (k + 1) * rank]
        width = outs[3 + k].shape[2]
        outs[3 + k][0] = total[3 * rank :, k * SLOT : k * SLOT + width]


def sets_call(marks, packs, sets, width):
    parts, four, depth = packs.shape
    rank = four // 4
    full = pl.BlockSpec((1, rank, depth), lambda j: (j, 0, 0))
    thin = pl.BlockSpec((1, rank, width), lambda j: (j, 0, 0))
    full_t = jax.ShapeDtypeStruct((sets, rank, depth), F32)
    thin_t = jax.ShapeDtypeStruct((sets, rank, width), F32)
    return pl.pallas_call(
        sets_kernel,
        grid=(sets,),
        in_specs=[whole(marks.shape), whole(packs.shape)],
        out_specs=[full, full, full, thin, thin, thin],
        out_shape=[full_t, full_t, full_t, thin_t, thin_t, thin_t],
        compiler_params=params(),
        name="set_sums",
    )(marks, packs)


def on_device(
    dp_count,
    tensor_count,
    tokens,
    segment_ids,
    adapter_choice,
    cotangent,
    weight_query,
    weight_key,
    weight_value,
    weight_output,
    weight_upward,
    weight_downward,
    query_lower,
    query_raise,
    key_lower,
    key_raise,
    value_lower,
    value_raise,
    output_lower,
    output_raise,
    upward_lower,
    upward_raise,
    downward_lower,
    downward_raise,
):
    across = functools.partial(swap, axis_name="tensor", count=tensor_count)
    x, g = tokens[0], cotangent[0]
    rows = x.shape[0]
    length = segment_ids.shape[1]
    sets, rank = query_lower.shape[:2]
    me = lax.axis_index("tensor").astype(jnp.int32)
    scal = jnp.stack([adapter_choice[0], me])
    seg_row = segment_ids
    seg_col = segment_ids.reshape(length, 1)

    own = norm_call(x, adapter_choice, output_lower, upward_raise, downward_lower)
    far = across(own, bit=2)
    near = across(own, bit=1)
    out_t, up_t, down_t, own = lax.optimization_barrier(
        (weight_output.T, weight_upward.T, weight_downward.T, own)
    )
    wt = jnp.concatenate([out_t, up_t, down_t], axis=0)
    share = wt.shape[0] // dp_count
    mine = lax.dynamic_slice_in_dim(wt, lax.axis_index("dp") * share, share, 0)
    fetched = across(mine, bit=2)
    wt_far = lax.all_gather(fetched, "dp", axis=0, tiled=True)
    wt_near = across(wt, bit=1)

    lowers = (query_lower, key_lower, value_lower)
    raises = (query_raise, key_raise, value_raise)
    weights = (weight_query.T, weight_key.T, weight_value.T)
    *so_far, stack = project_call(
        scal, 0, (own, near), weights, lowers, None, raises, None, rows, length
    )
    cross = across(far, bit=1)
    pieces = (own, near, far, cross)
    qt, kt, vt, k, v, low = project_call(
        scal, 2, (far, cross), None, None, stack, raises, so_far, rows, length
    )
    heads = qt.shape[0] // HD
    half = heads // 2
    ot, lse, *att = attend_call(scal, seg_row, seg_col, qt, k, vt, 0, half, None, rows)
    left = [att[0]] + [across(att[n], bit=n) for n in (1, 2, 3)]
    ot, lse, *att = attend_call(scal, seg_row, seg_col, qt, k, vt, half, half, (ot, lse), rows)
    wt_far, att[0] = lax.optimization_barrier((wt_far, att[0]))
    wt_cross = across(wt_far, bit=1)
    right = [att[0]] + [across(att[n], bit=n) for n in (1, 2, 3)]
    act, grad_middle, *more = middle_call(
        scal, x, g, (*left, *right), pieces, (wt, wt_near, wt_far, wt_cross),
        output_raise, upward_lower, downward_raise,
    )
    grads, packs = more[:4], more[4:]
    grads = [grads[0]] + [across(grads[n], bit=n) for n in (1, 2, 3)]
    back = attend_back_call(scal, seg_row, seg_col, qt, kt, k, v, ot, lse, grads)

    packs = [packs[0]] + [across(packs[n], bit=n) for n in (1, 2, 3)]
    packs = [p.astype(F32) for p in packs]
    first = ((packs[0] + packs[1]) + (packs[2] + packs[3])).astype(BF16)
    first_all = lax.all_gather(first, "dp", axis=0)

    low_back, pack = adapter_call(scal, back, low, pieces, raises, rows)
    lower_part = pack[: 3 * rank]
    others = [across(lower_part, bit=n).astype(F32) for n in (1, 2, 3)]
    lower_sum = (lower_part.astype(F32) + others[0]) + (others[1] + others[2])
    second = jnp.concatenate([lower_sum.astype(BF16), pack[3 * rank :]], axis=0)
    second_all = lax.all_gather(second, "dp", axis=0)

    partial_far = grad_in_call(scal, back, low_back, stack, 2, rows)
    near_far = across(partial_far[1], bit=1)
    to_far = (partial_far[0].astype(F32) + near_far.astype(F32)).astype(BF16)
    from_far = across(to_far, bit=2)
    partial = grad_in_call(scal, back, low_back, stack, 0, rows)
    near_mine = across(partial[1], bit=1)
    input_grad = last_call(x, grad_middle, partial, near_mine, from_far)

    out = list(sets_call(first_all, first_all, sets, query_raise.shape[2]))
    out += sets_call(first_all, second_all, sets, query_raise.shape[2])
    (out_raise_g, up_lower_g, down_raise_g, out_lower_g, up_raise_g, down_lower_g) = out[:6]
    (q_lower_g, k_lower_g, v_lower_g, q_raise_g, k_raise_g, v_raise_g) = out[6:]
    return (
        act[None],
        input_grad[None],
        q_lower_g,
        q_raise_g,
        k_lower_g,
        k_raise_g,
        v_lower_g,
        v_raise_g,
        out_lower_g,
        out_raise_g,
        up_lower_g,
        up_raise_g,
        down_lower_g,
        down_raise_g,
    )


def solution(mesh):
    split = P(None, None, "tensor")
    return jax.shard_map(
        functools.partial(on_device, mesh.shape["dp"], mesh.shape["tensor"]),
        mesh=mesh,
        in_specs=(
            P("dp", "tensor", None),
            P("dp", None),
            P("dp"),
            P("dp", "tensor", None),
            P(None, "tensor"),
            P(None, "tensor"),
            P(None, "tensor"),
            P(None, "tensor"),
            P(None, "tensor"),
            P(None, "tensor"),
            P(),
            split,
            P(),
            split,
            P(),
            split,
            split,
            P(),
            P(),
            split,
            split,
            P(),
        ),
        out_specs=(
            P("dp", "tensor", None),
            P("dp", "tensor", None),
            P(),
            split,
            P(),
            split,
            P(),
            split,
            split,
            P(),
            P(),
            split,
            split,
            P(),
        ),
        check_vma=False,
    )
```

```python
import functools
import math

import jax
import jax.numpy as jnp
from jax import lax
from jax.experimental import pallas as pl
from jax.experimental.pallas import tpu as pltpu
from jax.sharding import PartitionSpec as P

HD = 80
LANES = 128
EPS = 1e-06
NEG = -1e30
F32 = jnp.float32
BF16 = jnp.bfloat16
VMEM_BYTES = 60 * 2**20
SCORE_SCALE = HD ** (-0.5)
LOG2E = math.log2(math.e)
SLOT = 384
UNIT = 16
MESH = pl.DeviceIdType.MESH

NT = (((1,), (1,)), ((), ()))
TN = (((0,), (0,)), ((), ()))


def nn(left, right):
    return jnp.dot(left, right, preferred_element_type=F32)


def nt(left, right):
    return lax.dot_general(left, right, NT, preferred_element_type=F32)


def tn(left, right):
    return lax.dot_general(left, right, TN, preferred_element_type=F32)


def params(**more):
    return pltpu.CompilerParams(vmem_limit_bytes=VMEM_BYTES, **more)


def talking(number):
    return params(collective_id=number, has_side_effects=True)


def whole(shape):
    return pl.BlockSpec(shape, lambda *_: (0,) * len(shape))


ANY = pl.BlockSpec(memory_space=pl.ANY)
VMEM = pl.BlockSpec(memory_space=pltpu.VMEM)
DMA = pltpu.SemaphoreType.DMA


def across(bit):
    return {"tensor": lax.axis_index("tensor") ^ bit}


def along(step, count):
    return {"dp": lax.rem(lax.axis_index("dp") + step, count)}


def greet(peers):
    barrier = pltpu.get_barrier_semaphore()
    for peer in peers:
        pl.semaphore_signal(barrier, inc=1, device_id=peer, device_id_type=MESH)
    pl.semaphore_wait(barrier, len(peers))


def send(src, dst, send_sem, recv_sem, peer):
    return pltpu.make_async_remote_copy(
        src_ref=src, dst_ref=dst, send_sem=send_sem, recv_sem=recv_sem,
        device_id=peer, device_id_type=MESH,
    )


def place(bit, rows):
    return pl.multiple_of((lax.axis_index("tensor") ^ bit) * rows, rows)


def start_kernel(
    units, choice, x_ref, ql, kl, vl, orr, ul, dr, qr, kr, vr, ol, ur, dl, wo, wu, wd,
    own_ref, sel_ref, raise_ref, fetched_ref, mine, sems, sent, got,
):
    per_weight = wo.shape[0] // UNIT
    first = lax.axis_index("dp") * units

    def piece(u):
        return mine.at[pl.ds(u * UNIT, UNIT)]

    for u in range(units):
        number = lax.rem(first + u, 3 * per_weight)
        for n, w in enumerate((wo, wu, wd)):

            @pl.when(number // per_weight == n)
            def _(u=u, n=n, w=w, number=number):
                at = pl.multiple_of((number - n * per_weight) * UNIT, UNIT)
                pltpu.make_async_copy(w.at[pl.ds(at, UNIT)], piece(u), sems.at[u]).start()

    greet([across(2)])
    for u in range(units):
        pltpu.make_async_copy(wo.at[pl.ds(0, UNIT)], piece(u), sems.at[u]).wait()
    far = send(mine, fetched_ref, sent, got, across(2))
    far.start()

    rows = x_ref.shape[0]
    rank, width = ol.shape[1:]
    which = choice[0]
    x = x_ref[...].astype(F32)
    factor = lax.rsqrt(jnp.mean(x * x, axis=-1, keepdims=True) + EPS)
    own_ref[:rows] = (x * factor).astype(BF16)
    own_ref[rows:] = jnp.zeros_like(own_ref[rows:])
    for slot, ref in enumerate((ol, ur, dl)):
        own_ref[rows:, slot * SLOT : slot * SLOT + width] = ref[which]
    for n, ref in enumerate((ql, kl, vl, orr, ul, dr)):
        sel_ref[n * rank : (n + 1) * rank] = ref[which]
    mark = jnp.full((rank, x.shape[1]), which, jnp.int32).astype(F32)
    sel_ref[6 * rank :] = mark.astype(BF16)
    for n, ref in enumerate((qr, kr, vr)):
        raise_ref[n * rank : (n + 1) * rank] = ref[which]
    far.wait()


def start_call(dp_count, choice, x, wides, narrows, weights):
    rows, depth = x.shape
    rank, width = narrows[0].shape[1:]
    units = -(-3 * width // (UNIT * dp_count))
    fetched = jax.ShapeDtypeStruct((units * UNIT, depth), BF16)
    return pl.pallas_call(
        functools.partial(start_kernel, units),
        in_specs=[pl.BlockSpec(memory_space=pltpu.SMEM), VMEM] + [VMEM] * 12 + [ANY] * 3,
        out_specs=[VMEM, VMEM, VMEM, ANY],
        out_shape=[
            jax.ShapeDtypeStruct((rows + rank, depth), BF16),
            jax.ShapeDtypeStruct((7 * rank, depth), BF16),
            jax.ShapeDtypeStruct((3 * rank, width), BF16),
            fetched,
        ],
        scratch_shapes=[
            pltpu.VMEM(fetched.shape, BF16), DMA((units,)), DMA, DMA,
        ],
        compiler_params=talking(0),
        name="start",
    )(choice, x, *wides, *narrows, *weights)


def project_kernel(
    heads, own, wq, wk, wv, sel, rsel,
    qt_out, kt_out, vt_out, k_out, v_out, low_out, stack_out, near_out, far_out, cross_out,
    near, far, cross, stack, qt, kt, vt, k, v, low, sent, got, local,
):
    width = heads * HD
    rank = rsel.shape[0] // 3
    rows = own.shape[0] - rank
    half = rows // 2
    cuts = ((0, half), (half, rows + rank - half))

    def part(ref, c):
        return ref.at[pl.ds(*cuts[c])]

    greet([across(1), across(2)])
    to_far = [send(part(own, c), part(far, c), sent.at[c], got.at[c], across(2)) for c in (0, 1)]
    to_near = send(own, near, sent.at[2], got.at[2], across(1))
    on = [send(part(far, c), part(cross, c), sent.at[3 + c], got.at[3 + c], across(1)) for c in (0, 1)]
    for copy in to_far:
        copy.start()
    to_near.start()

    at = 0
    for ref in (wq, wk, wv):
        stack[at : at + width] = ref[...]
        at += width
    stack[at:] = sel[: 3 * rank]
    pending = [pltpu.make_async_copy(stack, stack_out, local.at[0])]
    pending[0].start()

    def keep(src, dst):
        copy = pltpu.make_async_copy(src, dst, local.at[len(pending)])
        copy.start()
        pending.append(copy)

    def project(ref, bit, c):
        block = ref[c * half : (c + 1) * half]
        out = nt(stack[...], block)
        down = out[3 * width :].astype(BF16)
        start = pl.multiple_of(place(bit, rows) + c * half, half)
        here = pl.ds(start, half)
        low[:, here] = down
        for n, (col, row) in enumerate(((qt, None), (kt, k), (vt, v))):
            low_n = slice(n * rank, (n + 1) * rank)
            value = out[n * width : (n + 1) * width] + tn(rsel[low_n], down[low_n])
            if n == 0:
                value = value * (SCORE_SCALE * LOG2E)
            value = value.astype(BF16)
            col[:, here] = value
            if row is not None:
                for h in range(heads):
                    row[here, h * LANES : h * LANES + HD] = value[h * HD : (h + 1) * HD].T
        for src, dst in ((qt, qt_out), (kt, kt_out), (vt, vt_out), (low, low_out)):
            keep(src.at[:, here], dst.at[:, here])
        for src, dst in ((k, k_out), (v, v_out)):
            keep(src.at[here], dst.at[here])

    project(own, 0, 0)
    project(own, 0, 1)
    to_near.wait_recv()
    keep(near, near_out)
    project(near, 1, 0)
    project(near, 1, 1)
    for c in (0, 1):
        to_far[c].wait_recv()
        on[c].start()
        keep(part(far, c), part(far_out, c))
        project(far, 2, c)
        on[c].wait_recv()
        keep(part(cross, c), part(cross_out, c))
        project(cross, 3, c)
    for copy in (*to_far, to_near, *on):
        copy.wait_send()
    for copy in pending:
        copy.wait()


def project_call(own, weights, sel, rsel, length):
    depth = own.shape[1]
    rank, width = rsel.shape[0] // 3, rsel.shape[1]
    heads = width // HD
    total = 3 * (width + rank)
    shapes = [
        (width, length), (width, length), (width, length),
        (length, heads * LANES), (length, heads * LANES), (3 * rank, length), (total, depth),
    ] + [own.shape] * 3
    kinds = [jax.ShapeDtypeStruct(s, BF16) for s in shapes]
    return pl.pallas_call(
        functools.partial(project_kernel, heads),
        in_specs=[VMEM] * 6,
        out_specs=[ANY] * 10,
        out_shape=kinds,
        scratch_shapes=[pltpu.VMEM(own.shape, BF16)] * 3
        + [pltpu.VMEM((total, depth), BF16)]
        + [pltpu.VMEM(s, BF16) for s in shapes[:6]]
        + [DMA((5,)), DMA((5,)), DMA((1 + 8 * 6 + 5,))],
        compiler_params=talking(1),
        name="project",
    )(own, *weights, sel, rsel)


def allowed_mask(seg_row, seg_col, last, start, size):
    key = lax.broadcasted_iota(jnp.int32, (last, size), 0)
    query = lax.broadcasted_iota(jnp.int32, (last, size), 1) + start
    return (seg_col[:last, :] == seg_row[:, start : start + size]) & (key <= query)


def attend_kernel(
    step, heads, seg_row, seg_col, qt_ref, k_ref, vt_ref, ot_ref, lse_ref, att_ref,
    wide, sent, got, local,
):
    h = pl.program_id(0)
    length = qt_ref.shape[1]
    rows = att_ref.shape[1]
    width = heads * HD

    @pl.when(h == 0)
    def _():
        greet([across(1), across(2), across(3)])

    for i in range(length // step):
        start, last = i * step, (i + 1) * step
        s = nn(k_ref[:last, :HD], qt_ref[:, start:last])
        s = jnp.where(allowed_mask(seg_row, seg_col, last, start, step), s, NEG)
        top = jnp.max(s, axis=0, keepdims=True)
        p = jnp.exp2(s - top)
        total = jnp.sum(p, axis=0, keepdims=True)
        out = (nn(vt_ref[:, :last], p.astype(BF16)) / total).astype(BF16)
        ot_ref[:, start:last] = out
        wide[pl.ds(pl.multiple_of(h * HD, UNIT), HD), start:last] = out
        lse_ref[0, :, start:last] = top + jnp.log2(total)

    def piece(bit, head):
        src = wide.at[pl.ds(pl.multiple_of(head * HD, UNIT), HD), pl.ds(place(bit, rows), rows)]
        dst = att_ref.at[pl.ds(pl.multiple_of(bit * width + head * HD, UNIT), HD)]
        if bit == 0:
            return pltpu.make_async_copy(src, dst, local.at[head])
        return send(src, dst, sent.at[bit - 1, head], got.at[bit - 1, head], across(bit))

    for bit in (2, 3, 1, 0):
        piece(bit, h).start()

    @pl.when(h == heads - 1)
    def _():
        for head in range(heads):
            for bit in range(4):
                piece(bit, head).wait()


def attend_call(seg_row, seg_col, qt, k, vt, rows):
    width, length = qt.shape
    heads = width // HD
    col = pl.BlockSpec((HD, length), lambda h: (h, 0))
    return pl.pallas_call(
        functools.partial(attend_kernel, 512, heads),
        grid=(heads,),
        in_specs=[
            whole((1, length)), whole((length, 1)), col,
            pl.BlockSpec((length, LANES), lambda h: (0, h)), col,
        ],
        out_specs=[col, pl.BlockSpec((1, 1, length), lambda h: (h, 0, 0)), ANY],
        scratch_shapes=[
            pltpu.VMEM((width, length), BF16), DMA((3, heads)), DMA((3, heads)), DMA((heads,)),
        ],
        out_shape=[
            jax.ShapeDtypeStruct((width, length), BF16),
            jax.ShapeDtypeStruct((heads, 1, length), F32),
            jax.ShapeDtypeStruct((4 * width, rows), BF16),
        ],
        compiler_params=talking(2),
        name="attend",
    )(seg_row, seg_col, qt, k, vt)


def attend_back_kernel(
    step, dp_count, seg_row, seg_col, qt_ref, kt_ref, k_ref, v_ref, ot_ref, lse_ref, grad_ref, pack_ref,
    dq_ref, dk_ref, dv_ref, all_ref, other_ref, dk_sum, dv_sum, sent, got, local, near_sems,
):
    h = pl.program_id(0)
    last_step = pl.num_programs(0) - 1
    length = qt_ref.shape[1]
    shared = other_ref.shape[1]
    mine = all_ref.at[lax.axis_index("dp")]
    keep = pltpu.make_async_copy(pack_ref, mine, local)
    spread = [
        send(pack_ref, mine, sent.at[n - 1], got.at[n - 1], along(n, dp_count))
        for n in range(1, dp_count)
    ]
    pair = send(
        all_ref.at[:, pl.ds(0, shared)], other_ref, near_sems.at[0], near_sems.at[1], across(1)
    )

    @pl.when(h == 0)
    def _():
        greet([across(1)] + [along(n, dp_count) for n in range(1, dp_count)])
        keep.start()
        for copy in spread:
            copy.start()

    @pl.when(h == last_step)
    def _():
        keep.wait()
        for copy in spread:
            copy.wait()
        pair.start()

    row_dot = jnp.sum(grad_ref[...].astype(F32) * ot_ref[...].astype(F32), axis=0, keepdims=True)
    for i in range(length // step):
        start, last = i * step, (i + 1) * step
        grad, query = grad_ref[:, start:last], qt_ref[:, start:last]
        s = nn(k_ref[:last, :HD], query)
        dp = nn(v_ref[:last, :HD], grad)
        s = jnp.where(allowed_mask(seg_row, seg_col, last, start, step), s, NEG)
        p = jnp.exp2(s - lse_ref[0, :, start:last])
        ds = (p * (dp - row_dot[:, start:last])).astype(BF16)
        dv = nt(grad, p.astype(BF16))
        dk = nt(query, ds)
        dq = nn(kt_ref[:, :last], ds)
        if start:
            dv_sum[:, :start] += dv[:, :start]
            dk_sum[:, :start] += dk[:, :start]
        dv_sum[:, start:last] = dv[:, start:]
        dk_sum[:, start:last] = dk[:, start:]
        dq_ref[:, start:last] = (dq * SCORE_SCALE).astype(BF16)
    dk_ref[...] = (dk_sum[...] * (1.0 / LOG2E)).astype(BF16)
    dv_ref[...] = dv_sum[...].astype(BF16)

    @pl.when(h == last_step)
    def _():
        pair.wait()


def attend_back_call(dp_count, seg_row, seg_col, qt, kt, k, v, ot, lse, grad, pack):
    width, length = qt.shape
    heads = width // HD
    shared = pack.shape[0] * 3 // 5
    row = pl.BlockSpec((length, LANES), lambda h: (0, h))
    col = pl.BlockSpec((HD, length), lambda h: (h, 0))
    col_t = jax.ShapeDtypeStruct((width, length), BF16)
    return pl.pallas_call(
        functools.partial(attend_back_kernel, 256, dp_count),
        grid=(heads,),
        in_specs=[
            whole((1, length)), whole((length, 1)), col, col, row, row, col,
            pl.BlockSpec((1, 1, length), lambda h: (h, 0, 0)), col, ANY,
        ],
        out_specs=[col, col, col, ANY, ANY],
        scratch_shapes=[
            pltpu.VMEM((HD, length), F32),
            pltpu.VMEM((HD, length), F32),
            DMA((dp_count - 1,)), DMA((dp_count - 1,)), DMA, DMA((2,)),
        ],
        out_shape=[
            col_t, col_t, col_t,
            jax.ShapeDtypeStruct((dp_count, *pack.shape), BF16),
            jax.ShapeDtypeStruct((dp_count, shared, pack.shape[1]), BF16),
        ],
        compiler_params=talking(4),
        name="attend_back",
    )(seg_row, seg_col, qt, kt, k, v, ot, lse, grad, pack)


def own_half(half):
    parity = lax.rem(lax.axis_index("tensor"), 2)
    return pl.multiple_of(parity * half, half), pl.multiple_of((1 - parity) * half, half)


def middle_kernel(
    x_ref, g_ref, att_ref, s0, s1, s2, s3, sel, wo_own, wu_own, wd_own, w_far,
    act_ref, gm_ref, grad_out, pack_ref,
    wo, wu, wd, ol, ur, dl, gt, e_sum, whole_b, near_b, half_b, far_b, mine_b, theirs_b,
    w_local, w_sent, w_got, g_sent, g_got, g_local, e_sent, e_got,
):
    width = wo_own.shape[0]
    rank = s0.shape[0]
    rows = x_ref.shape[0]
    half = rows // 2
    me = lax.axis_index("tensor")

    greet([across(1), across(2), across(3)])
    weights = []
    for n, (own, dst) in enumerate(((wo_own, wo), (wu_own, wu), (wd_own, wd))):
        far = w_far.at[pl.ds(n * width, width)]

        def rows_of(x, dst=dst):
            return dst.at[pl.ds(x * width, width)]

        group = [
            send(far, rows_of(3), w_sent.at[n, 1], w_got.at[n, 1], across(1)),
            send(own, rows_of(1), w_sent.at[n, 0], w_got.at[n, 0], across(1)),
            pltpu.make_async_copy(own, rows_of(0), w_local.at[n, 0]),
            pltpu.make_async_copy(far, rows_of(2), w_local.at[n, 1]),
        ]
        for copy in group:
            copy.start()
        weights.append(group)

    def arrived(n):
        for copy in weights[n]:
            copy.wait()

    smalls = (s0, s1, s2, s3)
    for x, src in enumerate(smalls):
        for slot, dst in enumerate((ol, ur, dl)):
            dst[:, x * width : (x + 1) * width] = src[:, slot * SLOT : slot * SLOT + width].astype(F32)
    out_lower, up_raise, down_lower = (r[...].astype(BF16) for r in (ol, ur, dl))
    out_raise, up_lower, down_raise = (
        sel[n * rank : (n + 1) * rank] for n in (3, 4, 5)
    )

    back = {}
    for r in range(2):
        here = slice(r * half, (r + 1) * half)
        grad = g_ref[here]
        att = att_ref[:, here].astype(F32).T.astype(BF16)
        low_out = nt(att, out_lower).astype(BF16)
        grad_low_down = nt(grad, down_raise).astype(BF16)
        if r == 0:
            arrived(0)
        middle = x_ref[here].astype(F32) + (nn(att, wo[...]) + nn(low_out, out_raise))
        factor = lax.rsqrt(jnp.mean(middle * middle, axis=-1, keepdims=True) + EPS)
        unit = middle * factor
        normed = unit.astype(BF16)
        low_up = nt(normed, up_lower).astype(BF16)
        if r == 0:
            arrived(1)
        preact = nt(normed, wu[...]) + nn(low_up, up_raise)
        sigma = 1.0 / (1.0 + jnp.exp(-preact))
        active = (preact * sigma).astype(BF16)
        if r == 0:
            arrived(2)
        low_down = nt(active, down_lower).astype(BF16)
        grad_act = nt(grad, wd[...]) + nn(grad_low_down, down_lower)
        grad_pre = (grad_act * (sigma * (1.0 + preact * (1.0 - sigma)))).astype(BF16)
        grad_low_up = nt(grad_pre, up_raise).astype(BF16)
        grad_mid = nn(grad_pre, wu[...]) + nn(grad_low_up, up_lower)
        dot = jnp.mean(grad_mid * unit, axis=-1, keepdims=True)
        grad_middle = grad.astype(F32) + factor * (grad_mid - unit * dot)
        gm_ref[here] = grad_middle
        grad_attn = grad_middle.astype(BF16)
        grad_low_out = nt(out_raise, grad_attn).astype(BF16)
        for x in (2, 3, 1, 0):
            value = nt(wo[x * width : (x + 1) * width], grad_attn)
            value = value + tn(smalls[x][:, :width], grad_low_out)
            gt[x, :, here] = value.astype(BF16)
            src = gt.at[x, :, pl.ds(r * half, half)]
            dst = grad_out.at[:, pl.ds(pl.multiple_of(me * rows + r * half, half), half)]
            if x:
                copy = send(src, dst, g_sent.at[x - 1, r], g_got.at[x - 1, r], across(x))
            else:
                copy = pltpu.make_async_copy(src, dst, g_local.at[r])
            copy.start()
            back[x, r] = copy
        act_ref[here] = (middle + (nn(active, wd[...]) + nn(low_down, down_raise))).astype(BF16)
        parts = [
            tn(low_out, grad_attn), tn(grad_low_up, normed), tn(low_down, grad),
            nn(grad_low_out, att), tn(low_up, grad_pre), tn(grad_low_down, active),
        ]
        for n, part in enumerate(parts):
            block = slice(n * rank, (n + 1) * rank)
            e_sum[block] = e_sum[block] + part if r else part

    columns = half_b.shape[1]
    keep, give = own_half(columns)
    whole_b[...] = e_sum[: 3 * rank].astype(BF16)
    one = send(whole_b.at[:, pl.ds(give, columns)], near_b, e_sent.at[0], e_got.at[0], across(1))
    one.start()
    quarter = []
    for x in range(4):
        mine_b[x] = jnp.zeros(mine_b.shape[1:], BF16)
        for slot in range(3):
            part = e_sum[(3 + slot) * rank : (4 + slot) * rank, x * width : (x + 1) * width]
            mine_b[x, :, slot * SLOT : slot * SLOT + width] = part.astype(BF16)
        if x:
            copy = send(mine_b.at[x], theirs_b.at[x - 1], e_sent.at[1 + x], e_got.at[1 + x], across(x))
            copy.start()
            quarter.append(copy)
    one.wait()
    half_b[...] = (e_sum[: 3 * rank, pl.ds(keep, columns)] + near_b[...].astype(F32)).astype(BF16)
    two = send(half_b, far_b, e_sent.at[1], e_got.at[1], across(2))
    two.start()
    for copy in quarter:
        copy.wait()
    sums = (mine_b[0].astype(F32) + theirs_b[0].astype(F32)) + (
        theirs_b[1].astype(F32) + theirs_b[2].astype(F32)
    )
    mark = sel[6 * rank :, : SLOT - width].astype(F32)
    sums = jnp.concatenate([sums[:, : sums.shape[1] - mark.shape[1]], mark], axis=1)
    pack_ref[3 * rank : 4 * rank] = sums[:, :columns].astype(BF16)
    pack_ref[4 * rank :] = sums[:, columns:].astype(BF16)
    two.wait()
    pack_ref[: 3 * rank] = (half_b[...].astype(F32) + far_b[...].astype(F32)).astype(BF16)
    for copy in back.values():
        copy.wait()


def middle_call(x, g, att, pieces, sel, weights, w_far, length):
    rows, depth = x.shape
    width = weights[0].shape[0]
    rank = sel.shape[0] // 7
    small = pl.BlockSpec((rank, depth), lambda c: (rows // rank, 0))
    square = pltpu.VMEM((4 * width, depth), BF16)
    thin = pltpu.VMEM((rank, depth), F32)
    pack = (5 * rank, depth // 2)
    halves = pltpu.VMEM((3 * rank, depth // 2), BF16)
    return pl.pallas_call(
        middle_kernel,
        grid=(1,),
        in_specs=[whole((rows, depth))] * 2 + [whole((4 * width, rows))] + [small] * 4
        + [whole(sel.shape)] + [ANY] * 4,
        out_specs=[whole((rows, depth))] * 2 + [ANY, whole(pack)],
        scratch_shapes=[
            square, square, square, thin, thin, thin,
            pltpu.VMEM((4, width, rows), BF16),
            pltpu.VMEM((6 * rank, depth), F32),
            pltpu.VMEM((3 * rank, depth), BF16),
            halves, halves, halves,
            pltpu.VMEM((4, rank, depth), BF16),
            pltpu.VMEM((3, rank, depth), BF16),
            DMA((3, 2)), DMA((3, 2)), DMA((3, 2)),
            DMA((3, 2)), DMA((3, 2)), DMA((2,)), DMA((5,)), DMA((5,)),
        ],
        out_shape=[
            jax.ShapeDtypeStruct((rows, depth), BF16),
            jax.ShapeDtypeStruct((rows, depth), F32),
            jax.ShapeDtypeStruct((width, length), BF16),
            jax.ShapeDtypeStruct(pack, BF16),
        ],
        compiler_params=talking(3),
        name="feed_forward",
    )(x, g, att, *pieces, sel, *weights, w_far)


def tail_kernel(
    dp_count, dq, dk, dv, low, p0, p1, p2, p3, rsel, stack_hbm, x_hbm, gm_hbm,
    out_ref, all_ref, other_ref,
    grads, normed, stack, x_buf, gm_buf, ours, to_near, from_near, to_far, from_far,
    lower_sum, raise_sum, whole_b, near_b, half_b, far_b, pack_b,
    loads, g_sent, g_got, e_sent, e_got, dp_sent, dp_got, last,
):
    rank, width = rsel.shape[0] // 3, rsel.shape[1]
    rows = out_ref.shape[0]
    chunks = from_far.shape[0]
    step = rows // chunks
    shared = 3 * rank
    load = {}
    order = (3, 2, 1, 0)
    for x in order:
        here = pl.ds(place(x, rows), rows)
        for n, src in enumerate((dq, dk, dv)):
            load[x, n] = pltpu.make_async_copy(
                src.at[:, here], grads.at[x, pl.ds(n * width, width)], loads.at[x, n]
            )
        load[x, 3] = pltpu.make_async_copy(
            (p0, p1, p2, p3)[x].at[pl.ds(0, rows)], normed.at[x], loads.at[x, 3]
        )
    load["stack"] = pltpu.make_async_copy(stack_hbm, stack, last.at[0])
    load["x"] = pltpu.make_async_copy(x_hbm, x_buf, last.at[1])
    load["gm"] = pltpu.make_async_copy(gm_hbm, gm_buf, last.at[2])
    for key in [(3, 0), (3, 1), (3, 2), "stack", (2, 0), (2, 1), (2, 2), (3, 3), (2, 3),
                (1, 0), (1, 1), (1, 2), (1, 3), (0, 0), (0, 1), (0, 2), (0, 3), "x", "gm"]:
        load[key].start()
    greet(
        [across(1), across(2)] + [along(n, dp_count) for n in range(1, dp_count)]
    )

    def adapters(x):
        load[x, 3].wait()
        here = pl.ds(place(x, rows), rows)
        for n in range(3):
            value = grads[x, n * width : (n + 1) * width]
            part = nt(low[n * rank : (n + 1) * rank, here], value)
            at = slice(n * SLOT, n * SLOT + width)
            raise_sum[:, at] = part if x == order[0] else raise_sum[:, at] + part
        part = nn(grads[x, 3 * width :], normed[x])
        lower_sum[...] = part if x == order[0] else lower_sum[...] + part

    def through(x):
        for n in range(3):
            load[x, n].wait()
            value = grads[x, n * width : (n + 1) * width]
            grads[x, 3 * width + n * rank : 3 * width + (n + 1) * rank] = nn(
                rsel[n * rank : (n + 1) * rank], value
            ).astype(BF16)
        if x == order[0]:
            load["stack"].wait()
        return tn(grads[x], stack[...])

    pair = [
        send(to_near.at[n], from_near.at[n], g_sent.at[n], g_got.at[n], across(1)) for n in range(2)
    ]
    far = [
        send(to_far.at[c], from_far.at[c], g_sent.at[2 + c], g_got.at[2 + c], across(2))
        for c in range(chunks)
    ]
    raise_sum[...] = jnp.zeros_like(raise_sum)
    to_near[1] = through(3).astype(BF16)
    pair[1].start()
    ours[...] = through(2)
    pair[1].wait()
    for c in range(chunks):
        here = slice(c * step, (c + 1) * step)
        to_far[c] = (ours[here] + from_near[1, here].astype(F32)).astype(BF16)
        far[c].start()
    adapters(3)
    adapters(2)
    to_near[0] = through(1).astype(BF16)
    pair[0].start()
    adapters(1)
    ours[...] = through(0)
    adapters(0)

    columns = half_b.shape[1]
    keep, give = own_half(columns)
    whole_b[...] = lower_sum[...].astype(BF16)
    one = send(whole_b.at[:, pl.ds(give, columns)], near_b, e_sent.at[0], e_got.at[0], across(1))
    one.start()
    pack_b[shared : shared + rank] = raise_sum[:, :columns].astype(BF16)
    pack_b[shared + rank :] = raise_sum[:, columns:].astype(BF16)
    one.wait()
    half_b[...] = (lower_sum[:, pl.ds(keep, columns)] + near_b[...].astype(F32)).astype(BF16)
    two = send(half_b, far_b, e_sent.at[1], e_got.at[1], across(2))
    two.start()
    pair[0].wait()
    ours[...] = ours[...] + from_near[0].astype(F32)
    two.wait()
    pack_b[:shared] = (half_b[...].astype(F32) + far_b[...].astype(F32)).astype(BF16)
    mine = all_ref.at[lax.axis_index("dp")]
    stay = pltpu.make_async_copy(pack_b, mine, last.at[3])
    stay.start()
    spread = [
        send(pack_b, mine, dp_sent.at[n - 1], dp_got.at[n - 1], along(n, dp_count))
        for n in range(1, dp_count)
    ]
    for copy in spread:
        copy.start()

    load["x"].wait()
    load["gm"].wait()
    stay.wait()
    for copy in spread:
        copy.wait()
    swap = send(
        all_ref.at[:, pl.ds(0, shared)], other_ref, e_sent.at[2], e_got.at[2], across(1)
    )
    swap.start()
    for c in range(chunks):
        here = slice(c * step, (c + 1) * step)
        far[c].wait()
        x = x_buf[here].astype(F32)
        factor = lax.rsqrt(jnp.mean(x * x, axis=-1, keepdims=True) + EPS)
        unit = x * factor
        grad = ours[here] + from_far[c].astype(F32)
        dot = jnp.mean(grad * unit, axis=-1, keepdims=True)
        out_ref[here] = (gm_buf[here] + factor * (grad - unit * dot)).astype(BF16)
    swap.wait()


def tail_call(dp_count, grads, low, pieces, rsel, stack, x, gm):
    rows, depth = x.shape
    rank, width = rsel.shape[0] // 3, rsel.shape[1]
    total = stack.shape[0]
    chunks = 4
    pack = (5 * rank, depth // 2)
    halves = pltpu.VMEM((3 * rank, depth // 2), BF16)
    lines = pltpu.VMEM((chunks, rows // chunks, depth), BF16)
    return pl.pallas_call(
        functools.partial(tail_kernel, dp_count),
        in_specs=[ANY] * 3 + [VMEM] + [ANY] * 4 + [VMEM] + [ANY] * 3,
        out_specs=[VMEM, ANY, ANY],
        scratch_shapes=[
            pltpu.VMEM((4, total, rows), BF16),
            pltpu.VMEM((4, rows, depth), BF16),
            pltpu.VMEM((total, depth), BF16),
            pltpu.VMEM((rows, depth), BF16),
            pltpu.VMEM((rows, depth), F32),
            pltpu.VMEM((rows, depth), F32),
            pltpu.VMEM((2, rows, depth), BF16),
            pltpu.VMEM((2, rows, depth), BF16),
            lines, lines,
            pltpu.VMEM((3 * rank, depth), F32),
            pltpu.VMEM((rank, depth), F32),
            pltpu.VMEM((3 * rank, depth), BF16),
            halves, halves, halves,
            pltpu.VMEM(pack, BF16),
            DMA((4, 4)), DMA((2 + chunks,)), DMA((2 + chunks,)), DMA((3,)), DMA((3,)),
            DMA((dp_count - 1,)), DMA((dp_count - 1,)), DMA((4,)),
        ],
        out_shape=[
            jax.ShapeDtypeStruct((rows, depth), BF16),
            jax.ShapeDtypeStruct((dp_count, *pack), BF16),
            jax.ShapeDtypeStruct((dp_count, 3 * rank, depth // 2), BF16),
        ],
        compiler_params=talking(5),
        name="tail",
    )(*grads, low, *pieces, rsel, stack, x, gm)


def sets_kernel(scal, mark_ref, pack_ref, other_ref, *outs):
    j = pl.program_id(0)
    rank = outs[0].shape[1]
    columns = pack_ref.shape[2]
    total = jnp.zeros(pack_ref.shape[1:], F32)
    other = jnp.zeros(other_ref.shape[1:], F32)
    for n in range(pack_ref.shape[0]):
        chosen = mark_ref[n, 4 * rank : 4 * rank + 1, columns - 1 : columns].astype(F32)
        pick = (chosen == j.astype(F32)).astype(F32)
        total = total + pack_ref[n].astype(F32) * pick
        other = other + other_ref[n].astype(F32) * pick
    here = pl.ds(pl.multiple_of(scal[0] * columns, columns), columns)
    there = pl.ds(pl.multiple_of((1 - scal[0]) * columns, columns), columns)
    rows = jnp.concatenate([total[3 * rank : 4 * rank], total[4 * rank :]], axis=1)
    for k in range(3):
        outs[k][0, :, here] = total[k * rank : (k + 1) * rank]
        outs[k][0, :, there] = other[k * rank : (k + 1) * rank]
        width = outs[3 + k].shape[2]
        outs[3 + k][0] = rows[:, k * SLOT : k * SLOT + width]


def sets_call(parity, marks, packs, others, sets, width):
    parts, five, columns = packs.shape
    rank, depth = five // 5, 2 * columns
    full = pl.BlockSpec((1, rank, depth), lambda j, s: (j, 0, 0))
    thin = pl.BlockSpec((1, rank, width), lambda j, s: (j, 0, 0))
    full_t = jax.ShapeDtypeStruct((sets, rank, depth), F32)
    thin_t = jax.ShapeDtypeStruct((sets, rank, width), F32)
    return pl.pallas_call(
        sets_kernel,
        grid_spec=pltpu.PrefetchScalarGridSpec(
            num_scalar_prefetch=1,
            grid=(sets,),
            in_specs=[whole(marks.shape), whole(packs.shape), whole(others.shape)],
            out_specs=[full, full, full, thin, thin, thin],
        ),
        out_shape=[full_t, full_t, full_t, thin_t, thin_t, thin_t],
        compiler_params=params(),
        name="set_sums",
    )(parity, marks, packs, others)


def on_device(
    dp_count,
    tokens,
    segment_ids,
    adapter_choice,
    cotangent,
    weight_query,
    weight_key,
    weight_value,
    weight_output,
    weight_upward,
    weight_downward,
    query_lower,
    query_raise,
    key_lower,
    key_raise,
    value_lower,
    value_raise,
    output_lower,
    output_raise,
    upward_lower,
    upward_raise,
    downward_lower,
    downward_raise,
):
    x, g = tokens[0], cotangent[0]
    rows = x.shape[0]
    length = segment_ids.shape[1]
    sets = query_lower.shape[0]
    width = query_raise.shape[2]
    seg_row = segment_ids
    seg_col = segment_ids.reshape(length, 1)
    parity = lax.rem(lax.axis_index("tensor").astype(jnp.int32), 2).reshape(1)

    feed = (weight_output.T, weight_upward.T, weight_downward.T)
    own, sel, rsel, fetched = start_call(
        dp_count,
        adapter_choice,
        x,
        (query_lower, key_lower, value_lower, output_raise, upward_lower, downward_raise),
        (query_raise, key_raise, value_raise, output_lower, upward_raise, downward_lower),
        feed,
    )
    w_far = lax.all_gather(fetched, "dp", axis=0, tiled=True)
    qt, kt, vt, k, v, low, stack, near, far, cross = project_call(
        own, (weight_query.T, weight_key.T, weight_value.T), sel, rsel, length
    )
    pieces = (own, near, far, cross)
    ot, lse, att = attend_call(seg_row, seg_col, qt, k, vt, rows)
    w_far, att = lax.optimization_barrier((w_far, att))
    act, gm, grad, pack = middle_call(x, g, att, pieces, sel, feed, w_far, length)
    dq, dk, dv, first, first_other = attend_back_call(
        dp_count, seg_row, seg_col, qt, kt, k, v, ot, lse, grad, pack
    )
    input_grad, second, second_other = tail_call(
        dp_count, (dq, dk, dv), low, pieces, rsel, stack, x, gm
    )
    (out_raise_g, up_lower_g, down_raise_g, out_lower_g, up_raise_g, down_lower_g) = sets_call(
        parity, first, first, first_other, sets, width
    )
    (q_lower_g, k_lower_g, v_lower_g, q_raise_g, k_raise_g, v_raise_g) = sets_call(
        parity, first, second, second_other, sets, width
    )
    return (
        act[None],
        input_grad[None],
        q_lower_g,
        q_raise_g,
        k_lower_g,
        k_raise_g,
        v_lower_g,
        v_raise_g,
        out_lower_g,
        out_raise_g,
        up_lower_g,
        up_raise_g,
        down_lower_g,
        down_raise_g,
    )


def solution(mesh):
    split = P(None, None, "tensor")
    rows = P("dp", "tensor", None)
    columns = P(None, "tensor")
    return jax.shard_map(
        functools.partial(on_device, mesh.shape["dp"]),
        mesh=mesh,
        in_specs=(rows, P("dp", None), P("dp"), rows)
        + (columns,) * 6
        + (P(), split) * 3
        + (split, P(), P(), split, split, P()),
        out_specs=(rows, rows)
        + (P(), split) * 3
        + (split, P(), P(), split, split, P()),
        check_vma=False,
    )
```

```python
import functools
import math

import jax
import jax.numpy as jnp
from jax import lax
from jax.experimental import pallas as pl
from jax.experimental.pallas import tpu as pltpu
from jax.sharding import PartitionSpec as P

HD = 80
LANES = 128
EPS = 1e-06
NEG = -1e30
F32 = jnp.float32
BF16 = jnp.bfloat16
VMEM_BYTES = 60 * 2**20
SCORE_SCALE = HD ** (-0.5)
LOG2E = math.log2(math.e)
SLOT = 384
UNIT = 16
MESH = pl.DeviceIdType.MESH

NT = (((1,), (1,)), ((), ()))
TN = (((0,), (0,)), ((), ()))


def nn(left, right):
    return jnp.dot(left, right, preferred_element_type=F32)


def nt(left, right):
    return lax.dot_general(left, right, NT, preferred_element_type=F32)


def tn(left, right):
    return lax.dot_general(left, right, TN, preferred_element_type=F32)


def params(**more):
    return pltpu.CompilerParams(vmem_limit_bytes=VMEM_BYTES, **more)


def talking(number):
    return params(collective_id=number, has_side_effects=True)


def whole(shape):
    return pl.BlockSpec(shape, lambda *_: (0,) * len(shape))


ANY = pl.BlockSpec(memory_space=pl.ANY)
VMEM = pl.BlockSpec(memory_space=pltpu.VMEM)
DMA = pltpu.SemaphoreType.DMA


def across(bit):
    return {"tensor": lax.axis_index("tensor") ^ bit}


def along(step, count):
    return {"dp": lax.rem(lax.axis_index("dp") + step, count)}


def hello(peers):
    for peer in peers:
        pl.semaphore_signal(
            pltpu.get_barrier_semaphore(), inc=1, device_id=peer, device_id_type=MESH
        )


def met(peers):
    pl.semaphore_wait(pltpu.get_barrier_semaphore(), len(peers))


def send(src, dst, send_sem, recv_sem, peer):
    return pltpu.make_async_remote_copy(
        src_ref=src, dst_ref=dst, send_sem=send_sem, recv_sem=recv_sem,
        device_id=peer, device_id_type=MESH,
    )


class Spread:
    def __init__(self, count, source, slot, sems):
        me = lax.axis_index("dp")
        sent, got, x_sent, x_got = sems
        self.ring = [{"dp": lax.rem(me + 2 * n, count)} for n in range(1, count // 2)]
        self.partner = {"dp": me + 1 - 2 * lax.rem(me, 2)}
        self.direct = [
            send(source, slot(me), sent.at[n], got.at[n], peer) for n, peer in enumerate(self.ring)
        ]
        self.own = send(source, slot(me), x_sent.at[0], x_got.at[0], self.partner)
        self.onward = []
        for n in range(1, count // 2):
            block = slot(lax.rem(me + count - 2 * n, count))
            self.onward.append(send(block, block, x_sent.at[n], x_got.at[n], self.partner))

    @staticmethod
    def sems(count):
        half = count // 2
        return [DMA((half - 1,)), DMA((half - 1,)), DMA((half,)), DMA((half,))]

    @property
    def peers(self):
        return [self.partner, *self.ring]

    def start(self):
        for copy in self.direct:
            copy.start()
        self.own.start()

    def pass_on(self, n):
        self.direct[n].wait_recv()
        self.onward[n].start()

    def pass_all(self):
        for n in range(len(self.direct)):
            self.pass_on(n)

    def finish(self):
        self.own.wait()
        for copy in self.onward:
            copy.wait()
        for copy in self.direct:
            copy.wait_send()


def place(bit, rows):
    return pl.multiple_of((lax.axis_index("tensor") ^ bit) * rows, rows)


def start_kernel(
    units, choice, x_ref, ql, kl, vl, orr, ul, dr, qr, kr, vr, ol, ur, dl, wo, wu, wd,
    own_ref, sel_ref, raise_ref, fetched_ref, mine, sems, sent, got,
):
    hello([across(2)])
    per_weight = wo.shape[0] // UNIT
    first = lax.axis_index("dp") * units

    def piece(u):
        return mine.at[pl.ds(u * UNIT, UNIT)]

    for u in range(units):
        number = lax.rem(first + u, 3 * per_weight)
        for n, w in enumerate((wo, wu, wd)):

            @pl.when(number // per_weight == n)
            def _(u=u, n=n, w=w, number=number):
                at = pl.multiple_of((number - n * per_weight) * UNIT, UNIT)
                pltpu.make_async_copy(w.at[pl.ds(at, UNIT)], piece(u), sems.at[u]).start()

    met([across(2)])
    for u in range(units):
        pltpu.make_async_copy(wo.at[pl.ds(0, UNIT)], piece(u), sems.at[u]).wait()
    far = send(mine, fetched_ref, sent, got, across(2))
    far.start()

    rows = x_ref.shape[0]
    rank, width = ol.shape[1:]
    which = choice[0]
    x = x_ref[...].astype(F32)
    factor = lax.rsqrt(jnp.mean(x * x, axis=-1, keepdims=True) + EPS)
    own_ref[:rows] = (x * factor).astype(BF16)
    own_ref[rows:] = jnp.zeros_like(own_ref[rows:])
    for slot, ref in enumerate((ol, ur, dl)):
        own_ref[rows:, slot * SLOT : slot * SLOT + width] = ref[which]
    for n, ref in enumerate((ql, kl, vl, orr, ul, dr)):
        sel_ref[n * rank : (n + 1) * rank] = ref[which]
    mark = jnp.full((rank, x.shape[1]), which, jnp.int32).astype(F32)
    sel_ref[6 * rank :] = mark.astype(BF16)
    for n, ref in enumerate((qr, kr, vr)):
        raise_ref[n * rank : (n + 1) * rank] = ref[which]
    far.wait()


def start_call(dp_count, choice, x, wides, narrows, weights):
    rows, depth = x.shape
    rank, width = narrows[0].shape[1:]
    units = -(-3 * width // (UNIT * dp_count))
    fetched = jax.ShapeDtypeStruct((units * UNIT, depth), BF16)
    return pl.pallas_call(
        functools.partial(start_kernel, units),
        in_specs=[pl.BlockSpec(memory_space=pltpu.SMEM), VMEM] + [VMEM] * 12 + [ANY] * 3,
        out_specs=[VMEM, VMEM, VMEM, ANY],
        out_shape=[
            jax.ShapeDtypeStruct((rows + rank, depth), BF16),
            jax.ShapeDtypeStruct((7 * rank, depth), BF16),
            jax.ShapeDtypeStruct((3 * rank, width), BF16),
            fetched,
        ],
        scratch_shapes=[
            pltpu.VMEM(fetched.shape, BF16), DMA((units,)), DMA, DMA,
        ],
        compiler_params=talking(0),
        name="start",
    )(choice, x, *wides, *narrows, *weights)


def project_kernel(
    heads, dp_count, own, wq, wk, wv, sel, rsel, fetched,
    qt_out, kt_out, vt_out, k_out, v_out, low_out, stack_out, near_out, far_out, cross_out, w_far,
    near, far, cross, stack, qt, kt, vt, k, v, low, sent, got, local, *spread_sems,
):
    width = heads * HD
    rank = rsel.shape[0] // 3
    rows = own.shape[0] - rank
    half = rows // 2
    cuts = ((0, half), (half, rows + rank - half))

    def part(ref, c):
        return ref.at[pl.ds(*cuts[c])]

    share = fetched.shape[0]

    def slot(n):
        return w_far.at[pl.ds(pl.multiple_of(n * share, UNIT), share)]

    weights = Spread(dp_count, fetched, slot, spread_sems)
    peers = [across(1), across(2)] + weights.peers
    hello(peers)
    to_far = [send(part(own, c), part(far, c), sent.at[c], got.at[c], across(2)) for c in (0, 1)]
    to_near = send(own, near, sent.at[2], got.at[2], across(1))
    on = [send(part(far, c), part(cross, c), sent.at[3 + c], got.at[3 + c], across(1)) for c in (0, 1)]
    at = 0
    for ref in (wq, wk, wv):
        stack[at : at + width] = ref[...]
        at += width
    stack[at:] = sel[: 3 * rank]
    met(peers)
    for copy in to_far:
        copy.start()
    to_near.start()
    weights.start()
    pending = [
        pltpu.make_async_copy(stack, stack_out, local.at[0]),
        pltpu.make_async_copy(fetched, slot(lax.axis_index("dp")), local.at[1]),
    ]
    for copy in pending:
        copy.start()

    def keep(src, dst):
        copy = pltpu.make_async_copy(src, dst, local.at[len(pending)])
        copy.start()
        pending.append(copy)

    def project(ref, bit, c):
        block = ref[c * half : (c + 1) * half]
        out = nt(stack[...], block)
        down = out[3 * width :].astype(BF16)
        start = pl.multiple_of(place(bit, rows) + c * half, half)
        here = pl.ds(start, half)
        low[:, here] = down
        for n, (col, row) in enumerate(((qt, None), (kt, k), (vt, v))):
            low_n = slice(n * rank, (n + 1) * rank)
            value = out[n * width : (n + 1) * width] + tn(rsel[low_n], down[low_n])
            if n == 0:
                value = value * (SCORE_SCALE * LOG2E)
            value = value.astype(BF16)
            col[:, here] = value
            if row is not None:
                for h in range(heads):
                    row[here, h * LANES : h * LANES + HD] = value[h * HD : (h + 1) * HD].T
        for src, dst in ((qt, qt_out), (kt, kt_out), (vt, vt_out), (low, low_out)):
            keep(src.at[:, here], dst.at[:, here])
        for src, dst in ((k, k_out), (v, v_out)):
            keep(src.at[here], dst.at[here])

    project(own, 0, 0)
    project(own, 0, 1)
    to_near.wait_recv()
    keep(near, near_out)
    project(near, 1, 0)
    project(near, 1, 1)
    for c in (0, 1):
        to_far[c].wait_recv()
        on[c].start()
        keep(part(far, c), part(far_out, c))
        project(far, 2, c)
        if c == 0:
            weights.pass_all()
        on[c].wait_recv()
        keep(part(cross, c), part(cross_out, c))
        project(cross, 3, c)
    weights.finish()
    for copy in (*to_far, to_near, *on):
        copy.wait_send()
    for copy in pending:
        copy.wait()


def project_call(dp_count, own, weights, sel, rsel, fetched, length):
    depth = own.shape[1]
    rank, width = rsel.shape[0] // 3, rsel.shape[1]
    heads = width // HD
    total = 3 * (width + rank)
    shapes = [
        (width, length), (width, length), (width, length),
        (length, heads * LANES), (length, heads * LANES), (3 * rank, length), (total, depth),
    ] + [own.shape] * 3 + [(dp_count * fetched.shape[0], depth)]
    kinds = [jax.ShapeDtypeStruct(s, BF16) for s in shapes]
    return pl.pallas_call(
        functools.partial(project_kernel, heads, dp_count),
        in_specs=[VMEM] * 6 + [ANY],
        out_specs=[ANY] * 11,
        out_shape=kinds,
        scratch_shapes=[pltpu.VMEM(own.shape, BF16)] * 3
        + [pltpu.VMEM((total, depth), BF16)]
        + [pltpu.VMEM(s, BF16) for s in shapes[:6]]
        + [DMA((5,)), DMA((5,)), DMA((2 + 8 * 6 + 5,))]
        + Spread.sems(dp_count),
        compiler_params=talking(1),
        name="project",
    )(own, *weights, sel, rsel, fetched)


def allowed_mask(seg_row, seg_col, last, start, size):
    key = lax.broadcasted_iota(jnp.int32, (last, size), 0)
    query = lax.broadcasted_iota(jnp.int32, (last, size), 1) + start
    return (seg_col[:last, :] == seg_row[:, start : start + size]) & (key <= query)


def attend_kernel(
    step, heads, seg_row, seg_col, qt_ref, k_ref, vt_ref, wo, wu, wd, w_far, ot_ref, lse_ref, att_ref,
    w_near, w_cross, wide, sent, got, local, w_sent, w_got,
):
    h = pl.program_id(0)
    length = qt_ref.shape[1]
    rows = att_ref.shape[1]
    width = heads * HD

    peers = [across(1), across(2), across(3)]
    swaps = [
        send(w, w_near.at[pl.ds(n * width, width)], w_sent.at[n], w_got.at[n], across(1))
        for n, w in enumerate((wo, wu, wd))
    ]
    swaps.append(send(w_far, w_cross, w_sent.at[3], w_got.at[3], across(1)))

    @pl.when(h == 0)
    def _():
        hello(peers)

    for i in range(length // step):
        start, last = i * step, (i + 1) * step
        s = nn(k_ref[:last, :HD], qt_ref[:, start:last])
        s = jnp.where(allowed_mask(seg_row, seg_col, last, start, step), s, NEG)
        top = jnp.max(s, axis=0, keepdims=True)
        p = jnp.exp2(s - top)
        total = jnp.sum(p, axis=0, keepdims=True)
        out = (nn(vt_ref[:, :last], p.astype(BF16)) / total).astype(BF16)
        ot_ref[:, start:last] = out
        wide[pl.ds(pl.multiple_of(h * HD, UNIT), HD), start:last] = out
        lse_ref[0, :, start:last] = top + jnp.log2(total)

    def piece(bit, head):
        src = wide.at[pl.ds(pl.multiple_of(head * HD, UNIT), HD), pl.ds(place(bit, rows), rows)]
        dst = att_ref.at[pl.ds(pl.multiple_of(bit * width + head * HD, UNIT), HD)]
        if bit == 0:
            return pltpu.make_async_copy(src, dst, local.at[head])
        return send(src, dst, sent.at[bit - 1, head], got.at[bit - 1, head], across(bit))

    @pl.when(h == 0)
    def _():
        met(peers)

    for bit in (2, 3, 1, 0):
        piece(bit, h).start()

    @pl.when(h == 0)
    def _():
        for copy in swaps:
            copy.start()

    @pl.when(h == heads - 1)
    def _():
        for copy in swaps:
            copy.wait()
        for head in range(heads):
            for bit in range(4):
                piece(bit, head).wait()


def attend_call(seg_row, seg_col, qt, k, vt, weights, w_far, rows):
    width, length = qt.shape
    heads = width // HD
    col = pl.BlockSpec((HD, length), lambda h: (h, 0))
    return pl.pallas_call(
        functools.partial(attend_kernel, 512, heads),
        grid=(heads,),
        in_specs=[
            whole((1, length)), whole((length, 1)), col,
            pl.BlockSpec((length, LANES), lambda h: (0, h)), col, ANY, ANY, ANY, ANY,
        ],
        out_specs=[col, pl.BlockSpec((1, 1, length), lambda h: (h, 0, 0)), ANY, ANY, ANY],
        scratch_shapes=[
            pltpu.VMEM((width, length), BF16), DMA((3, heads)), DMA((3, heads)), DMA((heads,)),
            DMA((4,)), DMA((4,)),
        ],
        out_shape=[
            jax.ShapeDtypeStruct((width, length), BF16),
            jax.ShapeDtypeStruct((heads, 1, length), F32),
            jax.ShapeDtypeStruct((4 * width, rows), BF16),
            jax.ShapeDtypeStruct((3 * width, w_far.shape[1]), BF16),
            jax.ShapeDtypeStruct(w_far.shape, BF16),
        ],
        compiler_params=talking(2),
        name="attend",
    )(seg_row, seg_col, qt, k, vt, *weights, w_far)


def attend_back_kernel(
    step, dp_count, seg_row, seg_col, qt_ref, kt_ref, k_ref, v_ref, ot_ref, lse_ref, grad_ref, pack_ref,
    dq_ref, dk_ref, dv_ref, all_ref, other_ref, dk_sum, dv_sum, local, near_sems, *spread_sems,
):
    h = pl.program_id(0)
    last_step = pl.num_programs(0) - 1
    length = qt_ref.shape[1]
    shared = other_ref.shape[1]
    spread = Spread(dp_count, pack_ref, lambda n: all_ref.at[n], spread_sems)
    keep = pltpu.make_async_copy(pack_ref, all_ref.at[lax.axis_index("dp")], local)
    pair = send(
        all_ref.at[:, pl.ds(0, shared)], other_ref, near_sems.at[0], near_sems.at[1], across(1)
    )
    peers = [across(1)] + spread.peers

    @pl.when(h == 0)
    def _():
        hello(peers)

    row_dot = jnp.sum(grad_ref[...].astype(F32) * ot_ref[...].astype(F32), axis=0, keepdims=True)
    for i in range(length // step):
        start, last = i * step, (i + 1) * step
        grad, query = grad_ref[:, start:last], qt_ref[:, start:last]
        s = nn(k_ref[:last, :HD], query)
        dp = nn(v_ref[:last, :HD], grad)
        s = jnp.where(allowed_mask(seg_row, seg_col, last, start, step), s, NEG)
        p = jnp.exp2(s - lse_ref[0, :, start:last])
        ds = (p * (dp - row_dot[:, start:last])).astype(BF16)
        dv = nt(grad, p.astype(BF16))
        dk = nt(query, ds)
        dq = nn(kt_ref[:, :last], ds)
        if start:
            dv_sum[:, :start] += dv[:, :start]
            dk_sum[:, :start] += dk[:, :start]
        dv_sum[:, start:last] = dv[:, start:]
        dk_sum[:, start:last] = dk[:, start:]
        dq_ref[:, start:last] = (dq * SCORE_SCALE).astype(BF16)
    dk_ref[...] = (dk_sum[...] * (1.0 / LOG2E)).astype(BF16)
    dv_ref[...] = dv_sum[...].astype(BF16)

    @pl.when(h == 0)
    def _():
        met(peers)
        keep.start()
        spread.start()

    @pl.when(h == 1)
    def _():
        spread.pass_all()

    @pl.when(h == last_step - 1)
    def _():
        keep.wait()
        spread.finish()
        pair.start()

    @pl.when(h == last_step)
    def _():
        pair.wait()


def attend_back_call(dp_count, seg_row, seg_col, qt, kt, k, v, ot, lse, grad, pack):
    width, length = qt.shape
    heads = width // HD
    shared = pack.shape[0] * 3 // 5
    row = pl.BlockSpec((length, LANES), lambda h: (0, h))
    col = pl.BlockSpec((HD, length), lambda h: (h, 0))
    col_t = jax.ShapeDtypeStruct((width, length), BF16)
    return pl.pallas_call(
        functools.partial(attend_back_kernel, 256, dp_count),
        grid=(heads,),
        in_specs=[
            whole((1, length)), whole((length, 1)), col, col, row, row, col,
            pl.BlockSpec((1, 1, length), lambda h: (h, 0, 0)), col, ANY,
        ],
        out_specs=[col, col, col, ANY, ANY],
        scratch_shapes=[
            pltpu.VMEM((HD, length), F32),
            pltpu.VMEM((HD, length), F32),
            DMA, DMA((2,)), *Spread.sems(dp_count),
        ],
        out_shape=[
            col_t, col_t, col_t,
            jax.ShapeDtypeStruct((dp_count, *pack.shape), BF16),
            jax.ShapeDtypeStruct((dp_count, shared, pack.shape[1]), BF16),
        ],
        compiler_params=talking(4),
        name="attend_back",
    )(seg_row, seg_col, qt, kt, k, v, ot, lse, grad, pack)


def own_half(half):
    parity = lax.rem(lax.axis_index("tensor"), 2)
    return pl.multiple_of(parity * half, half), pl.multiple_of((1 - parity) * half, half)


def middle_kernel(
    x_ref, g_ref, att_ref, s0, s1, s2, s3, sel, wo_own, wu_own, wd_own, w_near, w_far, w_cross,
    act_ref, gm_ref, grad_out, pack_ref,
    wo, wu, wd, ol, ur, dl, gt, e_sum, whole_b, near_b, half_b, far_b, mine_b, theirs_b,
    w_local, g_sent, g_got, g_local, e_sent, e_got,
):
    width = wo_own.shape[0]
    rank = s0.shape[0]
    rows = x_ref.shape[0]
    half = rows // 2
    me = lax.axis_index("tensor")

    peers = [across(1), across(2), across(3)]
    hello(peers)
    weights = []
    for n, (own, dst) in enumerate(((wo_own, wo), (wu_own, wu), (wd_own, wd))):
        here = pl.ds(n * width, width)
        group = [
            pltpu.make_async_copy(src, dst.at[pl.ds(x * width, width)], w_local.at[n, x])
            for x, src in enumerate((own, w_near.at[here], w_far.at[here], w_cross.at[here]))
        ]
        for copy in group:
            copy.start()
        weights.append(group)

    def arrived(n):
        for copy in weights[n]:
            copy.wait()

    smalls = (s0, s1, s2, s3)
    for x, src in enumerate(smalls):
        for slot, dst in enumerate((ol, ur, dl)):
            dst[:, x * width : (x + 1) * width] = src[:, slot * SLOT : slot * SLOT + width].astype(F32)
    out_lower, up_raise, down_lower = (r[...].astype(BF16) for r in (ol, ur, dl))
    out_raise, up_lower, down_raise = (
        sel[n * rank : (n + 1) * rank] for n in (3, 4, 5)
    )

    back = {}
    for r in range(2):
        here = slice(r * half, (r + 1) * half)
        grad = g_ref[here]
        att = att_ref[:, here].astype(F32).T.astype(BF16)
        low_out = nt(att, out_lower).astype(BF16)
        grad_low_down = nt(grad, down_raise).astype(BF16)
        if r == 0:
            arrived(0)
        middle = x_ref[here].astype(F32) + (nn(att, wo[...]) + nn(low_out, out_raise))
        factor = lax.rsqrt(jnp.mean(middle * middle, axis=-1, keepdims=True) + EPS)
        unit = middle * factor
        normed = unit.astype(BF16)
        low_up = nt(normed, up_lower).astype(BF16)
        if r == 0:
            arrived(1)
        preact = nt(normed, wu[...]) + nn(low_up, up_raise)
        sigma = 1.0 / (1.0 + jnp.exp(-preact))
        active = (preact * sigma).astype(BF16)
        if r == 0:
            arrived(2)
        low_down = nt(active, down_lower).astype(BF16)
        grad_act = nt(grad, wd[...]) + nn(grad_low_down, down_lower)
        grad_pre = (grad_act * (sigma * (1.0 + preact * (1.0 - sigma)))).astype(BF16)
        grad_low_up = nt(grad_pre, up_raise).astype(BF16)
        grad_mid = nn(grad_pre, wu[...]) + nn(grad_low_up, up_lower)
        dot = jnp.mean(grad_mid * unit, axis=-1, keepdims=True)
        grad_middle = grad.astype(F32) + factor * (grad_mid - unit * dot)
        gm_ref[here] = grad_middle
        grad_attn = grad_middle.astype(BF16)
        grad_low_out = nt(out_raise, grad_attn).astype(BF16)
        if r == 0:
            met(peers)
        for x in (2, 3, 1, 0):
            value = nt(wo[x * width : (x + 1) * width], grad_attn)
            value = value + tn(smalls[x][:, :width], grad_low_out)
            gt[x, :, here] = value.astype(BF16)
            src = gt.at[x, :, pl.ds(r * half, half)]
            dst = grad_out.at[:, pl.ds(pl.multiple_of(me * rows + r * half, half), half)]
            if x:
                copy = send(src, dst, g_sent.at[x - 1, r], g_got.at[x - 1, r], across(x))
            else:
                copy = pltpu.make_async_copy(src, dst, g_local.at[r])
            copy.start()
            back[x, r] = copy
        act_ref[here] = (middle + (nn(active, wd[...]) + nn(low_down, down_raise))).astype(BF16)
        parts = [
            tn(low_out, grad_attn), tn(grad_low_up, normed), tn(low_down, grad),
            nn(grad_low_out, att), tn(low_up, grad_pre), tn(grad_low_down, active),
        ]
        for n, part in enumerate(parts):
            block = slice(n * rank, (n + 1) * rank)
            e_sum[block] = e_sum[block] + part if r else part

    columns = half_b.shape[1]
    keep, give = own_half(columns)
    whole_b[...] = e_sum[: 3 * rank].astype(BF16)
    one = send(whole_b.at[:, pl.ds(give, columns)], near_b, e_sent.at[0], e_got.at[0], across(1))
    one.start()
    quarter = []
    for x in range(4):
        mine_b[x] = jnp.zeros(mine_b.shape[1:], BF16)
        for slot in range(3):
            part = e_sum[(3 + slot) * rank : (4 + slot) * rank, x * width : (x + 1) * width]
            mine_b[x, :, slot * SLOT : slot * SLOT + width] = part.astype(BF16)
        if x:
            copy = send(mine_b.at[x], theirs_b.at[x - 1], e_sent.at[1 + x], e_got.at[1 + x], across(x))
            copy.start()
            quarter.append(copy)
    one.wait()
    half_b[...] = (e_sum[: 3 * rank, pl.ds(keep, columns)] + near_b[...].astype(F32)).astype(BF16)
    two = send(half_b, far_b, e_sent.at[1], e_got.at[1], across(2))
    two.start()
    for copy in quarter:
        copy.wait()
    sums = (mine_b[0].astype(F32) + theirs_b[0].astype(F32)) + (
        theirs_b[1].astype(F32) + theirs_b[2].astype(F32)
    )
    mark = sel[6 * rank :, : SLOT - width].astype(F32)
    sums = jnp.concatenate([sums[:, : sums.shape[1] - mark.shape[1]], mark], axis=1)
    pack_ref[3 * rank : 4 * rank] = sums[:, :columns].astype(BF16)
    pack_ref[4 * rank :] = sums[:, columns:].astype(BF16)
    two.wait()
    pack_ref[: 3 * rank] = (half_b[...].astype(F32) + far_b[...].astype(F32)).astype(BF16)
    for copy in back.values():
        copy.wait()


def middle_call(x, g, att, pieces, sel, weights, fetched, length):
    rows, depth = x.shape
    width = weights[0].shape[0]
    rank = sel.shape[0] // 7
    small = pl.BlockSpec((rank, depth), lambda c: (rows // rank, 0))
    square = pltpu.VMEM((4 * width, depth), BF16)
    thin = pltpu.VMEM((rank, depth), F32)
    pack = (5 * rank, depth // 2)
    halves = pltpu.VMEM((3 * rank, depth // 2), BF16)
    return pl.pallas_call(
        middle_kernel,
        grid=(1,),
        in_specs=[whole((rows, depth))] * 2 + [whole((4 * width, rows))] + [small] * 4
        + [whole(sel.shape)] + [ANY] * 6,
        out_specs=[whole((rows, depth))] * 2 + [ANY, whole(pack)],
        scratch_shapes=[
            square, square, square, thin, thin, thin,
            pltpu.VMEM((4, width, rows), BF16),
            pltpu.VMEM((6 * rank, depth), F32),
            pltpu.VMEM((3 * rank, depth), BF16),
            halves, halves, halves,
            pltpu.VMEM((4, rank, depth), BF16),
            pltpu.VMEM((3, rank, depth), BF16),
            DMA((3, 4)), DMA((3, 2)), DMA((3, 2)), DMA((2,)), DMA((5,)), DMA((5,)),
        ],
        out_shape=[
            jax.ShapeDtypeStruct((rows, depth), BF16),
            jax.ShapeDtypeStruct((rows, depth), F32),
            jax.ShapeDtypeStruct((width, length), BF16),
            jax.ShapeDtypeStruct(pack, BF16),
        ],
        compiler_params=talking(3),
        name="feed_forward",
    )(x, g, att, *pieces, sel, *weights, *fetched)


def tail_kernel(
    dp_count, dq, dk, dv, low, p0, p1, p2, p3, rsel, stack_hbm, x_hbm, gm_hbm,
    out_ref, all_ref, other_ref,
    grads, normed, stack, x_buf, gm_buf, ours, to_near, from_near, to_far, from_far,
    lower_sum, raise_sum, whole_b, near_b, half_b, far_b, pack_b,
    loads, g_sent, g_got, e_sent, e_got, last, *spread_sems,
):
    rank, width = rsel.shape[0] // 3, rsel.shape[1]
    rows = out_ref.shape[0]
    chunks = from_far.shape[0]
    step = rows // chunks
    shared = 3 * rank
    load = {}
    order = (3, 2, 1, 0)
    for x in order:
        here = pl.ds(place(x, rows), rows)
        for n, src in enumerate((dq, dk, dv)):
            load[x, n] = pltpu.make_async_copy(
                src.at[:, here], grads.at[x, pl.ds(n * width, width)], loads.at[x, n]
            )
        load[x, 3] = pltpu.make_async_copy(
            (p0, p1, p2, p3)[x].at[pl.ds(0, rows)], normed.at[x], loads.at[x, 3]
        )
    load["stack"] = pltpu.make_async_copy(stack_hbm, stack, last.at[0])
    load["x"] = pltpu.make_async_copy(x_hbm, x_buf, last.at[1])
    load["gm"] = pltpu.make_async_copy(gm_hbm, gm_buf, last.at[2])
    for key in [(3, 0), (3, 1), (3, 2), "stack", (2, 0), (2, 1), (2, 2), (3, 3), (2, 3),
                (1, 0), (1, 1), (1, 2), (1, 3), (0, 0), (0, 1), (0, 2), (0, 3), "x", "gm"]:
        load[key].start()
    spread = Spread(dp_count, pack_b, lambda n: all_ref.at[n], spread_sems)
    peers = [across(1), across(2)] + spread.peers
    hello(peers)

    def adapters(x):
        load[x, 3].wait()
        here = pl.ds(place(x, rows), rows)
        for n in range(3):
            value = grads[x, n * width : (n + 1) * width]
            part = nt(low[n * rank : (n + 1) * rank, here], value)
            at = slice(n * SLOT, n * SLOT + width)
            raise_sum[:, at] = part if x == order[0] else raise_sum[:, at] + part
        part = nn(grads[x, 3 * width :], normed[x])
        lower_sum[...] = part if x == order[0] else lower_sum[...] + part

    def ready(x):
        for n in range(3):
            load[x, n].wait()
            value = grads[x, n * width : (n + 1) * width]
            grads[x, 3 * width + n * rank : 3 * width + (n + 1) * rank] = nn(
                rsel[n * rank : (n + 1) * rank], value
            ).astype(BF16)

    half = rows // 2

    def through(x, r):
        return tn(grads[x, :, r * half : (r + 1) * half], stack[...])

    pair = [
        [
            send(
                to_near.at[n, pl.ds(r * half, half)], from_near.at[n, pl.ds(r * half, half)],
                g_sent.at[2 * n + r], g_got.at[2 * n + r], across(1),
            )
            for r in range(2)
        ]
        for n in range(2)
    ]
    far = [
        send(to_far.at[c], from_far.at[c], g_sent.at[4 + c], g_got.at[4 + c], across(2))
        for c in range(chunks)
    ]
    raise_sum[...] = jnp.zeros_like(raise_sum)
    ready(3)
    load["stack"].wait()
    for r in range(2):
        to_near[1, r * half : (r + 1) * half] = through(3, r).astype(BF16)
        if r == 0:
            met(peers)
        pair[1][r].start()
    ready(2)

    def to_go(r):
        total = through(2, r)
        pair[1][r].wait()
        for c in range(r * chunks // 2, (r + 1) * chunks // 2):
            here = slice(c * step - r * half, (c + 1) * step - r * half)
            there = slice(c * step, (c + 1) * step)
            to_far[c] = (total[here] + from_near[1, there].astype(F32)).astype(BF16)
            far[c].start()

    to_go(0)
    adapters(3)
    adapters(2)
    ready(1)
    adapters(1)
    ready(0)
    adapters(0)

    columns = half_b.shape[1]
    keep, give = own_half(columns)
    whole_b[...] = lower_sum[...].astype(BF16)
    one = send(whole_b.at[:, pl.ds(give, columns)], near_b, e_sent.at[0], e_got.at[0], across(1))
    one.start()
    pack_b[shared : shared + rank] = raise_sum[:, :columns].astype(BF16)
    pack_b[shared + rank :] = raise_sum[:, columns:].astype(BF16)
    one.wait()
    half_b[...] = (lower_sum[:, pl.ds(keep, columns)] + near_b[...].astype(F32)).astype(BF16)
    two = send(half_b, far_b, e_sent.at[1], e_got.at[1], across(2))
    two.start()
    to_go(1)
    for r in range(2):
        to_near[0, r * half : (r + 1) * half] = through(1, r).astype(BF16)
        pair[0][r].start()
    two.wait()
    pack_b[:shared] = (half_b[...].astype(F32) + far_b[...].astype(F32)).astype(BF16)
    stay = pltpu.make_async_copy(pack_b, all_ref.at[lax.axis_index("dp")], last.at[3])
    stay.start()
    spread.start()
    for r in range(2):
        ours[r * half : (r + 1) * half] = through(0, r)
    for r in range(2):
        here = slice(r * half, (r + 1) * half)
        pair[0][r].wait()
        ours[here] = ours[here] + from_near[0, here].astype(F32)
    spread.pass_all()
    load["x"].wait()
    load["gm"].wait()
    stay.wait()
    spread.finish()
    swap = send(
        all_ref.at[:, pl.ds(0, shared)], other_ref, e_sent.at[2], e_got.at[2], across(1)
    )
    swap.start()
    for c in range(chunks):
        here = slice(c * step, (c + 1) * step)
        far[c].wait()
        x = x_buf[here].astype(F32)
        factor = lax.rsqrt(jnp.mean(x * x, axis=-1, keepdims=True) + EPS)
        unit = x * factor
        grad = ours[here] + from_far[c].astype(F32)
        dot = jnp.mean(grad * unit, axis=-1, keepdims=True)
        out_ref[here] = (gm_buf[here] + factor * (grad - unit * dot)).astype(BF16)
    swap.wait()


def tail_call(dp_count, grads, low, pieces, rsel, stack, x, gm):
    rows, depth = x.shape
    rank, width = rsel.shape[0] // 3, rsel.shape[1]
    total = stack.shape[0]
    chunks = 4
    pack = (5 * rank, depth // 2)
    halves = pltpu.VMEM((3 * rank, depth // 2), BF16)
    lines = pltpu.VMEM((chunks, rows // chunks, depth), BF16)
    return pl.pallas_call(
        functools.partial(tail_kernel, dp_count),
        in_specs=[ANY] * 3 + [VMEM] + [ANY] * 4 + [VMEM] + [ANY] * 3,
        out_specs=[VMEM, ANY, ANY],
        scratch_shapes=[
            pltpu.VMEM((4, total, rows), BF16),
            pltpu.VMEM((4, rows, depth), BF16),
            pltpu.VMEM((total, depth), BF16),
            pltpu.VMEM((rows, depth), BF16),
            pltpu.VMEM((rows, depth), F32),
            pltpu.VMEM((rows, depth), F32),
            pltpu.VMEM((2, rows, depth), BF16),
            pltpu.VMEM((2, rows, depth), BF16),
            lines, lines,
            pltpu.VMEM((3 * rank, depth), F32),
            pltpu.VMEM((rank, depth), F32),
            pltpu.VMEM((3 * rank, depth), BF16),
            halves, halves, halves,
            pltpu.VMEM(pack, BF16),
            DMA((4, 4)), DMA((4 + chunks,)), DMA((4 + chunks,)), DMA((3,)), DMA((3,)),
            DMA((4,)), *Spread.sems(dp_count),
        ],
        out_shape=[
            jax.ShapeDtypeStruct((rows, depth), BF16),
            jax.ShapeDtypeStruct((dp_count, *pack), BF16),
            jax.ShapeDtypeStruct((dp_count, 3 * rank, depth // 2), BF16),
        ],
        compiler_params=talking(5),
        name="tail",
    )(*grads, low, *pieces, rsel, stack, x, gm)


def sets_kernel(scal, first, first_other, second, second_other, *outs):
    rank = outs[0].shape[1]
    columns = first.shape[2]
    count = first.shape[0]
    here = pl.ds(pl.multiple_of(scal[count] * columns, columns), columns)
    there = pl.ds(pl.multiple_of((1 - scal[count]) * columns, columns), columns)
    for ref in outs:
        ref[...] = jnp.zeros_like(ref)

    @pl.loop(0, count)
    def _(n):
        which = scal[n]
        for group, pack, other in ((outs[:6], first, first_other), (outs[6:], second, second_other)):
            for k in range(3):
                part = slice(k * rank, (k + 1) * rank)
                group[k][which, :, here] += pack[n, part].astype(F32)
                group[k][which, :, there] += other[n, part].astype(F32)
            thin = jnp.concatenate(
                [pack[n, 3 * rank : 4 * rank], pack[n, 4 * rank :]], axis=1
            ).astype(F32)
            for k in range(3):
                width = group[3 + k].shape[2]
                group[3 + k][which] += thin[:, k * SLOT : k * SLOT + width]


def sets_call(scal, packs, sets, width):
    _, five, columns = packs[0].shape
    rank, depth = five // 5, 2 * columns
    full = jax.ShapeDtypeStruct((sets, rank, depth), F32)
    thin = jax.ShapeDtypeStruct((sets, rank, width), F32)
    shapes = [full, full, full, thin, thin, thin] * 2
    return pl.pallas_call(
        sets_kernel,
        grid_spec=pltpu.PrefetchScalarGridSpec(
            num_scalar_prefetch=1,
            grid=(1,),
            in_specs=[whole(p.shape) for p in packs],
            out_specs=[whole(t.shape) for t in shapes],
        ),
        out_shape=shapes,
        compiler_params=params(),
        name="set_sums",
    )(scal, *packs)


def on_device(
    dp_count,
    tokens,
    segment_ids,
    adapter_choice,
    cotangent,
    weight_query,
    weight_key,
    weight_value,
    weight_output,
    weight_upward,
    weight_downward,
    query_lower,
    query_raise,
    key_lower,
    key_raise,
    value_lower,
    value_raise,
    output_lower,
    output_raise,
    upward_lower,
    upward_raise,
    downward_lower,
    downward_raise,
):
    x, g = tokens[0], cotangent[0]
    rows = x.shape[0]
    length = segment_ids.shape[1]
    sets = query_lower.shape[0]
    width = query_raise.shape[2]
    seg_row = segment_ids
    seg_col = segment_ids.reshape(length, 1)
    parity = lax.rem(lax.axis_index("tensor").astype(jnp.int32), 2).reshape(1)

    feed = (weight_output.T, weight_upward.T, weight_downward.T)
    own, sel, rsel, fetched = start_call(
        dp_count,
        adapter_choice,
        x,
        (query_lower, key_lower, value_lower, output_raise, upward_lower, downward_raise),
        (query_raise, key_raise, value_raise, output_lower, upward_raise, downward_lower),
        feed,
    )
    qt, kt, vt, k, v, low, stack, near, far, cross, w_far = project_call(
        dp_count, own, (weight_query.T, weight_key.T, weight_value.T), sel, rsel, fetched, length
    )
    pieces = (own, near, far, cross)
    ot, lse, att, w_near, w_cross = attend_call(seg_row, seg_col, qt, k, vt, feed, w_far, rows)
    act, gm, grad, pack = middle_call(
        x, g, att, pieces, sel, feed, (w_near, w_far, w_cross), length
    )
    dq, dk, dv, first, first_other = attend_back_call(
        dp_count, seg_row, seg_col, qt, kt, k, v, ot, lse, grad, pack
    )
    chosen = first[:, -1, -1].astype(jnp.int32)
    input_grad, second, second_other = tail_call(
        dp_count, (dq, dk, dv), low, pieces, rsel, stack, x, gm
    )
    out = sets_call(
        jnp.concatenate([chosen, parity]), (first, first_other, second, second_other), sets, width
    )
    (out_raise_g, up_lower_g, down_raise_g, out_lower_g, up_raise_g, down_lower_g) = out[:6]
    (q_lower_g, k_lower_g, v_lower_g, q_raise_g, k_raise_g, v_raise_g) = out[6:]
    return (
        act[None],
        input_grad[None],
        q_lower_g,
        q_raise_g,
        k_lower_g,
        k_raise_g,
        v_lower_g,
        v_raise_g,
        out_lower_g,
        out_raise_g,
        up_lower_g,
        up_raise_g,
        down_lower_g,
        down_raise_g,
    )


def solution(mesh):
    split = P(None, None, "tensor")
    rows = P("dp", "tensor", None)
    columns = P(None, "tensor")
    return jax.shard_map(
        functools.partial(on_device, mesh.shape["dp"]),
        mesh=mesh,
        in_specs=(rows, P("dp", None), P("dp"), rows)
        + (columns,) * 6
        + (P(), split) * 3
        + (split, P(), P(), split, split, P()),
        out_specs=(rows, rows)
        + (P(), split) * 3
        + (split, P(), P(), split, split, P()),
        check_vma=False,
    )
```

```python
import functools
import math

import jax
import jax.numpy as jnp
from jax import lax
from jax.experimental import pallas as pl
from jax.experimental.pallas import tpu as pltpu
from jax.sharding import PartitionSpec as P

HD = 80
LANES = 128
EPS = 1e-06
NEG = -1e30
F32 = jnp.float32
BF16 = jnp.bfloat16
VMEM_BYTES = 60 * 2**20
SCORE_SCALE = HD ** (-0.5)
LOG2E = math.log2(math.e)
SLOT = 384
UNIT = 16
MESH = pl.DeviceIdType.MESH

NT = (((1,), (1,)), ((), ()))
TN = (((0,), (0,)), ((), ()))


def nn(left, right):
    return jnp.dot(left, right, preferred_element_type=F32)


def nt(left, right):
    return lax.dot_general(left, right, NT, preferred_element_type=F32)


def tn(left, right):
    return lax.dot_general(left, right, TN, preferred_element_type=F32)


def params(**more):
    return pltpu.CompilerParams(vmem_limit_bytes=VMEM_BYTES, **more)


def talking(number):
    return params(collective_id=number, has_side_effects=True)


def whole(shape):
    return pl.BlockSpec(shape, lambda *_: (0,) * len(shape))


ANY = pl.BlockSpec(memory_space=pl.ANY)
VMEM = pl.BlockSpec(memory_space=pltpu.VMEM)
DMA = pltpu.SemaphoreType.DMA


def across(bit):
    return {"tensor": lax.axis_index("tensor") ^ bit}


def along(step, count):
    return {"dp": lax.rem(lax.axis_index("dp") + step, count)}


def hello(peers):
    for peer in peers:
        pl.semaphore_signal(
            pltpu.get_barrier_semaphore(), inc=1, device_id=peer, device_id_type=MESH
        )


def met(peers):
    pl.semaphore_wait(pltpu.get_barrier_semaphore(), len(peers))


def send(src, dst, send_sem, recv_sem, peer):
    return pltpu.make_async_remote_copy(
        src_ref=src, dst_ref=dst, send_sem=send_sem, recv_sem=recv_sem,
        device_id=peer, device_id_type=MESH,
    )


class Spread:
    def __init__(self, count, source, slot, sems):
        me = lax.axis_index("dp")
        sent, got, x_sent, x_got = sems
        self.ring = [{"dp": lax.rem(me + 2 * n, count)} for n in range(1, count // 2)]
        self.partner = {"dp": me + 1 - 2 * lax.rem(me, 2)}
        self.direct = [
            send(source, slot(me), sent.at[n], got.at[n], peer) for n, peer in enumerate(self.ring)
        ]
        self.own = send(source, slot(me), x_sent.at[0], x_got.at[0], self.partner)
        self.onward = []
        for n in range(1, count // 2):
            block = slot(lax.rem(me + count - 2 * n, count))
            self.onward.append(send(block, block, x_sent.at[n], x_got.at[n], self.partner))

    @staticmethod
    def sems(count):
        half = count // 2
        return [DMA((half - 1,)), DMA((half - 1,)), DMA((half,)), DMA((half,))]

    @property
    def peers(self):
        return [self.partner, *self.ring]

    def start(self):
        for copy in self.direct:
            copy.start()
        self.own.start()

    def pass_on(self, n):
        self.direct[n].wait_recv()
        self.onward[n].start()

    def pass_all(self):
        for n in range(len(self.direct)):
            self.pass_on(n)

    def finish(self):
        self.own.wait()
        for copy in self.onward:
            copy.wait()
        for copy in self.direct:
            copy.wait_send()


def place(bit, rows):
    return pl.multiple_of((lax.axis_index("tensor") ^ bit) * rows, rows)


def front_kernel(
    heads, dp_count, choice, x_hbm, ql, kl, vl, orr, ul, dr, ol, ur, dl, qr, kr, vr, wq, wk, wv, wo, wu, wd,
    qt_out, kt_out, vt_out, k_out, v_out, low_out, stack_out, own_out, near_out, far_out, cross_out,
    sel_out, rsel_out, w_far, w_later,
    x_buf, wide, thin, mine, mine_later, fetched, own, near, far, cross, stack, sel, rsel,
    qt, kt, vt, k, v, low, loads, unit_sems, w_sent, w_got, sent, got, local, *spread_sems,
):
    width = heads * HD
    rank = rsel.shape[0] // 3
    rows = x_buf.shape[0]
    half = rows // 2
    cuts = ((0, half), (half, rows + rank - half))
    share = fetched.shape[0]
    me = lax.axis_index("dp")

    def slot(n):
        return w_far.at[pl.ds(pl.multiple_of(n * share, UNIT), share)]

    weights = Spread(dp_count, fetched, slot, spread_sems)
    peers = [across(1), across(2)] + weights.peers
    hello(peers)

    per_weight = wo.shape[0] // UNIT

    piles = [(mine, 0), (mine_later, dp_count * (mine.shape[0] // UNIT))]
    pieces = []
    for pile, first in piles:
        count = pile.shape[0] // UNIT
        for u in range(count):
            number = lax.rem(first + me * count + u, 3 * per_weight)
            pieces.append((pile.at[pl.ds(u * UNIT, UNIT)], number, unit_sems.at[len(pieces)]))
    for dst, number, sem in pieces:
        for n, w in enumerate((wo, wu, wd)):

            @pl.when(number // per_weight == n)
            def _(dst=dst, number=number, sem=sem, n=n, w=w):
                at = pl.multiple_of((number - n * per_weight) * UNIT, UNIT)
                pltpu.make_async_copy(w.at[pl.ds(at, UNIT)], dst, sem).start()

    lines = [
        pltpu.make_async_copy(
            x_hbm.at[pl.ds(c * half, half)], x_buf.at[pl.ds(c * half, half)], loads.at[c]
        )
        for c in range(2)
    ]
    for copy in lines:
        copy.start()
    thins = [
        pltpu.make_async_copy(ref, thin.at[n], loads.at[2 + n])
        for n, ref in enumerate((ol, ur, dl, qr, kr, vr))
    ]
    wides = [
        pltpu.make_async_copy(ref, wide.at[n], loads.at[8 + n])
        for n, ref in enumerate((ql, kl, vl, orr, ul, dr))
    ]
    squares = [
        pltpu.make_async_copy(ref, stack.at[pl.ds(n * width, width)], loads.at[14 + n])
        for n, ref in enumerate((wq, wk, wv))
    ]
    for copy in (*thins, *wides, *squares):
        copy.start()

    def part(ref, c):
        return ref.at[pl.ds(*cuts[c])]

    to_far = [send(part(own, c), part(far, c), sent.at[c], got.at[c], across(2)) for c in (0, 1)]
    to_near = [send(part(own, c), part(near, c), sent.at[2 + c], got.at[2 + c], across(1)) for c in (0, 1)]
    on = [send(part(far, c), part(cross, c), sent.at[4 + c], got.at[4 + c], across(1)) for c in (0, 1)]
    shares = [
        send(mine, fetched, w_sent.at[0], w_got.at[0], across(2)),
        send(mine_later, w_later, w_sent.at[1], w_got.at[1], across(2)),
    ]
    which = choice[0]
    for dst, number, sem in pieces:
        pltpu.make_async_copy(wo.at[pl.ds(0, UNIT)], dst, sem).wait()
    met(peers)
    for c in range(2):
        shares[c].start()
        here = slice(c * half, (c + 1) * half)
        lines[c].wait()
        x = x_buf[here].astype(F32)
        factor = lax.rsqrt(jnp.mean(x * x, axis=-1, keepdims=True) + EPS)
        own[here] = (x * factor).astype(BF16)
        if c == 1:
            own[rows:] = jnp.zeros((rank, own.shape[1]), BF16)
            for copy in thins:
                copy.wait()
            for n in range(3):
                own[rows:, n * SLOT : n * SLOT + width] = thin[n, which]
        to_far[c].start()
        to_near[c].start()

    pending = []

    def keep(src, dst):
        copy = pltpu.make_async_copy(src, dst, local.at[len(pending)])
        copy.start()
        pending.append(copy)

    keep(own, own_out)
    for copy in wides:
        copy.wait()
    for n in range(6):
        sel[n * rank : (n + 1) * rank] = wide[n, which]
    mark = jnp.full((rank, sel.shape[1]), which, jnp.int32).astype(F32)
    sel[6 * rank :] = mark.astype(BF16)
    keep(sel, sel_out)
    for n in range(3):
        rsel[n * rank : (n + 1) * rank] = thin[3 + n, which]
    keep(rsel, rsel_out)
    stack[3 * width :] = sel[: 3 * rank]
    for copy in squares:
        copy.wait()
    keep(stack, stack_out)

    def project(ref, bit, c):
        block = ref[c * half : (c + 1) * half]
        out = nt(stack[...], block)
        down = out[3 * width :].astype(BF16)
        start = pl.multiple_of(place(bit, rows) + c * half, half)
        here = pl.ds(start, half)
        low[:, here] = down
        for n, (col, row) in enumerate(((qt, None), (kt, k), (vt, v))):
            low_n = slice(n * rank, (n + 1) * rank)
            value = out[n * width : (n + 1) * width] + tn(rsel[low_n], down[low_n])
            if n == 0:
                value = value * (SCORE_SCALE * LOG2E)
            value = value.astype(BF16)
            col[:, here] = value
            if row is not None:
                for h in range(heads):
                    row[here, h * LANES : h * LANES + HD] = value[h * HD : (h + 1) * HD].T
        for src, dst in ((qt, qt_out), (kt, kt_out), (vt, vt_out), (low, low_out)):
            keep(src.at[:, here], dst.at[:, here])
        for src, dst in ((k, k_out), (v, v_out)):
            keep(src.at[here], dst.at[here])

    project(own, 0, 0)
    shares[0].wait_recv()
    weights.start()
    keep(fetched, slot(me))
    project(own, 0, 1)
    for c in (0, 1):
        to_near[c].wait_recv()
        keep(part(near, c), part(near_out, c))
        project(near, 1, c)
    for c in (0, 1):
        to_far[c].wait_recv()
        on[c].start()
        keep(part(far, c), part(far_out, c))
        project(far, 2, c)
        on[c].wait_recv()
        keep(part(cross, c), part(cross_out, c))
        project(cross, 3, c)
        if c == 0:
            weights.pass_all()
    shares[0].wait_send()
    shares[1].wait()
    weights.finish()
    for copy in (*to_far, *to_near, *on):
        copy.wait_send()
    for copy in pending:
        copy.wait()


def front_call(dp_count, choice, x, wides, thins, weights, feed, length):
    rows, depth = x.shape
    sets, rank, width = thins[0].shape
    heads = width // HD
    total = 3 * (width + rank)
    units = max(2, -(-3 * width // (UNIT * dp_count)))
    later = max(1, units // 4)
    share, share_later = ((units - later) * UNIT, depth), (later * UNIT, depth)
    block = (rows + rank, depth)
    shapes = [
        (width, length), (width, length), (width, length),
        (length, heads * LANES), (length, heads * LANES), (3 * rank, length), (total, depth),
    ] + [block] * 4 + [(7 * rank, depth), (3 * rank, width), (dp_count * share[0], depth), share_later]
    return pl.pallas_call(
        functools.partial(front_kernel, heads, dp_count),
        in_specs=[pl.BlockSpec(memory_space=pltpu.SMEM)] + [ANY] * 19,
        out_specs=[ANY] * 15,
        out_shape=[jax.ShapeDtypeStruct(t, BF16) for t in shapes],
        scratch_shapes=[
            pltpu.VMEM((rows, depth), BF16),
            pltpu.VMEM((6, sets, rank, depth), BF16),
            pltpu.VMEM((6, sets, rank, width), BF16),
            pltpu.VMEM(share, BF16),
            pltpu.VMEM(share_later, BF16),
            pltpu.VMEM(share, BF16),
        ]
        + [pltpu.VMEM(block, BF16)] * 4
        + [pltpu.VMEM(t, BF16) for t in (shapes[6], shapes[11], shapes[12], *shapes[:6])]
        + [DMA((17,)), DMA((units,)), DMA((2,)), DMA((2,)), DMA((6,)), DMA((6,)), DMA((5 + 8 * 6 + 6,))]
        + Spread.sems(dp_count),
        compiler_params=talking(0),
        name="front",
    )(choice, x, *wides, *thins, *weights, *feed)


def allowed_mask(seg_row, seg_col, last, start, size):
    key = lax.broadcasted_iota(jnp.int32, (last, size), 0)
    query = lax.broadcasted_iota(jnp.int32, (last, size), 1) + start
    return (seg_col[:last, :1] == seg_row[:, start : start + size]) & (key <= query)


def column_of(seg_row):
    return jnp.broadcast_to(seg_row[...], (8, seg_row.shape[1])).T


def attend_kernel(
    step, heads, dp_count, seg_row, qt_ref, k_ref, vt_ref, wo, wu, wd, w_far, fetched,
    ot_ref, lse_ref, att_ref, w_near, w_cross, w_later,
    seg_col, wide, sent, got, local, w_sent, w_got, *spread_sems,
):
    h = pl.program_id(0)
    length = qt_ref.shape[1]
    rows = att_ref.shape[1]
    width = heads * HD

    share = fetched.shape[0]

    def slot(n):
        return w_later.at[pl.ds(pl.multiple_of(n * share, UNIT), share)]

    weights = Spread(dp_count, fetched, slot, spread_sems)
    stay = pltpu.make_async_copy(fetched, slot(lax.axis_index("dp")), local.at[heads])
    peers = [across(1), across(2), across(3)] + weights.peers
    swaps = [
        send(w, w_near.at[pl.ds(n * width, width)], w_sent.at[n], w_got.at[n], across(1))
        for n, w in enumerate((wo, wu, wd))
    ]
    swaps.append(send(w_far, w_cross, w_sent.at[3], w_got.at[3], across(1)))

    @pl.when(h == 0)
    def _():
        hello(peers)
        seg_col[...] = column_of(seg_row)

    for i in range(length // step):
        start, last = i * step, (i + 1) * step
        s = nn(k_ref[:last, :HD], qt_ref[:, start:last])
        s = jnp.where(allowed_mask(seg_row, seg_col, last, start, step), s, NEG)
        top = jnp.max(s, axis=0, keepdims=True)
        p = jnp.exp2(s - top)
        total = jnp.sum(p, axis=0, keepdims=True)
        out = (nn(vt_ref[:, :last], p.astype(BF16)) / total).astype(BF16)
        ot_ref[:, start:last] = out
        wide[pl.ds(pl.multiple_of(h * HD, UNIT), HD), start:last] = out
        lse_ref[0, :, start:last] = top + jnp.log2(total)

    def piece(bit, head):
        src = wide.at[pl.ds(pl.multiple_of(head * HD, UNIT), HD), pl.ds(place(bit, rows), rows)]
        dst = att_ref.at[pl.ds(pl.multiple_of(bit * width + head * HD, UNIT), HD)]
        if bit == 0:
            return pltpu.make_async_copy(src, dst, local.at[head])
        return send(src, dst, sent.at[bit - 1, head], got.at[bit - 1, head], across(bit))

    @pl.when(h == 0)
    def _():
        met(peers)

    for bit in (2, 3, 1, 0):
        piece(bit, h).start()

    @pl.when(h == 0)
    def _():
        weights.start()
        stay.start()
        for copy in swaps:
            copy.start()

    @pl.when(h == heads - 2)
    def _():
        weights.pass_all()

    @pl.when(h == heads - 1)
    def _():
        for copy in swaps:
            copy.wait()
        stay.wait()
        weights.finish()
        for head in range(heads):
            for bit in range(4):
                piece(bit, head).wait()


def attend_call(dp_count, seg_row, qt, k, vt, weights, w_far, fetched, rows):
    width, length = qt.shape
    heads = width // HD
    col = pl.BlockSpec((HD, length), lambda h: (h, 0))
    return pl.pallas_call(
        functools.partial(attend_kernel, 512, heads, dp_count),
        grid=(heads,),
        in_specs=[
            whole((1, length)), col,
            pl.BlockSpec((length, LANES), lambda h: (0, h)), col, ANY, ANY, ANY, ANY, ANY,
        ],
        out_specs=[col, pl.BlockSpec((1, 1, length), lambda h: (h, 0, 0)), ANY, ANY, ANY, ANY],
        scratch_shapes=[
            pltpu.VMEM((length, 8), jnp.int32),
            pltpu.VMEM((width, length), BF16), DMA((3, heads)), DMA((3, heads)), DMA((heads + 1,)),
            DMA((4,)), DMA((4,)), *Spread.sems(dp_count),
        ],
        out_shape=[
            jax.ShapeDtypeStruct((width, length), BF16),
            jax.ShapeDtypeStruct((heads, 1, length), F32),
            jax.ShapeDtypeStruct((4 * width, rows), BF16),
            jax.ShapeDtypeStruct((3 * width, w_far.shape[1]), BF16),
            jax.ShapeDtypeStruct(w_far.shape, BF16),
            jax.ShapeDtypeStruct((dp_count * fetched.shape[0], w_far.shape[1]), BF16),
        ],
        compiler_params=talking(2),
        name="attend",
    )(seg_row, qt, k, vt, *weights, w_far, fetched)


def own_half(half):
    parity = lax.rem(lax.axis_index("tensor"), 2)
    return pl.multiple_of(parity * half, half), pl.multiple_of((1 - parity) * half, half)


def middle_kernel(
    x_ref, g_ref, att_ref, s0, s1, s2, s3, sel, wo_own, wu_own, wd_own,
    w_near, w_far, w_cross, w_later,
    act_ref, gm_ref, grad_out, pack_ref,
    wo, wu, wd, ol, ur, dl, gt, e_sum, whole_b, near_b, half_b, far_b, mine_b, theirs_b,
    w_local, w_sent, w_got, g_sent, g_got, g_local, e_sent, e_got,
):
    width = wo_own.shape[0]
    rank = s0.shape[0]
    rows = x_ref.shape[0]
    half = rows // 2
    me = lax.axis_index("tensor")

    peers = [across(1), across(2), across(3)]
    hello(peers)
    weights, swaps = [], []
    border = w_far.shape[0]
    for n, (own, dst) in enumerate(((wo_own, wo), (wu_own, wu), (wd_own, wd))):
        first, last = n * width, (n + 1) * width
        sources = [(own, 0, 0, width), (w_near, first, width, width)]
        before = max(0, min(border, last) - first)
        if before:
            sources.append((w_far, first, 2 * width, before))
            sources.append((w_cross, first, 3 * width, before))
        group = []
        if before < width:
            later = w_later.at[pl.ds(first + before - border, width - before)]
            sources.append((w_later, first + before - border, 2 * width + before, width - before))
            swap = send(
                later, dst.at[pl.ds(3 * width + before, width - before)],
                w_sent.at[n], w_got.at[n], across(1),
            )
            swaps.append(swap)
            group.append(swap)
        for m, (src, at, to, count) in enumerate(sources):
            copy = pltpu.make_async_copy(
                src.at[pl.ds(at, count)], dst.at[pl.ds(to, count)], w_local.at[n, m]
            )
            copy.start()
            group.append(copy)
        weights.append(group)

    def arrived(n):
        for copy in weights[n]:
            copy.wait()

    smalls = (s0, s1, s2, s3)
    for x, src in enumerate(smalls):
        for slot, dst in enumerate((ol, ur, dl)):
            dst[:, x * width : (x + 1) * width] = src[:, slot * SLOT : slot * SLOT + width].astype(F32)
    out_lower, up_raise, down_lower = (r[...].astype(BF16) for r in (ol, ur, dl))
    out_raise, up_lower, down_raise = (
        sel[n * rank : (n + 1) * rank] for n in (3, 4, 5)
    )

    back = {}
    for r in range(2):
        here = slice(r * half, (r + 1) * half)
        grad = g_ref[here]
        att = att_ref[:, here].astype(F32).T.astype(BF16)
        if r == 0:
            met(peers)
            for swap in swaps:
                swap.start()
        low_out = nt(att, out_lower).astype(BF16)
        grad_low_down = nt(grad, down_raise).astype(BF16)
        if r == 0:
            arrived(0)
        middle = x_ref[here].astype(F32) + (nn(att, wo[...]) + nn(low_out, out_raise))
        factor = lax.rsqrt(jnp.mean(middle * middle, axis=-1, keepdims=True) + EPS)
        unit = middle * factor
        normed = unit.astype(BF16)
        low_up = nt(normed, up_lower).astype(BF16)
        if r == 0:
            arrived(1)
        preact = nt(normed, wu[...]) + nn(low_up, up_raise)
        sigma = 1.0 / (1.0 + jnp.exp(-preact))
        active = (preact * sigma).astype(BF16)
        if r == 0:
            arrived(2)
        low_down = nt(active, down_lower).astype(BF16)
        grad_act = nt(grad, wd[...]) + nn(grad_low_down, down_lower)
        grad_pre = (grad_act * (sigma * (1.0 + preact * (1.0 - sigma)))).astype(BF16)
        grad_low_up = nt(grad_pre, up_raise).astype(BF16)
        grad_mid = nn(grad_pre, wu[...]) + nn(grad_low_up, up_lower)
        dot = jnp.mean(grad_mid * unit, axis=-1, keepdims=True)
        grad_middle = grad.astype(F32) + factor * (grad_mid - unit * dot)
        gm_ref[here] = grad_middle
        grad_attn = grad_middle.astype(BF16)
        grad_low_out = nt(out_raise, grad_attn).astype(BF16)
        for x in (2, 3, 1, 0):
            value = nt(wo[x * width : (x + 1) * width], grad_attn)
            value = value + tn(smalls[x][:, :width], grad_low_out)
            gt[x, :, here] = value.astype(BF16)
            src = gt.at[x, :, pl.ds(r * half, half)]
            dst = grad_out.at[:, pl.ds(pl.multiple_of(me * rows + r * half, half), half)]
            if x:
                copy = send(src, dst, g_sent.at[x - 1, r], g_got.at[x - 1, r], across(x))
            else:
                copy = pltpu.make_async_copy(src, dst, g_local.at[r])
            copy.start()
            back[x, r] = copy
        act_ref[here] = (middle + (nn(active, wd[...]) + nn(low_down, down_raise))).astype(BF16)
        parts = [
            tn(low_out, grad_attn), tn(grad_low_up, normed), tn(low_down, grad),
            nn(grad_low_out, att), tn(low_up, grad_pre), tn(grad_low_down, active),
        ]
        for n, part in enumerate(parts):
            block = slice(n * rank, (n + 1) * rank)
            e_sum[block] = e_sum[block] + part if r else part

    columns = half_b.shape[1]
    keep, give = own_half(columns)
    whole_b[...] = e_sum[: 3 * rank].astype(BF16)
    one = send(whole_b.at[:, pl.ds(give, columns)], near_b, e_sent.at[0], e_got.at[0], across(1))
    one.start()
    quarter = []
    for x in range(4):
        mine_b[x] = jnp.zeros(mine_b.shape[1:], BF16)
        for slot in range(3):
            part = e_sum[(3 + slot) * rank : (4 + slot) * rank, x * width : (x + 1) * width]
            mine_b[x, :, slot * SLOT : slot * SLOT + width] = part.astype(BF16)
        if x:
            copy = send(mine_b.at[x], theirs_b.at[x - 1], e_sent.at[1 + x], e_got.at[1 + x], across(x))
            copy.start()
            quarter.append(copy)
    one.wait()
    half_b[...] = (e_sum[: 3 * rank, pl.ds(keep, columns)] + near_b[...].astype(F32)).astype(BF16)
    two = send(half_b, far_b, e_sent.at[1], e_got.at[1], across(2))
    two.start()
    for copy in quarter:
        copy.wait()
    sums = (mine_b[0].astype(F32) + theirs_b[0].astype(F32)) + (
        theirs_b[1].astype(F32) + theirs_b[2].astype(F32)
    )
    mark = sel[6 * rank :, : SLOT - width].astype(F32)
    sums = jnp.concatenate([sums[:, : sums.shape[1] - mark.shape[1]], mark], axis=1)
    pack_ref[3 * rank : 4 * rank] = sums[:, :columns].astype(BF16)
    pack_ref[4 * rank :] = sums[:, columns:].astype(BF16)
    two.wait()
    pack_ref[: 3 * rank] = (half_b[...].astype(F32) + far_b[...].astype(F32)).astype(BF16)
    for copy in back.values():
        copy.wait()


def middle_call(x, g, att, pieces, sel, weights, fetched, length):
    rows, depth = x.shape
    width = weights[0].shape[0]
    rank = sel.shape[0] // 7
    small = pl.BlockSpec((rank, depth), lambda c: (rows // rank, 0))
    square = pltpu.VMEM((4 * width, depth), BF16)
    thin = pltpu.VMEM((rank, depth), F32)
    pack = (5 * rank, depth // 2)
    halves = pltpu.VMEM((3 * rank, depth // 2), BF16)
    return pl.pallas_call(
        middle_kernel,
        grid=(1,),
        in_specs=[whole((rows, depth))] * 2 + [whole((4 * width, rows))] + [small] * 4
        + [whole(sel.shape)] + [ANY] * 7,
        out_specs=[whole((rows, depth))] * 2 + [ANY, whole(pack)],
        scratch_shapes=[
            square, square, square, thin, thin, thin,
            pltpu.VMEM((4, width, rows), BF16),
            pltpu.VMEM((6 * rank, depth), F32),
            pltpu.VMEM((3 * rank, depth), BF16),
            halves, halves, halves,
            pltpu.VMEM((4, rank, depth), BF16),
            pltpu.VMEM((3, rank, depth), BF16),
            DMA((3, 5)), DMA((3,)), DMA((3,)), DMA((3, 2)), DMA((3, 2)), DMA((2,)), DMA((5,)), DMA((5,)),
        ],
        out_shape=[
            jax.ShapeDtypeStruct((rows, depth), BF16),
            jax.ShapeDtypeStruct((rows, depth), F32),
            jax.ShapeDtypeStruct((width, length), BF16),
            jax.ShapeDtypeStruct(pack, BF16),
        ],
        compiler_params=talking(3),
        name="feed_forward",
    )(x, g, att, *pieces, sel, *weights, *fetched)


def backward_kernel(
    heads, dp_count, seg_row, pack_ref, low, rsel,
    qt_hbm, kt_hbm, ot_hbm, grad_hbm, k_hbm, v_hbm, lse_hbm, p0, p1, p2, p3, stack_hbm, x_hbm, gm_hbm,
    out_ref, first_ref, first_other, all_ref, other_ref,
    seg_col, qt, kt, ot, grad, k, v, lse, row_dot, dq, dk, dv,
    grads, normed, stack, x_buf, gm_buf, ours, to_near, from_near, to_far, from_far,
    lower_sum, raise_sum, whole_b, near_b, half_b, far_b, pack_b,
    head_sems, loads, g_sent, g_got, e_sent, e_got, last, *spread_sems,
):
    rank, width = rsel.shape[0] // 3, rsel.shape[1]
    length = qt.shape[1]
    rows = out_ref.shape[0]
    middle = length // 2
    chunks = from_far.shape[0]
    step = rows // chunks
    block = 256
    shared = 3 * rank
    me = lax.axis_index("tensor")
    mine = lax.axis_index("dp")
    early = Spread(dp_count, pack_ref, lambda n: first_ref.at[n], spread_sems[:4])
    spread = Spread(dp_count, pack_b, lambda n: all_ref.at[n], spread_sems[4:])
    peers = [across(1), across(2)] + spread.peers
    hello(peers)

    def of_head(h):
        lines = pl.ds(pl.multiple_of(h * HD, UNIT), HD)
        lanes = pl.ds(pl.multiple_of(h * LANES, LANES), LANES)
        return [
            pltpu.make_async_copy(src.at[lines], dst.at[lines], head_sems.at[n, h])
            for n, (src, dst) in enumerate(((qt_hbm, qt), (kt_hbm, kt), (ot_hbm, ot), (grad_hbm, grad)))
        ] + [
            pltpu.make_async_copy(src.at[:, lanes], dst.at[:, lanes], head_sems.at[4 + n, h])
            for n, (src, dst) in enumerate(((k_hbm, k), (v_hbm, v)))
        ]

    load = {"lse": pltpu.make_async_copy(lse_hbm, lse, last.at[4])}
    load["lse"].start()

    @pl.loop(0, heads)
    def _(h):
        for copy in of_head(h):
            copy.start()

    for x in range(4):
        load[x] = pltpu.make_async_copy((p0, p1, p2, p3)[x].at[pl.ds(0, rows)], normed.at[x], loads.at[x])
    load["stack"] = pltpu.make_async_copy(stack_hbm, stack, last.at[0])
    load["x"] = pltpu.make_async_copy(x_hbm, x_buf, last.at[1])
    load["gm"] = pltpu.make_async_copy(gm_hbm, gm_buf, last.at[2])
    for key in ("stack", 3, 2, 1, 0, "x", "gm"):
        load[key].start()
    seg_col[...] = column_of(seg_row)
    load["lse"].wait()
    met(peers)
    stays = [pltpu.make_async_copy(pack_ref, first_ref.at[mine], last.at[5])]
    stays[0].start()
    early.start()

    def tile(h, keys, count, queries, masked):
        lines = pl.ds(pl.multiple_of(h * HD, UNIT), HD)
        lanes = pl.ds(pl.multiple_of(h * LANES, LANES), LANES)
        at = pl.ds(queries, block)
        over = pl.ds(keys, count)
        query, given = qt[lines, at], grad[lines, at]
        s = nn(k[over, lanes][:, :HD], query)
        dp = nn(v[over, lanes][:, :HD], given)
        ok = seg_col[over, :1] == seg_row[:, at]
        if masked:
            key = lax.broadcasted_iota(jnp.int32, (count, block), 0)
            place_of = lax.broadcasted_iota(jnp.int32, (count, block), 1) + (count - block)
            ok = ok & (key <= place_of)
        p = jnp.exp2(jnp.where(ok, s, NEG) - lse[h, :, at])
        ds = (p * (dp - row_dot[h, :, at])).astype(BF16)
        return nn(kt[lines, over], ds), nt(query, ds), nt(given, p.astype(BF16))

    def corner(h, base):
        lines = pl.ds(pl.multiple_of(h * HD, UNIT), HD)
        for i in range(middle // block):
            count = (i + 1) * block
            queries = pl.multiple_of(base + i * block, block)
            a, b, c = tile(h, base, count, queries, True)
            dq[lines, pl.ds(queries, block)] += a
            dk[lines, pl.ds(base, count)] += b
            dv[lines, pl.ds(base, count)] += c

    far_base = pl.multiple_of((1 - me // 2) * middle, middle)
    near_base = pl.multiple_of((me // 2) * middle, middle)

    @pl.loop(0, heads)
    def _(h):
        for copy in of_head(h):
            copy.wait()
        lines = pl.ds(pl.multiple_of(h * HD, UNIT), HD)
        row_dot[h] = jnp.sum(grad[lines].astype(F32) * ot[lines].astype(F32), axis=0, keepdims=True)
        nothing = jnp.zeros((HD, middle), F32)
        dq[lines, :middle] = nothing
        dk[lines, middle:] = nothing
        dv[lines, middle:] = nothing
        for i in range(middle // block):
            at = middle + i * block
            a, b, c = tile(h, 0, middle, at, False)
            dq[lines, at : at + block] = a
            dk[lines, :middle] = dk[lines, :middle] + b if i else b
            dv[lines, :middle] = dv[lines, :middle] + c if i else c
        corner(h, far_base)

    def ready(x):
        here = pl.ds(place(x, rows), rows)
        for n, (src, factor) in enumerate(((dq, SCORE_SCALE), (dk, 1.0 / LOG2E), (dv, None))):
            value = src[:, here]
            value = (value if factor is None else value * factor).astype(BF16)
            grads[x, n * width : (n + 1) * width] = value
            grads[x, 3 * width + n * rank : 3 * width + (n + 1) * rank] = nn(
                rsel[n * rank : (n + 1) * rank], value
            ).astype(BF16)

    def adapters(x, starts=False):
        load[x].wait()
        here = pl.ds(place(x, rows), rows)
        for n in range(3):
            value = grads[x, n * width : (n + 1) * width]
            part = nt(low[n * rank : (n + 1) * rank, here], value)
            at = slice(n * SLOT, n * SLOT + width)
            raise_sum[:, at] = part if starts else raise_sum[:, at] + part
        part = nn(grads[x, 3 * width :], normed[x])
        lower_sum[...] = part if starts else lower_sum[...] + part

    half = rows // 2

    def through(x, r):
        return tn(grads[x, :, r * half : (r + 1) * half], stack[...])

    pair = [
        [
            send(
                to_near.at[n, pl.ds(r * half, half)], from_near.at[n, pl.ds(r * half, half)],
                g_sent.at[2 * n + r], g_got.at[2 * n + r], across(1),
            )
            for r in range(2)
        ]
        for n in range(2)
    ]
    far = [
        send(to_far.at[c], from_far.at[c], g_sent.at[4 + c], g_got.at[4 + c], across(2))
        for c in range(chunks)
    ]
    raise_sum[...] = jnp.zeros_like(raise_sum)
    ready(3)
    load["stack"].wait()
    for r in range(2):
        to_near[1, r * half : (r + 1) * half] = through(3, r).astype(BF16)
        pair[1][r].start()
    ready(2)
    for r in range(2):
        total = through(2, r)
        pair[1][r].wait()
        for c in range(r * chunks // 2, (r + 1) * chunks // 2):
            here = slice(c * step - r * half, (c + 1) * step - r * half)
            there = slice(c * step, (c + 1) * step)
            to_far[c] = (total[here] + from_near[1, there].astype(F32)).astype(BF16)
            if c < chunks // 2:
                far[c].start()
    early.pass_all()
    adapters(3, True)
    adapters(2)

    @pl.loop(0, heads)
    def _(h):
        corner(h, near_base)

    stays[0].wait()
    early.finish()
    trade = [
        send(src.at[:, pl.ds(0, shared)], dst, e_sent.at[2 + n], e_got.at[2 + n], across(1))
        for n, (src, dst) in enumerate(((first_ref, first_other), (all_ref, other_ref)))
    ]
    trade[0].start()
    ready(1)
    adapters(1)
    ready(0)
    adapters(0)

    columns = half_b.shape[1]
    keep, give = own_half(columns)
    whole_b[...] = lower_sum[...].astype(BF16)
    one = send(whole_b.at[:, pl.ds(give, columns)], near_b, e_sent.at[0], e_got.at[0], across(1))
    one.start()
    pack_b[shared : shared + rank] = raise_sum[:, :columns].astype(BF16)
    pack_b[shared + rank :] = raise_sum[:, columns:].astype(BF16)
    one.wait()
    half_b[...] = (lower_sum[:, pl.ds(keep, columns)] + near_b[...].astype(F32)).astype(BF16)
    two = send(half_b, far_b, e_sent.at[1], e_got.at[1], across(2))
    two.start()
    for c in range(chunks // 2, chunks):
        far[c].start()
    for r in range(2):
        to_near[0, r * half : (r + 1) * half] = through(1, r).astype(BF16)
        pair[0][r].start()
    two.wait()
    pack_b[:shared] = (half_b[...].astype(F32) + far_b[...].astype(F32)).astype(BF16)
    stays.append(pltpu.make_async_copy(pack_b, all_ref.at[mine], last.at[3]))
    stays[1].start()
    spread.start()
    for r in range(2):
        ours[r * half : (r + 1) * half] = through(0, r)
    for r in range(2):
        here = slice(r * half, (r + 1) * half)
        pair[0][r].wait()
        ours[here] = ours[here] + from_near[0, here].astype(F32)
    load["x"].wait()
    load["gm"].wait()

    def conclude(c):
        here = slice(c * step, (c + 1) * step)
        far[c].wait()
        x = x_buf[here].astype(F32)
        factor = lax.rsqrt(jnp.mean(x * x, axis=-1, keepdims=True) + EPS)
        unit = x * factor
        grad_in = ours[here] + from_far[c].astype(F32)
        dot = jnp.mean(grad_in * unit, axis=-1, keepdims=True)
        out_ref[here] = (gm_buf[here] + factor * (grad_in - unit * dot)).astype(BF16)

    conclude(0)
    conclude(1)
    spread.pass_all()
    conclude(2)
    stays[1].wait()
    spread.finish()
    trade[1].start()
    conclude(3)
    trade[0].wait()
    trade[1].wait()


def backward_call(dp_count, seg_row, pack, low, rsel, columns, rows_of, lse, pieces, stack, x, gm):
    rows, depth = x.shape
    rank, width = rsel.shape[0] // 3, rsel.shape[1]
    heads = width // HD
    length = seg_row.shape[1]
    total = stack.shape[0]
    chunks = 4
    halves = pltpu.VMEM((3 * rank, depth // 2), BF16)
    lines = pltpu.VMEM((chunks, rows // chunks, depth), BF16)
    col = pltpu.VMEM((width, length), BF16)
    row = pltpu.VMEM((length, heads * LANES), BF16)
    sums = pltpu.VMEM((width, length), F32)
    return pl.pallas_call(
        functools.partial(backward_kernel, heads, dp_count),
        in_specs=[VMEM] * 4 + [ANY] * 14,
        out_specs=[VMEM, ANY, ANY, ANY, ANY],
        scratch_shapes=[
            pltpu.VMEM((length, 8), jnp.int32), col, col, col, col, row, row,
            pltpu.VMEM((heads, 1, length), F32),
            pltpu.VMEM((heads, 1, length), F32),
            sums, sums, sums,
            pltpu.VMEM((4, total, rows), BF16),
            pltpu.VMEM((4, rows, depth), BF16),
            pltpu.VMEM((total, depth), BF16),
            pltpu.VMEM((rows, depth), BF16),
            pltpu.VMEM((rows, depth), F32),
            pltpu.VMEM((rows, depth), F32),
            pltpu.VMEM((2, rows, depth), BF16),
            pltpu.VMEM((2, rows, depth), BF16),
            lines, lines,
            pltpu.VMEM((3 * rank, depth), F32),
            pltpu.VMEM((rank, depth), F32),
            pltpu.VMEM((3 * rank, depth), BF16),
            halves, halves, halves,
            pltpu.VMEM(pack.shape, BF16),
            DMA((6, heads)), DMA((4,)), DMA((4 + chunks,)), DMA((4 + chunks,)), DMA((4,)), DMA((4,)),
            DMA((6,)), *Spread.sems(dp_count), *Spread.sems(dp_count),
        ],
        out_shape=[
            jax.ShapeDtypeStruct((rows, depth), BF16),
            jax.ShapeDtypeStruct((dp_count, *pack.shape), BF16),
            jax.ShapeDtypeStruct((dp_count, 3 * rank, depth // 2), BF16),
            jax.ShapeDtypeStruct((dp_count, *pack.shape), BF16),
            jax.ShapeDtypeStruct((dp_count, 3 * rank, depth // 2), BF16),
        ],
        compiler_params=talking(4),
        name="backward",
    )(seg_row, pack, low, rsel, *columns, *rows_of, lse, *pieces, stack, x, gm)


def sets_kernel(scal, first, first_other, second, second_other, *outs):
    rank = outs[0].shape[1]
    columns = first.shape[2]
    count = first.shape[0]
    here = pl.ds(pl.multiple_of(scal[count] * columns, columns), columns)
    there = pl.ds(pl.multiple_of((1 - scal[count]) * columns, columns), columns)
    for ref in outs:
        ref[...] = jnp.zeros_like(ref)

    @pl.loop(0, count)
    def _(n):
        which = scal[n]
        for group, pack, other in ((outs[:6], first, first_other), (outs[6:], second, second_other)):
            for k in range(3):
                part = slice(k * rank, (k + 1) * rank)
                group[k][which, :, here] += pack[n, part].astype(F32)
                group[k][which, :, there] += other[n, part].astype(F32)
            thin = jnp.concatenate(
                [pack[n, 3 * rank : 4 * rank], pack[n, 4 * rank :]], axis=1
            ).astype(F32)
            for k in range(3):
                width = group[3 + k].shape[2]
                group[3 + k][which] += thin[:, k * SLOT : k * SLOT + width]


def sets_call(scal, packs, sets, width):
    _, five, columns = packs[0].shape
    rank, depth = five // 5, 2 * columns
    full = jax.ShapeDtypeStruct((sets, rank, depth), F32)
    thin = jax.ShapeDtypeStruct((sets, rank, width), F32)
    shapes = [full, full, full, thin, thin, thin] * 2
    return pl.pallas_call(
        sets_kernel,
        grid_spec=pltpu.PrefetchScalarGridSpec(
            num_scalar_prefetch=1,
            grid=(1,),
            in_specs=[whole(p.shape) for p in packs],
            out_specs=[whole(t.shape) for t in shapes],
        ),
        out_shape=shapes,
        compiler_params=params(),
        name="set_sums",
    )(scal, *packs)


def on_device(
    dp_count,
    tokens,
    segment_ids,
    adapter_choice,
    cotangent,
    weight_query,
    weight_key,
    weight_value,
    weight_output,
    weight_upward,
    weight_downward,
    query_lower,
    query_raise,
    key_lower,
    key_raise,
    value_lower,
    value_raise,
    output_lower,
    output_raise,
    upward_lower,
    upward_raise,
    downward_lower,
    downward_raise,
):
    x, g = tokens[0], cotangent[0]
    rows = x.shape[0]
    length = segment_ids.shape[1]
    sets = query_lower.shape[0]
    width = query_raise.shape[2]
    seg_row = segment_ids
    parity = lax.rem(lax.axis_index("tensor").astype(jnp.int32), 2).reshape(1)

    feed = (weight_output.T, weight_upward.T, weight_downward.T)
    (qt, kt, vt, k, v, low, stack, own, near, far, cross, sel, rsel, w_far, fetched) = front_call(
        dp_count,
        adapter_choice,
        x,
        (query_lower, key_lower, value_lower, output_raise, upward_lower, downward_raise),
        (output_lower, upward_raise, downward_lower, query_raise, key_raise, value_raise),
        (weight_query.T, weight_key.T, weight_value.T),
        feed,
        length,
    )
    pieces = (own, near, far, cross)
    ot, lse, att, w_near, w_cross, w_later = attend_call(
        dp_count, seg_row, qt, k, vt, feed, w_far, fetched, rows
    )
    act, gm, grad, pack = middle_call(
        x, g, att, pieces, sel, feed, (w_near, w_far, w_cross, w_later), length
    )
    input_grad, first, first_other, second, second_other = backward_call(
        dp_count, seg_row, pack, low, rsel, (qt, kt, ot, grad), (k, v), lse, pieces, stack, x, gm
    )
    chosen = first[:, -1, -1].astype(jnp.int32)
    out = sets_call(
        jnp.concatenate([chosen, parity]), (first, first_other, second, second_other), sets, width
    )
    (out_raise_g, up_lower_g, down_raise_g, out_lower_g, up_raise_g, down_lower_g) = out[:6]
    (q_lower_g, k_lower_g, v_lower_g, q_raise_g, k_raise_g, v_raise_g) = out[6:]
    return (
        act[None],
        input_grad[None],
        q_lower_g,
        q_raise_g,
        k_lower_g,
        k_raise_g,
        v_lower_g,
        v_raise_g,
        out_lower_g,
        out_raise_g,
        up_lower_g,
        up_raise_g,
        down_lower_g,
        down_raise_g,
    )


def solution(mesh):
    split = P(None, None, "tensor")
    rows = P("dp", "tensor", None)
    columns = P(None, "tensor")
    return jax.shard_map(
        functools.partial(on_device, mesh.shape["dp"]),
        mesh=mesh,
        in_specs=(rows, P("dp", None), P("dp"), rows)
        + (columns,) * 6
        + (P(), split) * 3
        + (split, P(), P(), split, split, P()),
        out_specs=(rows, rows)
        + (P(), split) * 3
        + (split, P(), P(), split, split, P()),
        check_vma=False,
    )
```

```python
import functools
import math

import jax
import jax.numpy as jnp
from jax import lax
from jax.experimental import pallas as pl
from jax.experimental.pallas import tpu as pltpu
from jax.sharding import PartitionSpec as P

HD = 80
LANES = 128
EPS = 1e-06
NEG = -1e30
F32 = jnp.float32
BF16 = jnp.bfloat16
VMEM_BYTES = 60 * 2**20
SCORE_SCALE = HD ** (-0.5)
LOG2E = math.log2(math.e)
SLOT = 384
UNIT = 16
MESH = pl.DeviceIdType.MESH

NT = (((1,), (1,)), ((), ()))
TN = (((0,), (0,)), ((), ()))


def nn(left, right):
    return jnp.dot(left, right, preferred_element_type=F32)


def nt(left, right):
    return lax.dot_general(left, right, NT, preferred_element_type=F32)


def tn(left, right):
    return lax.dot_general(left, right, TN, preferred_element_type=F32)


def params(**more):
    return pltpu.CompilerParams(vmem_limit_bytes=VMEM_BYTES, **more)


def talking(number):
    return params(collective_id=number, has_side_effects=True)


def whole(shape):
    return pl.BlockSpec(shape, lambda *_: (0,) * len(shape))


ANY = pl.BlockSpec(memory_space=pl.ANY)
VMEM = pl.BlockSpec(memory_space=pltpu.VMEM)
DMA = pltpu.SemaphoreType.DMA


def across(bit):
    return {"tensor": lax.axis_index("tensor") ^ bit}


def along(step, count):
    return {"dp": lax.rem(lax.axis_index("dp") + step, count)}


def hello(peers):
    for peer in peers:
        pl.semaphore_signal(
            pltpu.get_barrier_semaphore(), inc=1, device_id=peer, device_id_type=MESH
        )


def met(peers):
    pl.semaphore_wait(pltpu.get_barrier_semaphore(), len(peers))


def send(src, dst, send_sem, recv_sem, peer):
    return pltpu.make_async_remote_copy(
        src_ref=src, dst_ref=dst, send_sem=send_sem, recv_sem=recv_sem,
        device_id=peer, device_id_type=MESH,
    )


class Spread:
    def __init__(self, count, source, slot, sems):
        me = lax.axis_index("dp")
        sent, got, x_sent, x_got = sems
        self.ring = [{"dp": lax.rem(me + 2 * n, count)} for n in range(1, count // 2)]
        self.partner = {"dp": me + 1 - 2 * lax.rem(me, 2)}
        self.direct = [
            send(source, slot(me), sent.at[n], got.at[n], peer) for n, peer in enumerate(self.ring)
        ]
        self.own = send(source, slot(me), x_sent.at[0], x_got.at[0], self.partner)
        self.onward = []
        for n in range(1, count // 2):
            block = slot(lax.rem(me + count - 2 * n, count))
            self.onward.append(send(block, block, x_sent.at[n], x_got.at[n], self.partner))

    @staticmethod
    def sems(count):
        half = count // 2
        return [DMA((half - 1,)), DMA((half - 1,)), DMA((half,)), DMA((half,))]

    @property
    def peers(self):
        return [self.partner, *self.ring]

    def start(self):
        for copy in self.direct:
            copy.start()
        self.own.start()

    def pass_on(self, n):
        self.direct[n].wait_recv()
        self.onward[n].start()

    def pass_all(self):
        for n in range(len(self.direct)):
            self.pass_on(n)

    def finish(self):
        self.own.wait()
        for copy in self.onward:
            copy.wait()
        for copy in self.direct:
            copy.wait_send()


def place(bit, rows):
    return pl.multiple_of((lax.axis_index("tensor") ^ bit) * rows, rows)


def column_of(seg_row):
    return jnp.broadcast_to(seg_row[...], (8, seg_row.shape[1])).T


def front_kernel(
    heads, dp_count, choice, x_hbm, ql, kl, vl, orr, ul, dr, ol, ur, dl, qr, kr, vr, wq, wk, wv, wo, wu, wd,
    seg_row,
    qt_out, kt_out, k_out, v_out, low_out, stack_out, own_out, near_out, far_out, cross_out,
    sel_out, rsel_out, w_near, w_far_out, w_cross, ot_out, lse_out, att_out,
    x_buf, wide, thin, mine_0, mine_1, fetched_0, fetched_1, own, near, far, cross, stack, sel, rsel,
    qt, kt, vt, k, v, low, w_far, seg_col, acc, top_of, total_of, ot, lse,
    loads, unit_sems, w_sent, w_got, sent, got, local, a_sent, a_got, a_local, s_sent, s_got, *spread_sems,
):
    width = heads * HD
    rank = rsel.shape[0] // 3
    rows = x_buf.shape[0]
    half = rows // 2
    cuts = ((0, half), (half, rows // 4), (half + rows // 4, rows // 4 + rank))
    mine, fetched = (mine_0, mine_1), (fetched_0, fetched_1)
    shares_of = [ref.shape[0] for ref in fetched]
    begins = (0, dp_count * shares_of[0], dp_count * sum(shares_of))
    length = qt.shape[1]
    middle = length // 2
    me = lax.axis_index("dp")

    def slots(pile):
        return lambda n: w_far.at[
            pl.ds(pl.multiple_of(begins[pile] + n * shares_of[pile], UNIT), shares_of[pile])
        ]

    weights = [
        Spread(dp_count, fetched[pile], slots(pile), spread_sems[4 * pile : 4 * pile + 4])
        for pile in range(2)
    ]
    peers = [across(1), across(2), across(3)] + weights[0].peers
    hello(peers)

    per_weight = wo.shape[0] // UNIT

    pieces = []
    for pile in range(2):
        count = shares_of[pile] // UNIT
        for u in range(count):
            number = lax.rem(begins[pile] // UNIT + me * count + u, 3 * per_weight)
            pieces.append((mine[pile].at[pl.ds(u * UNIT, UNIT)], number, unit_sems.at[len(pieces)]))
    for dst, number, sem in pieces:
        for n, w in enumerate((wo, wu, wd)):

            @pl.when(number // per_weight == n)
            def _(dst=dst, number=number, sem=sem, n=n, w=w):
                at = pl.multiple_of((number - n * per_weight) * UNIT, UNIT)
                pltpu.make_async_copy(w.at[pl.ds(at, UNIT)], dst, sem).start()

    lines = [
        pltpu.make_async_copy(
            x_hbm.at[pl.ds(c * half, half)], x_buf.at[pl.ds(c * half, half)], loads.at[c]
        )
        for c in range(2)
    ]
    for copy in lines:
        copy.start()
    thins = [
        pltpu.make_async_copy(ref, thin.at[n], loads.at[2 + n])
        for n, ref in enumerate((ol, ur, dl, qr, kr, vr))
    ]
    wides = [
        pltpu.make_async_copy(ref, wide.at[n], loads.at[8 + n])
        for n, ref in enumerate((ql, kl, vl, orr, ul, dr))
    ]
    squares = [
        pltpu.make_async_copy(ref, stack.at[pl.ds(n * width, width)], loads.at[14 + n])
        for n, ref in enumerate((wq, wk, wv))
    ]
    for copy in (*thins, *wides, *squares):
        copy.start()

    def part(ref, c):
        return ref.at[pl.ds(*cuts[c])]

    parts = range(len(cuts))
    to_far = [send(part(own, c), part(far, c), sent.at[0, c], got.at[0, c], across(2)) for c in parts]
    to_near = [send(part(own, c), part(near, c), sent.at[1, c], got.at[1, c], across(1)) for c in parts]
    on = [send(part(far, c), part(cross, c), sent.at[2, c], got.at[2, c], across(1)) for c in parts]
    shares = [
        send(mine[n], fetched[n], w_sent.at[n], w_got.at[n], across(2)) for n in range(2)
    ]
    which = choice[0]
    for dst, number, sem in pieces:
        pltpu.make_async_copy(wo.at[pl.ds(0, UNIT)], dst, sem).wait()
    met(peers)
    shares[0].start()
    for c in range(2):
        here = slice(c * half, (c + 1) * half)
        lines[c].wait()
        x = x_buf[here].astype(F32)
        factor = lax.rsqrt(jnp.mean(x * x, axis=-1, keepdims=True) + EPS)
        own[here] = (x * factor).astype(BF16)
        if c == 1:
            own[rows:] = jnp.zeros((rank, own.shape[1]), BF16)
            for copy in thins:
                copy.wait()
            for n in range(3):
                own[rows:, n * SLOT : n * SLOT + width] = thin[n, which]
        for n in (0,) if c == 0 else parts[1:]:
            to_far[n].start()
            to_near[n].start()
    shares[1].start()

    pending = []

    def keep(src, dst):
        copy = pltpu.make_async_copy(src, dst, local.at[len(pending)])
        copy.start()
        pending.append(copy)

    keep(own, own_out)
    for copy in wides:
        copy.wait()
    for n in range(6):
        sel[n * rank : (n + 1) * rank] = wide[n, which]
    mark = jnp.full((rank, sel.shape[1]), which, jnp.int32).astype(F32)
    sel[6 * rank :] = mark.astype(BF16)
    keep(sel, sel_out)
    for n in range(3):
        rsel[n * rank : (n + 1) * rank] = thin[3 + n, which]
    keep(rsel, rsel_out)
    stack[3 * width :] = sel[: 3 * rank]
    for copy in squares:
        copy.wait()
    keep(stack, stack_out)

    def project(ref, bit, c):
        first, size = cuts[c][0], min(cuts[c][1], rows - cuts[c][0])
        block = ref[first : first + size]
        out = nt(stack[...], block)
        down = out[3 * width :].astype(BF16)
        here = pl.ds(pl.multiple_of(place(bit, rows) + first, LANES), size)
        low[:, here] = down
        for n, (col, row) in enumerate(((qt, None), (kt, k), (vt, v))):
            low_n = slice(n * rank, (n + 1) * rank)
            value = out[n * width : (n + 1) * width] + tn(rsel[low_n], down[low_n])
            if n == 0:
                value = value * (SCORE_SCALE * LOG2E)
            value = value.astype(BF16)
            col[:, here] = value
            if row is not None:
                for h in range(heads):
                    row[here, h * LANES : h * LANES + HD] = value[h * HD : (h + 1) * HD].T
        for src, dst in ((qt, qt_out), (kt, kt_out), (low, low_out)):
            keep(src.at[:, here], dst.at[:, here])
        for src, dst in ((k, k_out), (v, v_out)):
            keep(src.at[here], dst.at[here])

    seg_col[...] = column_of(seg_row)
    block = rows

    def of_head(h):
        lines = pl.ds(pl.multiple_of(h * HD, UNIT), HD)
        lanes = pl.ds(pl.multiple_of(h * LANES, LANES), LANES)
        return lines, lanes

    def attend(h, keys, count, queries, masked):
        lines, lanes = of_head(h)
        at, over = pl.ds(queries, block), pl.ds(keys, count)
        s = nn(k[over, lanes][:, :HD], qt[lines, at])
        ok = seg_col[over, :1] == seg_row[:, at]
        if masked:
            key = lax.broadcasted_iota(jnp.int32, (count, block), 0)
            ok = ok & (key <= lax.broadcasted_iota(jnp.int32, (count, block), 1) + (count - block))
        s = jnp.where(ok, s, NEG)
        top = jnp.max(s, axis=0, keepdims=True)
        p = jnp.exp2(s - top)
        return top, jnp.sum(p, axis=0, keepdims=True), nn(vt[lines, over], p.astype(BF16))

    def corner(h, base):
        lines, _ = of_head(h)
        for i in range(middle // block):
            queries = pl.multiple_of(base + i * block, block)
            top, total, out = attend(h, base, (i + 1) * block, queries, True)
            top_of[h, :, pl.ds(queries, block)] = top
            total_of[h, :, pl.ds(queries, block)] = total
            acc[lines, pl.ds(queries, block)] = out

    chip = lax.axis_index("tensor") // 2
    far_base = pl.multiple_of((1 - chip) * middle, middle)
    near_base = pl.multiple_of(chip * middle, middle)

    for c in parts:
        project(own, 0, c)
        if c == 0:
            shares[0].wait_recv()
            weights[0].start()
            keep(fetched[0], slots(0)(me))
    for c in parts:
        to_near[c].wait_recv()
        project(near, 1, c)
    keep(near, near_out)

    @pl.loop(0, heads)
    def _(h):
        corner(h, near_base)

    for c in parts:
        to_far[c].wait_recv()
        on[c].start()
        project(far, 2, c)
        on[c].wait_recv()
        project(cross, 3, c)
        if c == 0:
            weights[0].pass_all()
    shares[1].wait_recv()
    weights[1].start()
    keep(far, far_out)
    keep(cross, cross_out)
    keep(fetched[1], slots(1)(me))

    def piece(bit, head):
        src = ot.at[pl.ds(pl.multiple_of(head * HD, UNIT), HD), pl.ds(place(bit, rows), rows)]
        dst = att_out.at[pl.ds(pl.multiple_of(bit * width + head * HD, UNIT), HD)]
        if bit == 0:
            return pltpu.make_async_copy(src, dst, a_local.at[head])
        return send(src, dst, a_sent.at[bit - 1, head], a_got.at[bit - 1, head], across(bit))

    def region(ref, pile):
        return ref.at[pl.ds(begins[pile], begins[pile + 1] - begins[pile])]

    swaps = [
        send(w, w_near.at[pl.ds(n * width, width)], s_sent.at[n], s_got.at[n], across(1))
        for n, w in enumerate((wo, wu, wd))
    ] + [
        send(region(w_far, n), region(w_cross, n), s_sent.at[3 + n], s_got.at[3 + n], across(1))
        for n in range(2)
    ]
    saved = [
        pltpu.make_async_copy(region(w_far, n), region(w_far_out, n), a_local.at[heads + n])
        for n in range(2)
    ]
    for copy in pending:
        copy.wait()
    settled = len(pending)

    @pl.loop(0, heads)
    def _(h):
        lines, _ = of_head(h)
        corner(h, far_base)
        for i in range(middle // block):
            at = pl.ds(middle + i * block, block)
            top, total, out = attend(h, 0, middle, middle + i * block, False)
            before = top_of[h, :, at]
            high = jnp.maximum(before, top)
            left, right = jnp.exp2(before - high), jnp.exp2(top - high)
            top_of[h, :, at] = high
            total_of[h, :, at] = left * total_of[h, :, at] + right * total
            acc[lines, at] = left * acc[lines, at] + right * out
        ot[lines] = (acc[lines] / total_of[h]).astype(BF16)
        lse[h] = top_of[h] + jnp.log2(total_of[h])
        for bit in (2, 3, 1, 0):
            piece(bit, h).start()

        @pl.when(h == 0)
        def _():
            weights[0].finish()
            for copy in swaps[:4]:
                copy.start()
            saved[0].start()

        @pl.when(h == 1)
        def _():
            weights[1].pass_all()

        @pl.when(h == heads - 2)
        def _():
            weights[1].finish()
            swaps[4].start()
            saved[1].start()

    keep(ot, ot_out)
    keep(lse, lse_out)
    for copy in shares:
        copy.wait_send()
    for copy in (*to_far, *to_near, *on):
        copy.wait_send()
    for copy in (*swaps, *saved):
        copy.wait()

    @pl.loop(0, heads)
    def _(h):
        for bit in range(4):
            piece(bit, h).wait()

    for copy in pending[settled:]:
        copy.wait()


def front_call(dp_count, choice, x, wides, thins, weights, feed, seg_row):
    rows, depth = x.shape
    length = seg_row.shape[1]
    sets, rank, width = thins[0].shape
    heads = width // HD
    total = 3 * (width + rank)
    units = max(2, -(-3 * width // (UNIT * dp_count)))
    later = max(1, units // 4)
    shares = [pltpu.VMEM((n * UNIT, depth), BF16) for n in (units - later, later)]
    fetched = (dp_count * units * UNIT, depth)
    block = (rows + rank, depth)
    col, row, down = (width, length), (length, heads * LANES), (3 * rank, length)
    picked, raised = (7 * rank, depth), (3 * rank, width)

    def of(shape, dtype=BF16):
        return jax.ShapeDtypeStruct(shape, dtype)

    statistic = pltpu.VMEM((heads, 1, length), F32)
    return pl.pallas_call(
        functools.partial(front_kernel, heads, dp_count),
        in_specs=[pl.BlockSpec(memory_space=pltpu.SMEM)] + [ANY] * 19 + [VMEM],
        out_specs=[ANY] * 18,
        out_shape=[of(t) for t in (col, col, row, row, down, (total, depth), block, block, block, block)]
        + [of(t) for t in (picked, raised, (3 * width, depth), fetched, fetched, col)]
        + [of((heads, 1, length), F32), of((4 * width, rows))],
        scratch_shapes=[
            pltpu.VMEM((rows, depth), BF16),
            pltpu.VMEM((6, sets, rank, depth), BF16),
            pltpu.VMEM((6, sets, rank, width), BF16),
            *shares,
            *shares,
        ]
        + [pltpu.VMEM(block, BF16)] * 4
        + [pltpu.VMEM(t, BF16) for t in ((total, depth), picked, raised, col, col, col, row, row, down, fetched)]
        + [
            pltpu.VMEM((length, 8), jnp.int32), pltpu.VMEM(col, F32), statistic, statistic,
            pltpu.VMEM(col, BF16), statistic,
            DMA((17,)), DMA((units,)), DMA((2,)), DMA((2,)), DMA((3, 3)), DMA((3, 3)),
            DMA((4 + 12 * 5 + 3 + 2 + 2,)),
            DMA((3, heads)), DMA((3, heads)), DMA((heads + 2,)), DMA((5,)), DMA((5,)),
        ]
        + Spread.sems(dp_count) * 2,
        compiler_params=talking(0),
        name="front",
    )(choice, x, *wides, *thins, *weights, *feed, seg_row)


def own_half(half):
    parity = lax.rem(lax.axis_index("tensor"), 2)
    return pl.multiple_of(parity * half, half), pl.multiple_of((1 - parity) * half, half)


def middle_kernel(
    x_ref, g_ref, att_ref, s0, s1, s2, s3, sel, wo_own, wu_own, wd_own,
    w_near, w_far, w_cross,
    act_ref, gm_ref, grad_out, e_sum,
    wo, wu, wd, ol, ur, dl, gt,
    w_local, g_sent, g_got, g_local,
):
    width = wo_own.shape[0]
    rank = s0.shape[0]
    rows = x_ref.shape[0]
    half = rows // 2
    me = lax.axis_index("tensor")

    peers = [across(1), across(2), across(3)]
    hello(peers)
    weights = []
    for n, (own, dst) in enumerate(((wo_own, wo), (wu_own, wu), (wd_own, wd))):
        here = pl.ds(n * width, width)
        group = [
            pltpu.make_async_copy(src, dst.at[pl.ds(x * width, width)], w_local.at[n, x])
            for x, src in enumerate((own, w_near.at[here], w_far.at[here], w_cross.at[here]))
        ]
        for copy in group:
            copy.start()
        weights.append(group)

    def arrived(n):
        for copy in weights[n]:
            copy.wait()

    smalls = (s0, s1, s2, s3)
    for x, src in enumerate(smalls):
        for slot, dst in enumerate((ol, ur, dl)):
            dst[:, x * width : (x + 1) * width] = src[:, slot * SLOT : slot * SLOT + width].astype(F32)
    out_lower, up_raise, down_lower = (r[...].astype(BF16) for r in (ol, ur, dl))
    out_raise, up_lower, down_raise = (
        sel[n * rank : (n + 1) * rank] for n in (3, 4, 5)
    )

    back = {}
    for r in range(2):
        here = slice(r * half, (r + 1) * half)
        grad = g_ref[here]
        att = att_ref[:, here].astype(F32).T.astype(BF16)
        low_out = nt(att, out_lower).astype(BF16)
        grad_low_down = nt(grad, down_raise).astype(BF16)
        if r == 0:
            arrived(0)
        middle = x_ref[here].astype(F32) + (nn(att, wo[...]) + nn(low_out, out_raise))
        factor = lax.rsqrt(jnp.mean(middle * middle, axis=-1, keepdims=True) + EPS)
        unit = middle * factor
        normed = unit.astype(BF16)
        low_up = nt(normed, up_lower).astype(BF16)
        if r == 0:
            arrived(1)
        preact = nt(normed, wu[...]) + nn(low_up, up_raise)
        sigma = 1.0 / (1.0 + jnp.exp(-preact))
        active = (preact * sigma).astype(BF16)
        if r == 0:
            arrived(2)
        low_down = nt(active, down_lower).astype(BF16)
        grad_act = nt(grad, wd[...]) + nn(grad_low_down, down_lower)
        grad_pre = (grad_act * (sigma * (1.0 + preact * (1.0 - sigma)))).astype(BF16)
        grad_low_up = nt(grad_pre, up_raise).astype(BF16)
        grad_mid = nn(grad_pre, wu[...]) + nn(grad_low_up, up_lower)
        dot = jnp.mean(grad_mid * unit, axis=-1, keepdims=True)
        grad_middle = grad.astype(F32) + factor * (grad_mid - unit * dot)
        gm_ref[here] = grad_middle
        grad_attn = grad_middle.astype(BF16)
        grad_low_out = nt(out_raise, grad_attn).astype(BF16)
        if r == 0:
            met(peers)
        for x in (2, 3, 1, 0):
            value = nt(wo[x * width : (x + 1) * width], grad_attn)
            value = value + tn(smalls[x][:, :width], grad_low_out)
            gt[x, :, here] = value.astype(BF16)
            src = gt.at[x, :, pl.ds(r * half, half)]
            dst = grad_out.at[:, pl.ds(pl.multiple_of(me * rows + r * half, half), half)]
            if x:
                copy = send(src, dst, g_sent.at[x - 1, r], g_got.at[x - 1, r], across(x))
            else:
                copy = pltpu.make_async_copy(src, dst, g_local.at[r])
            copy.start()
            back[x, r] = copy
        act_ref[here] = (middle + (nn(active, wd[...]) + nn(low_down, down_raise))).astype(BF16)
        parts = [
            tn(low_out, grad_attn), tn(grad_low_up, normed), tn(low_down, grad),
            nn(grad_low_out, att), tn(low_up, grad_pre), tn(grad_low_down, active),
        ]
        for n, part in enumerate(parts):
            block = slice(n * rank, (n + 1) * rank)
            e_sum[block] = e_sum[block] + part if r else part

    for copy in back.values():
        copy.wait()


def middle_call(x, g, att, pieces, sel, weights, fetched, length):
    rows, depth = x.shape
    width = weights[0].shape[0]
    rank = sel.shape[0] // 7
    small = pl.BlockSpec((rank, depth), lambda c: (rows // rank, 0))
    square = pltpu.VMEM((4 * width, depth), BF16)
    thin = pltpu.VMEM((rank, depth), F32)
    sums = (6 * rank, depth)
    return pl.pallas_call(
        middle_kernel,
        grid=(1,),
        in_specs=[whole((rows, depth))] * 2 + [whole((4 * width, rows))] + [small] * 4
        + [whole(sel.shape)] + [ANY] * 6,
        out_specs=[whole((rows, depth))] * 2 + [ANY, whole(sums)],
        scratch_shapes=[
            square, square, square, thin, thin, thin,
            pltpu.VMEM((4, width, rows), BF16),
            DMA((3, 4)), DMA((3, 2)), DMA((3, 2)), DMA((2,)),
        ],
        out_shape=[
            jax.ShapeDtypeStruct((rows, depth), BF16),
            jax.ShapeDtypeStruct((rows, depth), F32),
            jax.ShapeDtypeStruct((width, length), BF16),
            jax.ShapeDtypeStruct(sums, F32),
        ],
        compiler_params=talking(3),
        name="feed_forward",
    )(x, g, att, *pieces, sel, *weights, *fetched)


def backward_kernel(
    heads, dp_count, seg_row, e_sum, sel, low, rsel,
    qt_hbm, kt_hbm, ot_hbm, grad_hbm, k_hbm, v_hbm, lse_hbm, p0, p1, p2, p3, stack_hbm, x_hbm, gm_hbm,
    out_ref, first_ref, first_other, all_ref, other_ref, chosen_ref,
    seg_col, qt, kt, ot, grad, k, v, lse, row_dot, dq, dk, dv,
    grads, normed, stack, x_buf, gm_buf, ours, to_near, from_near, to_far, from_far,
    lower_sum, raise_sum, whole_a, near_a, half_a, far_a, pack_a, whole_b, near_b, half_b, far_b, pack_b,
    mine_b, theirs_b, marks,
    head_sems, loads, g_sent, g_got, e_sent, e_got, last, *spread_sems,
):
    rank, width = rsel.shape[0] // 3, rsel.shape[1]
    length = qt.shape[1]
    rows = out_ref.shape[0]
    middle = length // 2
    chunks = from_far.shape[0]
    step = rows // chunks
    block = 256
    shared = 3 * rank
    me = lax.axis_index("tensor")
    mine = lax.axis_index("dp")
    early = Spread(dp_count, pack_a, lambda n: first_ref.at[n], spread_sems[:4])
    spread = Spread(dp_count, pack_b, lambda n: all_ref.at[n], spread_sems[4:])
    peers = [across(1), across(2), across(3)] + spread.peers
    hello(peers)

    def of_head(h):
        lines = pl.ds(pl.multiple_of(h * HD, UNIT), HD)
        lanes = pl.ds(pl.multiple_of(h * LANES, LANES), LANES)
        return [
            pltpu.make_async_copy(src.at[lines], dst.at[lines], head_sems.at[n, h])
            for n, (src, dst) in enumerate(((qt_hbm, qt), (kt_hbm, kt), (ot_hbm, ot), (grad_hbm, grad)))
        ] + [
            pltpu.make_async_copy(src.at[:, lanes], dst.at[:, lanes], head_sems.at[4 + n, h])
            for n, (src, dst) in enumerate(((k_hbm, k), (v_hbm, v)))
        ]

    load = {"lse": pltpu.make_async_copy(lse_hbm, lse, last.at[4])}
    load["lse"].start()

    @pl.loop(0, heads)
    def _(h):
        for copy in of_head(h):
            copy.start()

    for x in range(4):
        load[x] = pltpu.make_async_copy((p0, p1, p2, p3)[x].at[pl.ds(0, rows)], normed.at[x], loads.at[x])
    load["stack"] = pltpu.make_async_copy(stack_hbm, stack, last.at[0])
    load["x"] = pltpu.make_async_copy(x_hbm, x_buf, last.at[1])
    load["gm"] = pltpu.make_async_copy(gm_hbm, gm_buf, last.at[2])
    for key in ("stack", 3, 2, 1, 0, "x", "gm"):
        load[key].start()
    seg_col[...] = column_of(seg_row)
    stays = [
        pltpu.make_async_copy(pack_a, first_ref.at[mine], last.at[5]),
        pltpu.make_async_copy(pack_b, all_ref.at[mine], last.at[3]),
    ]
    columns = half_b.shape[1]
    keep, give = own_half(columns)

    def to_pair(src, dst, n):
        return send(src.at[:, pl.ds(give, columns)], dst, e_sent.at[n], e_got.at[n], across(1))

    whole_a[...] = e_sum[:shared].astype(BF16)
    for x in range(4):
        mine_b[x] = jnp.zeros(mine_b.shape[1:], BF16)
        for slot in range(3):
            part = e_sum[(3 + slot) * rank : (4 + slot) * rank, x * width : (x + 1) * width]
            mine_b[x, :, slot * SLOT : slot * SLOT + width] = part.astype(BF16)
    firsts = [to_pair(whole_a, near_a, 4)] + [
        send(mine_b.at[x], theirs_b.at[x - 1], e_sent.at[5 + x], e_got.at[5 + x], across(x))
        for x in (1, 2, 3)
    ]
    second = send(half_a, far_a, e_sent.at[5], e_got.at[5], across(2))
    load["lse"].wait()

    def tile(h, keys, count, queries, masked):
        lines = pl.ds(pl.multiple_of(h * HD, UNIT), HD)
        lanes = pl.ds(pl.multiple_of(h * LANES, LANES), LANES)
        at = pl.ds(queries, block)
        over = pl.ds(keys, count)
        query, given = qt[lines, at], grad[lines, at]
        s = nn(k[over, lanes][:, :HD], query)
        dp = nn(v[over, lanes][:, :HD], given)
        ok = seg_col[over, :1] == seg_row[:, at]
        if masked:
            key = lax.broadcasted_iota(jnp.int32, (count, block), 0)
            place_of = lax.broadcasted_iota(jnp.int32, (count, block), 1) + (count - block)
            ok = ok & (key <= place_of)
        p = jnp.exp2(jnp.where(ok, s, NEG) - lse[h, :, at])
        ds = (p * (dp - row_dot[h, :, at])).astype(BF16)
        return nn(kt[lines, over], ds), nt(query, ds), nt(given, p.astype(BF16))

    def corner(h, base):
        lines = pl.ds(pl.multiple_of(h * HD, UNIT), HD)
        for i in range(middle // block):
            count = (i + 1) * block
            queries = pl.multiple_of(base + i * block, block)
            a, b, c = tile(h, base, count, queries, True)
            dq[lines, pl.ds(queries, block)] += a
            dk[lines, pl.ds(base, count)] += b
            dv[lines, pl.ds(base, count)] += c

    far_base = pl.multiple_of((1 - me // 2) * middle, middle)
    near_base = pl.multiple_of((me // 2) * middle, middle)

    @pl.loop(0, heads)
    def _(h):
        for copy in of_head(h):
            copy.wait()
        lines = pl.ds(pl.multiple_of(h * HD, UNIT), HD)
        row_dot[h] = jnp.sum(grad[lines].astype(F32) * ot[lines].astype(F32), axis=0, keepdims=True)
        nothing = jnp.zeros((HD, middle), F32)
        dq[lines, :middle] = nothing
        dk[lines, middle:] = nothing
        dv[lines, middle:] = nothing
        for i in range(middle // block):
            at = middle + i * block
            a, b, c = tile(h, 0, middle, at, False)
            dq[lines, at : at + block] = a
            dk[lines, :middle] = dk[lines, :middle] + b if i else b
            dv[lines, :middle] = dv[lines, :middle] + c if i else c
        corner(h, far_base)

        @pl.when(h == 0)
        def _():
            met(peers)
            for copy in firsts:
                copy.start()

    for copy in firsts:
        copy.wait()
    half_a[...] = (e_sum[:shared, pl.ds(keep, columns)] + near_a[...].astype(F32)).astype(BF16)
    second.start()

    def ready(x):
        here = pl.ds(place(x, rows), rows)
        for n, (src, factor) in enumerate(((dq, SCORE_SCALE), (dk, 1.0 / LOG2E), (dv, None))):
            value = src[:, here]
            value = (value if factor is None else value * factor).astype(BF16)
            grads[x, n * width : (n + 1) * width] = value
            grads[x, 3 * width + n * rank : 3 * width + (n + 1) * rank] = nn(
                rsel[n * rank : (n + 1) * rank], value
            ).astype(BF16)

    def adapters(x, starts=False):
        load[x].wait()
        here = pl.ds(place(x, rows), rows)
        for n in range(3):
            value = grads[x, n * width : (n + 1) * width]
            part = nt(low[n * rank : (n + 1) * rank, here], value)
            at = slice(n * SLOT, n * SLOT + width)
            raise_sum[:, at] = part if starts else raise_sum[:, at] + part
        part = nn(grads[x, 3 * width :], normed[x])
        lower_sum[...] = part if starts else lower_sum[...] + part

    half = rows // 2

    def through(x, r):
        return tn(grads[x, :, r * half : (r + 1) * half], stack[...])

    pair = [
        [
            send(
                to_near.at[n, pl.ds(r * half, half)], from_near.at[n, pl.ds(r * half, half)],
                g_sent.at[2 * n + r], g_got.at[2 * n + r], across(1),
            )
            for r in range(2)
        ]
        for n in range(2)
    ]
    far = [
        send(to_far.at[c], from_far.at[c], g_sent.at[4 + c], g_got.at[4 + c], across(2))
        for c in range(chunks)
    ]
    raise_sum[...] = jnp.zeros_like(raise_sum)
    ready(3)
    load["stack"].wait()
    for r in range(2):
        to_near[1, r * half : (r + 1) * half] = through(3, r).astype(BF16)
        pair[1][r].start()
    ready(2)
    for r in range(2):
        total = through(2, r)
        pair[1][r].wait()
        for c in range(r * chunks // 2, (r + 1) * chunks // 2):
            here = slice(c * step - r * half, (c + 1) * step - r * half)
            there = slice(c * step, (c + 1) * step)
            to_far[c] = (total[here] + from_near[1, there].astype(F32)).astype(BF16)
            if c < chunks // 2:
                far[c].start()
    sums = (mine_b[0].astype(F32) + theirs_b[0].astype(F32)) + (
        theirs_b[1].astype(F32) + theirs_b[2].astype(F32)
    )
    mark = sel[6 * rank :, : SLOT - width].astype(F32)
    sums = jnp.concatenate([sums[:, : sums.shape[1] - mark.shape[1]], mark], axis=1)
    pack_a[shared : shared + rank] = sums[:, :columns].astype(BF16)
    pack_a[shared + rank :] = sums[:, columns:].astype(BF16)
    second.wait()
    pack_a[:shared] = (half_a[...].astype(F32) + far_a[...].astype(F32)).astype(BF16)
    stays[0].start()
    early.start()
    adapters(3, True)
    adapters(2)

    @pl.loop(0, heads)
    def _(h):
        corner(h, near_base)

    trade = [
        send(src.at[:, pl.ds(0, shared)], dst, e_sent.at[2 + n], e_got.at[2 + n], across(1))
        for n, (src, dst) in enumerate(((first_ref, first_other), (all_ref, other_ref)))
    ]
    ready(1)
    adapters(1)
    ready(0)
    adapters(0)

    whole_b[...] = lower_sum[...].astype(BF16)
    one = to_pair(whole_b, near_b, 0)
    one.start()
    early.pass_all()
    pack_b[shared : shared + rank] = raise_sum[:, :columns].astype(BF16)
    pack_b[shared + rank :] = raise_sum[:, columns:].astype(BF16)
    one.wait()
    half_b[...] = (lower_sum[:, pl.ds(keep, columns)] + near_b[...].astype(F32)).astype(BF16)
    two = send(half_b, far_b, e_sent.at[1], e_got.at[1], across(2))
    two.start()
    for c in range(chunks // 2, chunks):
        far[c].start()
    for r in range(2):
        to_near[0, r * half : (r + 1) * half] = through(1, r).astype(BF16)
        pair[0][r].start()
    two.wait()
    pack_b[:shared] = (half_b[...].astype(F32) + far_b[...].astype(F32)).astype(BF16)
    stays[1].start()
    spread.start()
    for r in range(2):
        ours[r * half : (r + 1) * half] = through(0, r)
    for r in range(2):
        here = slice(r * half, (r + 1) * half)
        pair[0][r].wait()
        ours[here] = ours[here] + from_near[0, here].astype(F32)
    load["x"].wait()
    load["gm"].wait()

    def conclude(c):
        here = slice(c * step, (c + 1) * step)
        far[c].wait()
        x = x_buf[here].astype(F32)
        factor = lax.rsqrt(jnp.mean(x * x, axis=-1, keepdims=True) + EPS)
        unit = x * factor
        grad_in = ours[here] + from_far[c].astype(F32)
        dot = jnp.mean(grad_in * unit, axis=-1, keepdims=True)
        out_ref[here] = (gm_buf[here] + factor * (grad_in - unit * dot)).astype(BF16)

    stays[0].wait()
    early.finish()
    trade[0].start()
    marked = pltpu.make_async_copy(
        first_ref.at[:, pl.ds(4 * rank, rank), pl.ds(columns - LANES, LANES)], marks, last.at[6]
    )
    marked.start()
    conclude(0)
    conclude(1)
    spread.pass_all()
    marked.wait()
    chosen = jnp.max(marks[...].astype(F32), axis=1).astype(jnp.int32)
    chosen_ref[...] = jnp.broadcast_to(chosen[:, LANES - 1 :], chosen.shape)
    conclude(2)
    stays[1].wait()
    spread.finish()
    trade[1].start()
    conclude(3)
    trade[0].wait()
    trade[1].wait()


def backward_call(dp_count, seg_row, sums, sel, low, rsel, columns, rows_of, lse, pieces, stack, x, gm):
    rows, depth = x.shape
    rank, width = rsel.shape[0] // 3, rsel.shape[1]
    heads = width // HD
    length = seg_row.shape[1]
    total = stack.shape[0]
    chunks = 4
    halves = pltpu.VMEM((3 * rank, depth // 2), BF16)
    lines = pltpu.VMEM((chunks, rows // chunks, depth), BF16)
    col = pltpu.VMEM((width, length), BF16)
    row = pltpu.VMEM((length, heads * LANES), BF16)
    total_t = pltpu.VMEM((width, length), F32)
    pack = (5 * rank, depth // 2)
    exchange = [pltpu.VMEM((3 * rank, depth), BF16), halves, halves, halves, pltpu.VMEM(pack, BF16)]
    return pl.pallas_call(
        functools.partial(backward_kernel, heads, dp_count),
        in_specs=[VMEM] * 5 + [ANY] * 14,
        out_specs=[VMEM, ANY, ANY, ANY, ANY, VMEM],
        scratch_shapes=[
            pltpu.VMEM((length, 8), jnp.int32), col, col, col, col, row, row,
            pltpu.VMEM((heads, 1, length), F32),
            pltpu.VMEM((heads, 1, length), F32),
            total_t, total_t, total_t,
            pltpu.VMEM((4, total, rows), BF16),
            pltpu.VMEM((4, rows, depth), BF16),
            pltpu.VMEM((total, depth), BF16),
            pltpu.VMEM((rows, depth), BF16),
            pltpu.VMEM((rows, depth), F32),
            pltpu.VMEM((rows, depth), F32),
            pltpu.VMEM((2, rows, depth), BF16),
            pltpu.VMEM((2, rows, depth), BF16),
            lines, lines,
            pltpu.VMEM((3 * rank, depth), F32),
            pltpu.VMEM((rank, depth), F32),
            *exchange, *exchange,
            pltpu.VMEM((4, rank, depth), BF16),
            pltpu.VMEM((3, rank, depth), BF16),
            pltpu.VMEM((dp_count, rank, LANES), BF16),
            DMA((6, heads)), DMA((4,)), DMA((4 + chunks,)), DMA((4 + chunks,)), DMA((9,)), DMA((9,)),
            DMA((7,)), *Spread.sems(dp_count), *Spread.sems(dp_count),
        ],
        out_shape=[
            jax.ShapeDtypeStruct((rows, depth), BF16),
            jax.ShapeDtypeStruct((dp_count, *pack), BF16),
            jax.ShapeDtypeStruct((dp_count, 3 * rank, depth // 2), BF16),
            jax.ShapeDtypeStruct((dp_count, *pack), BF16),
            jax.ShapeDtypeStruct((dp_count, 3 * rank, depth // 2), BF16),
            jax.ShapeDtypeStruct((dp_count, LANES), jnp.int32),
        ],
        compiler_params=talking(4),
        name="backward",
    )(seg_row, sums, sel, low, rsel, *columns, *rows_of, lse, *pieces, stack, x, gm)


def sets_kernel(
    chosen, first_hbm, first_other_hbm, second_hbm, second_other_hbm, act_in, grad_in, *rest
):
    outs, rest = rest[:12], rest[12:]
    act_out, grad_out, first, first_other, second, second_other, *rest = rest
    sums, (act, grad, loads, stores) = rest[:12], rest[12:]
    bring = [
        pltpu.make_async_copy(src, dst, loads.at[n])
        for n, (src, dst) in enumerate(
            (
                (first_hbm, first), (first_other_hbm, first_other),
                (act_in, act), (grad_in, grad),
                (second_hbm, second), (second_other_hbm, second_other),
            )
        )
    ]
    for copy in bring:
        copy.start()
    leave = [
        pltpu.make_async_copy(src, dst, stores.at[n])
        for n, (src, dst) in enumerate(
            (*zip(sums, outs), (act, act_out), (grad, grad_out))
        )
    ]
    rank = sums[0].shape[1]
    columns = first.shape[2]
    count = first.shape[0]
    parity = lax.rem(lax.axis_index("tensor"), 2)
    here = pl.ds(pl.multiple_of(parity * columns, columns), columns)
    there = pl.ds(pl.multiple_of((1 - parity) * columns, columns), columns)
    for ref in sums:
        ref[...] = jnp.zeros_like(ref)

    def add(group, pack, other):
        @pl.loop(0, count)
        def _(n):
            which = chosen[n, 0]
            for k in range(3):
                part = slice(k * rank, (k + 1) * rank)
                group[k][which, :, here] += pack[n, part].astype(F32)
                group[k][which, :, there] += other[n, part].astype(F32)
            thin = jnp.concatenate(
                [pack[n, 3 * rank : 4 * rank], pack[n, 4 * rank :]], axis=1
            ).astype(F32)
            for k in range(3):
                width = group[3 + k].shape[2]
                group[3 + k][which] += thin[:, k * SLOT : k * SLOT + width]

    bring[0].wait()
    bring[1].wait()
    add(sums[:6], first, first_other)
    for copy in leave[:6]:
        copy.start()
    for n in (0, 1):
        bring[2 + n].wait()
        leave[12 + n].start()
    bring[4].wait()
    bring[5].wait()
    add(sums[6:], second, second_other)
    for copy in leave[6:12]:
        copy.start()
    for copy in leave:
        copy.wait()


def sets_call(chosen, packs, results, sets, width):
    _, five, columns = packs[0].shape
    rank, depth = five // 5, 2 * columns
    full = jax.ShapeDtypeStruct((sets, rank, depth), F32)
    thin = jax.ShapeDtypeStruct((sets, rank, width), F32)
    shapes = [full, full, full, thin, thin, thin] * 2
    lines = [jax.ShapeDtypeStruct(r.shape, r.dtype) for r in results]
    return pl.pallas_call(
        sets_kernel,
        in_specs=[pl.BlockSpec(memory_space=pltpu.SMEM)] + [ANY] * 6,
        out_specs=[ANY] * 14,
        scratch_shapes=[pltpu.VMEM(p.shape, BF16) for p in packs]
        + [pltpu.VMEM(t.shape, t.dtype) for t in shapes + lines]
        + [DMA((6,)), DMA((14,))],
        out_shape=shapes + lines,
        compiler_params=params(),
        name="set_sums",
    )(chosen, *packs, *results)


def on_device(
    dp_count,
    tokens,
    segment_ids,
    adapter_choice,
    cotangent,
    weight_query,
    weight_key,
    weight_value,
    weight_output,
    weight_upward,
    weight_downward,
    query_lower,
    query_raise,
    key_lower,
    key_raise,
    value_lower,
    value_raise,
    output_lower,
    output_raise,
    upward_lower,
    upward_raise,
    downward_lower,
    downward_raise,
):
    x, g = tokens[0], cotangent[0]
    rows = x.shape[0]
    length = segment_ids.shape[1]
    sets = query_lower.shape[0]
    width = query_raise.shape[2]
    seg_row = segment_ids

    feed = (weight_output.T, weight_upward.T, weight_downward.T)
    (
        qt, kt, k, v, low, stack, own, near, far, cross, sel, rsel, w_near, w_far, w_cross, ot, lse, att,
    ) = front_call(
        dp_count,
        adapter_choice,
        x,
        (query_lower, key_lower, value_lower, output_raise, upward_lower, downward_raise),
        (output_lower, upward_raise, downward_lower, query_raise, key_raise, value_raise),
        (weight_query.T, weight_key.T, weight_value.T),
        feed,
        seg_row,
    )
    pieces = (own, near, far, cross)
    act, gm, grad, sums = middle_call(
        x, g, att, pieces, sel, feed, (w_near, w_far, w_cross), length
    )
    input_grad, first, first_other, second, second_other, chosen = backward_call(
        dp_count, seg_row, sums, sel, low, rsel, (qt, kt, ot, grad), (k, v), lse, pieces, stack, x, gm
    )
    *out, act, input_grad = sets_call(
        chosen, (first, first_other, second, second_other), (act, input_grad), sets, width
    )
    (out_raise_g, up_lower_g, down_raise_g, out_lower_g, up_raise_g, down_lower_g) = out[:6]
    (q_lower_g, k_lower_g, v_lower_g, q_raise_g, k_raise_g, v_raise_g) = out[6:12]
    return (
        act[None],
        input_grad[None],
        q_lower_g,
        q_raise_g,
        k_lower_g,
        k_raise_g,
        v_lower_g,
        v_raise_g,
        out_lower_g,
        out_raise_g,
        up_lower_g,
        up_raise_g,
        down_lower_g,
        down_raise_g,
    )


def solution(mesh):
    split = P(None, None, "tensor")
    rows = P("dp", "tensor", None)
    columns = P(None, "tensor")
    return jax.shard_map(
        functools.partial(on_device, mesh.shape["dp"]),
        mesh=mesh,
        in_specs=(rows, P("dp", None), P("dp"), rows)
        + (columns,) * 6
        + (P(), split) * 3
        + (split, P(), P(), split, split, P()),
        out_specs=(rows, rows)
        + (P(), split) * 3
        + (split, P(), P(), split, split, P()),
        check_vma=False,
    )
```

```python
import functools
import math

import jax
import jax.numpy as jnp
from jax import lax
from jax.experimental import pallas as pl
from jax.experimental.pallas import tpu as pltpu
from jax.sharding import PartitionSpec as P

HD = 80
LANES = 128
EPS = 1e-06
NEG = -1e30
F32 = jnp.float32
BF16 = jnp.bfloat16
VMEM_BYTES = 60 * 2**20
SCORE_SCALE = HD ** (-0.5)
LOG2E = math.log2(math.e)
SLOT = 384
UNIT = 16
MESH = pl.DeviceIdType.MESH

NT = (((1,), (1,)), ((), ()))
TN = (((0,), (0,)), ((), ()))


def nn(left, right):
    return jnp.dot(left, right, preferred_element_type=F32)


def nt(left, right):
    return lax.dot_general(left, right, NT, preferred_element_type=F32)


def tn(left, right):
    return lax.dot_general(left, right, TN, preferred_element_type=F32)


def params(**more):
    return pltpu.CompilerParams(vmem_limit_bytes=VMEM_BYTES, **more)


def talking(number):
    return params(collective_id=number, has_side_effects=True)


def whole(shape):
    return pl.BlockSpec(shape, lambda *_: (0,) * len(shape))


ANY = pl.BlockSpec(memory_space=pl.ANY)
VMEM = pl.BlockSpec(memory_space=pltpu.VMEM)
DMA = pltpu.SemaphoreType.DMA


def across(bit):
    return {"tensor": lax.axis_index("tensor") ^ bit}


def along(step, count):
    return {"dp": lax.rem(lax.axis_index("dp") + step, count)}


def hello(peers):
    for peer in peers:
        pl.semaphore_signal(
            pltpu.get_barrier_semaphore(), inc=1, device_id=peer, device_id_type=MESH
        )


def met(peers):
    pl.semaphore_wait(pltpu.get_barrier_semaphore(), len(peers))


def send(src, dst, send_sem, recv_sem, peer):
    return pltpu.make_async_remote_copy(
        src_ref=src, dst_ref=dst, send_sem=send_sem, recv_sem=recv_sem,
        device_id=peer, device_id_type=MESH,
    )


class Spread:
    def __init__(self, count, source, slot, sems):
        me = lax.axis_index("dp")
        sent, got, x_sent, x_got = sems
        self.ring = [{"dp": lax.rem(me + 2 * n, count)} for n in range(1, count // 2)]
        self.partner = {"dp": me + 1 - 2 * lax.rem(me, 2)}
        self.direct = [
            send(source, slot(me), sent.at[n], got.at[n], peer) for n, peer in enumerate(self.ring)
        ]
        self.own = send(source, slot(me), x_sent.at[0], x_got.at[0], self.partner)
        self.onward = []
        for n in range(1, count // 2):
            block = slot(lax.rem(me + count - 2 * n, count))
            self.onward.append(send(block, block, x_sent.at[n], x_got.at[n], self.partner))

    @staticmethod
    def sems(count):
        half = count // 2
        return [DMA((half - 1,)), DMA((half - 1,)), DMA((half,)), DMA((half,))]

    @property
    def peers(self):
        return [self.partner, *self.ring]

    def start(self):
        for copy in self.direct:
            copy.start()
        self.own.start()

    def pass_on(self, n):
        self.direct[n].wait_recv()
        self.onward[n].start()

    def pass_all(self):
        for n in range(len(self.direct)):
            self.pass_on(n)

    def finish(self):
        self.own.wait()
        for copy in self.onward:
            copy.wait()
        for copy in self.direct:
            copy.wait_send()


def place(bit, rows):
    return pl.multiple_of((lax.axis_index("tensor") ^ bit) * rows, rows)


def column_of(seg_row):
    return jnp.broadcast_to(seg_row[...], (8, seg_row.shape[1])).T


def front_kernel(
    heads, dp_count, choice, x_hbm, ql, kl, vl, orr, ul, dr, ol, ur, dl, qr, kr, vr, wq, wk, wv, wo, wu, wd,
    seg_row,
    qt_out, kt_out, k_out, v_out, low_out, stack_out, own_out, near_out, far_out, cross_out,
    sel_out, rsel_out, w_near, w_far_out, w_cross, ot_out, lse_out, att_out,
    x_buf, wide, thin, mine_0, mine_1, fetched_0, fetched_1, own, near, far, cross, stack, sel, rsel,
    qt, kt, vt, k, v, low, w_far, seg_col, acc, top_of, total_of, ot, lse,
    loads, unit_sems, w_sent, w_got, sent, got, local, a_sent, a_got, a_local, s_sent, s_got, *spread_sems,
):
    width = heads * HD
    rank = rsel.shape[0] // 3
    rows = x_buf.shape[0]
    half = rows // 2
    cuts = ((0, half), (half, rows // 4), (half + rows // 4, rows // 4 + rank))
    mine, fetched = (mine_0, mine_1), (fetched_0, fetched_1)
    shares_of = [ref.shape[0] for ref in fetched]
    begins = (0, dp_count * shares_of[0], dp_count * sum(shares_of))
    length = qt.shape[1]
    middle = length // 2
    me = lax.axis_index("dp")

    def slots(pile):
        return lambda n: w_far.at[
            pl.ds(pl.multiple_of(begins[pile] + n * shares_of[pile], UNIT), shares_of[pile])
        ]

    weights = [
        Spread(dp_count, fetched[pile], slots(pile), spread_sems[4 * pile : 4 * pile + 4])
        for pile in range(2)
    ]
    peers = [across(1), across(2), across(3)] + weights[0].peers
    hello(peers)

    per_weight = wo.shape[0] // UNIT

    pieces = []
    for pile in range(2):
        count = shares_of[pile] // UNIT
        for u in range(count):
            number = lax.rem(begins[pile] // UNIT + me * count + u, 3 * per_weight)
            pieces.append((mine[pile].at[pl.ds(u * UNIT, UNIT)], number, unit_sems.at[len(pieces)]))
    for dst, number, sem in pieces:
        for n, w in enumerate((wo, wu, wd)):

            @pl.when(number // per_weight == n)
            def _(dst=dst, number=number, sem=sem, n=n, w=w):
                at = pl.multiple_of((number - n * per_weight) * UNIT, UNIT)
                pltpu.make_async_copy(w.at[pl.ds(at, UNIT)], dst, sem).start()

    lines = [
        pltpu.make_async_copy(
            x_hbm.at[pl.ds(c * half, half)], x_buf.at[pl.ds(c * half, half)], loads.at[c]
        )
        for c in range(2)
    ]
    for copy in lines:
        copy.start()
    thins = [
        pltpu.make_async_copy(ref, thin.at[n], loads.at[2 + n])
        for n, ref in enumerate((ol, ur, dl, qr, kr, vr))
    ]
    wides = [
        pltpu.make_async_copy(ref, wide.at[n], loads.at[8 + n])
        for n, ref in enumerate((ql, kl, vl, orr, ul, dr))
    ]
    squares = [
        pltpu.make_async_copy(ref, stack.at[pl.ds(n * width, width)], loads.at[14 + n])
        for n, ref in enumerate((wq, wk, wv))
    ]
    for copy in (*thins, *wides, *squares):
        copy.start()

    def part(ref, c):
        return ref.at[pl.ds(*cuts[c])]

    parts = range(len(cuts))
    to_far = [send(part(own, c), part(far, c), sent.at[0, c], got.at[0, c], across(2)) for c in parts]
    to_near = [send(part(own, c), part(near, c), sent.at[1, c], got.at[1, c], across(1)) for c in parts]
    on = [send(part(far, c), part(cross, c), sent.at[2, c], got.at[2, c], across(1)) for c in parts]
    shares = [
        send(mine[n], fetched[n], w_sent.at[n], w_got.at[n], across(2)) for n in range(2)
    ]
    which = choice[0]
    for dst, number, sem in pieces:
        pltpu.make_async_copy(wo.at[pl.ds(0, UNIT)], dst, sem).wait()
    met(peers)
    shares[0].start()
    for c in range(2):
        here = slice(c * half, (c + 1) * half)
        lines[c].wait()
        x = x_buf[here].astype(F32)
        factor = lax.rsqrt(jnp.mean(x * x, axis=-1, keepdims=True) + EPS)
        own[here] = (x * factor).astype(BF16)
        if c == 1:
            own[rows:] = jnp.zeros((rank, own.shape[1]), BF16)
            for copy in thins:
                copy.wait()
            for n in range(3):
                own[rows:, n * SLOT : n * SLOT + width] = thin[n, which]
        for n in (0,) if c == 0 else parts[1:]:
            to_far[n].start()
            to_near[n].start()
    shares[1].start()

    pending = []

    def keep(src, dst):
        copy = pltpu.make_async_copy(src, dst, local.at[len(pending)])
        copy.start()
        pending.append(copy)

    keep(own, own_out)
    for copy in wides:
        copy.wait()
    for n in range(6):
        sel[n * rank : (n + 1) * rank] = wide[n, which]
    mark = jnp.full((rank, sel.shape[1]), which, jnp.int32).astype(F32)
    sel[6 * rank :] = mark.astype(BF16)
    keep(sel, sel_out)
    for n in range(3):
        rsel[n * rank : (n + 1) * rank] = thin[3 + n, which]
    keep(rsel, rsel_out)
    stack[3 * width :] = sel[: 3 * rank]
    for copy in squares:
        copy.wait()
    keep(stack, stack_out)

    def project(ref, bit, c):
        first, size = cuts[c][0], min(cuts[c][1], rows - cuts[c][0])
        block = ref[first : first + size]
        out = nt(stack[...], block)
        down = out[3 * width :].astype(BF16)
        here = pl.ds(pl.multiple_of(place(bit, rows) + first, LANES), size)
        low[:, here] = down
        for n, (col, row) in enumerate(((qt, None), (kt, k), (vt, v))):
            low_n = slice(n * rank, (n + 1) * rank)
            value = out[n * width : (n + 1) * width] + tn(rsel[low_n], down[low_n])
            if n == 0:
                value = value * (SCORE_SCALE * LOG2E)
            value = value.astype(BF16)
            col[:, here] = value
            if row is not None:
                for h in range(heads):
                    row[here, h * LANES : h * LANES + HD] = value[h * HD : (h + 1) * HD].T
        for src, dst in ((qt, qt_out), (kt, kt_out), (low, low_out)):
            keep(src.at[:, here], dst.at[:, here])
        for src, dst in ((k, k_out), (v, v_out)):
            keep(src.at[here], dst.at[here])

    seg_col[...] = column_of(seg_row)
    block = rows

    def of_head(h):
        lines = pl.ds(pl.multiple_of(h * HD, UNIT), HD)
        lanes = pl.ds(pl.multiple_of(h * LANES, LANES), LANES)
        return lines, lanes

    def attend(h, keys, count, queries, masked):
        lines, lanes = of_head(h)
        at, over = pl.ds(queries, block), pl.ds(keys, count)
        s = nn(k[over, lanes][:, :HD], qt[lines, at])
        ok = seg_col[over, :1] == seg_row[:, at]
        if masked:
            key = lax.broadcasted_iota(jnp.int32, (count, block), 0)
            ok = ok & (key <= lax.broadcasted_iota(jnp.int32, (count, block), 1) + (count - block))
        s = jnp.where(ok, s, NEG)
        top = jnp.max(s, axis=0, keepdims=True)
        p = jnp.exp2(s - top)
        return top, jnp.sum(p, axis=0, keepdims=True), nn(vt[lines, over], p.astype(BF16))

    def corner(h, base):
        lines, _ = of_head(h)
        for i in range(middle // block):
            queries = pl.multiple_of(base + i * block, block)
            top, total, out = attend(h, base, (i + 1) * block, queries, True)
            top_of[h, :, pl.ds(queries, block)] = top
            total_of[h, :, pl.ds(queries, block)] = total
            acc[lines, pl.ds(queries, block)] = out

    chip = lax.axis_index("tensor") // 2
    far_base = pl.multiple_of((1 - chip) * middle, middle)
    near_base = pl.multiple_of(chip * middle, middle)

    for c in parts:
        project(own, 0, c)
        if c == 0:
            shares[0].wait_recv()
            weights[0].start()
            keep(fetched[0], slots(0)(me))
    for c in parts:
        to_near[c].wait_recv()
        project(near, 1, c)
    keep(near, near_out)

    @pl.loop(0, heads)
    def _(h):
        corner(h, near_base)

    for c in parts:
        to_far[c].wait_recv()
        on[c].start()
        project(far, 2, c)
        on[c].wait_recv()
        project(cross, 3, c)
        if c == 0:
            weights[0].pass_all()
    shares[1].wait_recv()
    weights[1].start()
    keep(far, far_out)
    keep(cross, cross_out)
    keep(fetched[1], slots(1)(me))

    def piece(bit, head):
        src = ot.at[pl.ds(pl.multiple_of(head * HD, UNIT), HD), pl.ds(place(bit, rows), rows)]
        dst = att_out.at[pl.ds(pl.multiple_of(bit * width + head * HD, UNIT), HD)]
        if bit == 0:
            return pltpu.make_async_copy(src, dst, a_local.at[head])
        return send(src, dst, a_sent.at[bit - 1, head], a_got.at[bit - 1, head], across(bit))

    def region(ref, pile):
        return ref.at[pl.ds(begins[pile], begins[pile + 1] - begins[pile])]

    swaps = [
        send(w, w_near.at[pl.ds(n * width, width)], s_sent.at[n], s_got.at[n], across(1))
        for n, w in enumerate((wo, wu, wd))
    ] + [
        send(region(w_far, n), region(w_cross, n), s_sent.at[3 + n], s_got.at[3 + n], across(1))
        for n in range(2)
    ]
    saved = [
        pltpu.make_async_copy(region(w_far, n), region(w_far_out, n), a_local.at[heads + n])
        for n in range(2)
    ]
    for copy in pending:
        copy.wait()
    settled = len(pending)

    @pl.loop(0, heads)
    def _(h):
        lines, _ = of_head(h)
        corner(h, far_base)
        for i in range(middle // block):
            at = pl.ds(middle + i * block, block)
            top, total, out = attend(h, 0, middle, middle + i * block, False)
            before = top_of[h, :, at]
            high = jnp.maximum(before, top)
            left, right = jnp.exp2(before - high), jnp.exp2(top - high)
            top_of[h, :, at] = high
            total_of[h, :, at] = left * total_of[h, :, at] + right * total
            acc[lines, at] = left * acc[lines, at] + right * out
        ot[lines] = (acc[lines] / total_of[h]).astype(BF16)
        lse[h] = top_of[h] + jnp.log2(total_of[h])
        for bit in (2, 3, 1, 0):
            piece(bit, h).start()

        @pl.when(h == 0)
        def _():
            weights[0].finish()
            for copy in swaps[:4]:
                copy.start()
            saved[0].start()

        @pl.when(h == 1)
        def _():
            weights[1].pass_all()

        @pl.when(h == heads - 1)
        def _():
            weights[1].finish()
            swaps[4].start()
            saved[1].start()

    keep(ot, ot_out)
    keep(lse, lse_out)
    for copy in shares:
        copy.wait_send()
    for copy in (*to_far, *to_near, *on):
        copy.wait_send()
    for copy in (*swaps, *saved):
        copy.wait()

    @pl.loop(0, heads)
    def _(h):
        for bit in range(4):
            piece(bit, h).wait()

    for copy in pending[settled:]:
        copy.wait()


def front_call(dp_count, choice, x, wides, thins, weights, feed, seg_row):
    rows, depth = x.shape
    length = seg_row.shape[1]
    sets, rank, width = thins[0].shape
    heads = width // HD
    total = 3 * (width + rank)
    units = max(2, -(-3 * width // (UNIT * dp_count)))
    later = max(1, units // 4)
    shares = [pltpu.VMEM((n * UNIT, depth), BF16) for n in (units - later, later)]
    fetched = (dp_count * units * UNIT, depth)
    block = (rows + rank, depth)
    col, row, down = (width, length), (length, heads * LANES), (3 * rank, length)
    picked, raised = (7 * rank, depth), (3 * rank, width)

    def of(shape, dtype=BF16):
        return jax.ShapeDtypeStruct(shape, dtype)

    statistic = pltpu.VMEM((heads, 1, length), F32)
    return pl.pallas_call(
        functools.partial(front_kernel, heads, dp_count),
        in_specs=[pl.BlockSpec(memory_space=pltpu.SMEM)] + [ANY] * 19 + [VMEM],
        out_specs=[ANY] * 18,
        out_shape=[of(t) for t in (col, col, row, row, down, (total, depth), block, block, block, block)]
        + [of(t) for t in (picked, raised, (3 * width, depth), fetched, fetched, col)]
        + [of((heads, 1, length), F32), of((4 * width, rows))],
        scratch_shapes=[
            pltpu.VMEM((rows, depth), BF16),
            pltpu.VMEM((6, sets, rank, depth), BF16),
            pltpu.VMEM((6, sets, rank, width), BF16),
            *shares,
            *shares,
        ]
        + [pltpu.VMEM(block, BF16)] * 4
        + [pltpu.VMEM(t, BF16) for t in ((total, depth), picked, raised, col, col, col, row, row, down, fetched)]
        + [
            pltpu.VMEM((length, 8), jnp.int32), pltpu.VMEM(col, F32), statistic, statistic,
            pltpu.VMEM(col, BF16), statistic,
            DMA((17,)), DMA((units,)), DMA((2,)), DMA((2,)), DMA((3, 3)), DMA((3, 3)),
            DMA((4 + 12 * 5 + 3 + 2 + 2,)),
            DMA((3, heads)), DMA((3, heads)), DMA((heads + 2,)), DMA((5,)), DMA((5,)),
        ]
        + Spread.sems(dp_count) * 2,
        compiler_params=talking(0),
        name="front",
    )(choice, x, *wides, *thins, *weights, *feed, seg_row)


def own_half(half):
    parity = lax.rem(lax.axis_index("tensor"), 2)
    return pl.multiple_of(parity * half, half), pl.multiple_of((1 - parity) * half, half)


def middle_kernel(
    x_ref, g_ref, att_ref, s0, s1, s2, s3, sel, wo_own, wu_own, wd_own,
    w_near, w_far, w_cross,
    act_ref, gm_ref, grad_out, e_sum,
    wo, wu, wd, ol, ur, dl, gt,
    w_local, g_sent, g_got, g_local,
):
    width = wo_own.shape[0]
    rank = s0.shape[0]
    rows = x_ref.shape[0]
    half = rows // 2
    me = lax.axis_index("tensor")

    peers = [across(1), across(2), across(3)]
    hello(peers)
    weights = []
    for n, (own, dst) in enumerate(((wo_own, wo), (wu_own, wu), (wd_own, wd))):
        here = pl.ds(n * width, width)
        group = [
            pltpu.make_async_copy(src, dst.at[pl.ds(x * width, width)], w_local.at[n, x])
            for x, src in enumerate((own, w_near.at[here], w_far.at[here], w_cross.at[here]))
        ]
        for copy in group:
            copy.start()
        weights.append(group)

    def arrived(n):
        for copy in weights[n]:
            copy.wait()

    smalls = (s0, s1, s2, s3)
    for x, src in enumerate(smalls):
        for slot, dst in enumerate((ol, ur, dl)):
            dst[:, x * width : (x + 1) * width] = src[:, slot * SLOT : slot * SLOT + width].astype(F32)
    out_lower, up_raise, down_lower = (r[...].astype(BF16) for r in (ol, ur, dl))
    out_raise, up_lower, down_raise = (
        sel[n * rank : (n + 1) * rank] for n in (3, 4, 5)
    )

    back = {}
    for r in range(2):
        here = slice(r * half, (r + 1) * half)
        grad = g_ref[here]
        att = att_ref[:, here].astype(F32).T.astype(BF16)
        low_out = nt(att, out_lower).astype(BF16)
        grad_low_down = nt(grad, down_raise).astype(BF16)
        if r == 0:
            arrived(0)
        middle = x_ref[here].astype(F32) + (nn(att, wo[...]) + nn(low_out, out_raise))
        factor = lax.rsqrt(jnp.mean(middle * middle, axis=-1, keepdims=True) + EPS)
        unit = middle * factor
        normed = unit.astype(BF16)
        low_up = nt(normed, up_lower).astype(BF16)
        if r == 0:
            arrived(1)
        preact = nt(normed, wu[...]) + nn(low_up, up_raise)
        sigma = 1.0 / (1.0 + jnp.exp(-preact))
        active = (preact * sigma).astype(BF16)
        if r == 0:
            arrived(2)
        low_down = nt(active, down_lower).astype(BF16)
        grad_act = nt(grad, wd[...]) + nn(grad_low_down, down_lower)
        grad_pre = (grad_act * (sigma * (1.0 + preact * (1.0 - sigma)))).astype(BF16)
        grad_low_up = nt(grad_pre, up_raise).astype(BF16)
        grad_mid = nn(grad_pre, wu[...]) + nn(grad_low_up, up_lower)
        dot = jnp.mean(grad_mid * unit, axis=-1, keepdims=True)
        grad_middle = grad.astype(F32) + factor * (grad_mid - unit * dot)
        gm_ref[here] = grad_middle
        grad_attn = grad_middle.astype(BF16)
        grad_low_out = nt(out_raise, grad_attn).astype(BF16)
        if r == 0:
            met(peers)
        for x in (2, 3, 1, 0):
            value = nt(wo[x * width : (x + 1) * width], grad_attn)
            value = value + tn(smalls[x][:, :width], grad_low_out)
            gt[x, :, here] = value.astype(BF16)
            src = gt.at[x, :, pl.ds(r * half, half)]
            dst = grad_out.at[:, pl.ds(pl.multiple_of(me * rows + r * half, half), half)]
            if x:
                copy = send(src, dst, g_sent.at[x - 1, r], g_got.at[x - 1, r], across(x))
            else:
                copy = pltpu.make_async_copy(src, dst, g_local.at[r])
            copy.start()
            back[x, r] = copy
        act_ref[here] = (middle + (nn(active, wd[...]) + nn(low_down, down_raise))).astype(BF16)
        parts = [
            tn(low_out, grad_attn), tn(grad_low_up, normed), tn(low_down, grad),
            nn(grad_low_out, att), tn(low_up, grad_pre), tn(grad_low_down, active),
        ]
        for n, part in enumerate(parts):
            block = slice(n * rank, (n + 1) * rank)
            e_sum[block] = e_sum[block] + part if r else part

    for copy in back.values():
        copy.wait()


def middle_call(x, g, att, pieces, sel, weights, fetched, length):
    rows, depth = x.shape
    width = weights[0].shape[0]
    rank = sel.shape[0] // 7
    small = pl.BlockSpec((rank, depth), lambda c: (rows // rank, 0))
    square = pltpu.VMEM((4 * width, depth), BF16)
    thin = pltpu.VMEM((rank, depth), F32)
    sums = (6 * rank, depth)
    return pl.pallas_call(
        middle_kernel,
        grid=(1,),
        in_specs=[whole((rows, depth))] * 2 + [whole((4 * width, rows))] + [small] * 4
        + [whole(sel.shape)] + [ANY] * 6,
        out_specs=[whole((rows, depth))] * 2 + [ANY, whole(sums)],
        scratch_shapes=[
            square, square, square, thin, thin, thin,
            pltpu.VMEM((4, width, rows), BF16),
            DMA((3, 4)), DMA((3, 2)), DMA((3, 2)), DMA((2,)),
        ],
        out_shape=[
            jax.ShapeDtypeStruct((rows, depth), BF16),
            jax.ShapeDtypeStruct((rows, depth), F32),
            jax.ShapeDtypeStruct((width, length), BF16),
            jax.ShapeDtypeStruct(sums, F32),
        ],
        compiler_params=talking(3),
        name="feed_forward",
    )(x, g, att, *pieces, sel, *weights, *fetched)


def backward_kernel(
    heads, dp_count, seg_row, e_sum, sel, low, rsel,
    qt_hbm, kt_hbm, ot_hbm, grad_hbm, k_hbm, v_hbm, lse_hbm, p0, p1, p2, p3, stack_hbm, x_hbm, gm_hbm,
    out_ref, first_ref, first_other, all_ref, other_ref, chosen_ref,
    seg_col, qt, kt, ot, grad, k, v, lse, row_dot, dq, dk, dv,
    grads, normed, stack, x_buf, gm_buf, ours, to_near, from_near, to_far, from_far,
    lower_sum, raise_sum, whole_a, near_a, half_a, far_a, pack_a, whole_b, near_b, half_b, far_b, pack_b,
    mine_b, theirs_b, marks,
    head_sems, loads, g_sent, g_got, e_sent, e_got, last, *spread_sems,
):
    rank, width = rsel.shape[0] // 3, rsel.shape[1]
    length = qt.shape[1]
    rows = out_ref.shape[0]
    middle = length // 2
    chunks = from_far.shape[0]
    step = rows // chunks
    block = 256
    shared = 3 * rank
    me = lax.axis_index("tensor")
    mine = lax.axis_index("dp")
    early = Spread(dp_count, pack_a, lambda n: first_ref.at[n], spread_sems[:4])
    spread = Spread(dp_count, pack_b, lambda n: all_ref.at[n], spread_sems[4:])
    peers = [across(1), across(2), across(3)] + spread.peers
    hello(peers)

    def of_head(h):
        lines = pl.ds(pl.multiple_of(h * HD, UNIT), HD)
        lanes = pl.ds(pl.multiple_of(h * LANES, LANES), LANES)
        return [
            pltpu.make_async_copy(src.at[lines], dst.at[lines], head_sems.at[n, h])
            for n, (src, dst) in enumerate(((qt_hbm, qt), (kt_hbm, kt), (ot_hbm, ot), (grad_hbm, grad)))
        ] + [
            pltpu.make_async_copy(src.at[:, lanes], dst.at[:, lanes], head_sems.at[4 + n, h])
            for n, (src, dst) in enumerate(((k_hbm, k), (v_hbm, v)))
        ]

    load = {"lse": pltpu.make_async_copy(lse_hbm, lse, last.at[4])}
    load["lse"].start()

    @pl.loop(0, heads)
    def _(h):
        for copy in of_head(h):
            copy.start()

    for x in range(4):
        load[x] = pltpu.make_async_copy((p0, p1, p2, p3)[x].at[pl.ds(0, rows)], normed.at[x], loads.at[x])
    load["stack"] = pltpu.make_async_copy(stack_hbm, stack, last.at[0])
    load["x"] = pltpu.make_async_copy(x_hbm, x_buf, last.at[1])
    load["gm"] = pltpu.make_async_copy(gm_hbm, gm_buf, last.at[2])
    for key in ("stack", 3, 2, 1, 0, "x", "gm"):
        load[key].start()
    seg_col[...] = column_of(seg_row)
    stays = [
        pltpu.make_async_copy(pack_a, first_ref.at[mine], last.at[5]),
        pltpu.make_async_copy(pack_b, all_ref.at[mine], last.at[3]),
    ]
    columns = half_b.shape[1]
    keep, give = own_half(columns)

    def to_pair(src, dst, n):
        return send(src.at[:, pl.ds(give, columns)], dst, e_sent.at[n], e_got.at[n], across(1))

    whole_a[...] = e_sum[:shared].astype(BF16)
    for x in range(4):
        mine_b[x] = jnp.zeros(mine_b.shape[1:], BF16)
        for slot in range(3):
            part = e_sum[(3 + slot) * rank : (4 + slot) * rank, x * width : (x + 1) * width]
            mine_b[x, :, slot * SLOT : slot * SLOT + width] = part.astype(BF16)
    firsts = [to_pair(whole_a, near_a, 4)] + [
        send(mine_b.at[x], theirs_b.at[x - 1], e_sent.at[5 + x], e_got.at[5 + x], across(x))
        for x in (1, 2, 3)
    ]
    second = send(half_a, far_a, e_sent.at[5], e_got.at[5], across(2))
    load["lse"].wait()

    def tile(h, keys, count, queries, masked):
        lines = pl.ds(pl.multiple_of(h * HD, UNIT), HD)
        lanes = pl.ds(pl.multiple_of(h * LANES, LANES), LANES)
        at = pl.ds(queries, block)
        over = pl.ds(keys, count)
        query, given = qt[lines, at], grad[lines, at]
        s = nn(k[over, lanes][:, :HD], query)
        dp = nn(v[over, lanes][:, :HD], given)
        ok = seg_col[over, :1] == seg_row[:, at]
        if masked:
            key = lax.broadcasted_iota(jnp.int32, (count, block), 0)
            place_of = lax.broadcasted_iota(jnp.int32, (count, block), 1) + (count - block)
            ok = ok & (key <= place_of)
        p = jnp.exp2(jnp.where(ok, s, NEG) - lse[h, :, at])
        ds = (p * (dp - row_dot[h, :, at])).astype(BF16)
        return nn(kt[lines, over], ds), nt(query, ds), nt(given, p.astype(BF16))

    def corner(h, base):
        lines = pl.ds(pl.multiple_of(h * HD, UNIT), HD)
        for i in range(middle // block):
            count = (i + 1) * block
            queries = pl.multiple_of(base + i * block, block)
            a, b, c = tile(h, base, count, queries, True)
            dq[lines, pl.ds(queries, block)] += a
            dk[lines, pl.ds(base, count)] += b
            dv[lines, pl.ds(base, count)] += c

    far_base = pl.multiple_of((1 - me // 2) * middle, middle)
    near_base = pl.multiple_of((me // 2) * middle, middle)

    @pl.loop(0, heads)
    def _(h):
        for copy in of_head(h):
            copy.wait()
        lines = pl.ds(pl.multiple_of(h * HD, UNIT), HD)
        row_dot[h] = jnp.sum(grad[lines].astype(F32) * ot[lines].astype(F32), axis=0, keepdims=True)
        nothing = jnp.zeros((HD, middle), F32)
        dq[lines, :middle] = nothing
        dk[lines, middle:] = nothing
        dv[lines, middle:] = nothing
        for i in range(middle // block):
            at = middle + i * block
            a, b, c = tile(h, 0, middle, at, False)
            dq[lines, at : at + block] = a
            dk[lines, :middle] = dk[lines, :middle] + b if i else b
            dv[lines, :middle] = dv[lines, :middle] + c if i else c
        corner(h, far_base)

        @pl.when(h == 0)
        def _():
            met(peers)
            for copy in firsts:
                copy.start()

    for copy in firsts:
        copy.wait()
    half_a[...] = (e_sum[:shared, pl.ds(keep, columns)] + near_a[...].astype(F32)).astype(BF16)
    second.start()

    def ready(x):
        here = pl.ds(place(x, rows), rows)
        for n, (src, factor) in enumerate(((dq, SCORE_SCALE), (dk, 1.0 / LOG2E), (dv, None))):
            value = src[:, here]
            value = (value if factor is None else value * factor).astype(BF16)
            grads[x, n * width : (n + 1) * width] = value
            grads[x, 3 * width + n * rank : 3 * width + (n + 1) * rank] = nn(
                rsel[n * rank : (n + 1) * rank], value
            ).astype(BF16)

    def adapters(x, starts=False):
        load[x].wait()
        here = pl.ds(place(x, rows), rows)
        for n in range(3):
            value = grads[x, n * width : (n + 1) * width]
            part = nt(low[n * rank : (n + 1) * rank, here], value)
            at = slice(n * SLOT, n * SLOT + width)
            raise_sum[:, at] = part if starts else raise_sum[:, at] + part
        part = nn(grads[x, 3 * width :], normed[x])
        lower_sum[...] = part if starts else lower_sum[...] + part

    half = rows // 2

    def through(x, r):
        return tn(grads[x, :, r * half : (r + 1) * half], stack[...])

    pair = [
        [
            send(
                to_near.at[n, pl.ds(r * half, half)], from_near.at[n, pl.ds(r * half, half)],
                g_sent.at[2 * n + r], g_got.at[2 * n + r], across(1),
            )
            for r in range(2)
        ]
        for n in range(2)
    ]
    far = [
        send(to_far.at[c], from_far.at[c], g_sent.at[4 + c], g_got.at[4 + c], across(2))
        for c in range(chunks)
    ]
    raise_sum[...] = jnp.zeros_like(raise_sum)
    ready(3)
    load["stack"].wait()
    for r in range(2):
        to_near[1, r * half : (r + 1) * half] = through(3, r).astype(BF16)
        pair[1][r].start()
    ready(2)
    for r in range(2):
        total = through(2, r)
        pair[1][r].wait()
        for c in range(r * chunks // 2, (r + 1) * chunks // 2):
            here = slice(c * step - r * half, (c + 1) * step - r * half)
            there = slice(c * step, (c + 1) * step)
            to_far[c] = (total[here] + from_near[1, there].astype(F32)).astype(BF16)
            if c < chunks // 2:
                far[c].start()
    sums = (mine_b[0].astype(F32) + theirs_b[0].astype(F32)) + (
        theirs_b[1].astype(F32) + theirs_b[2].astype(F32)
    )
    mark = sel[6 * rank :, : SLOT - width].astype(F32)
    sums = jnp.concatenate([sums[:, : sums.shape[1] - mark.shape[1]], mark], axis=1)
    pack_a[shared : shared + rank] = sums[:, :columns].astype(BF16)
    pack_a[shared + rank :] = sums[:, columns:].astype(BF16)
    second.wait()
    pack_a[:shared] = (half_a[...].astype(F32) + far_a[...].astype(F32)).astype(BF16)
    stays[0].start()
    early.start()
    adapters(3, True)
    adapters(2)

    @pl.loop(0, heads)
    def _(h):
        corner(h, near_base)

    trade = [
        send(src.at[:, pl.ds(0, shared)], dst, e_sent.at[2 + n], e_got.at[2 + n], across(1))
        for n, (src, dst) in enumerate(((first_ref, first_other), (all_ref, other_ref)))
    ]
    ready(1)
    adapters(1)
    ready(0)
    adapters(0)

    whole_b[...] = lower_sum[...].astype(BF16)
    one = to_pair(whole_b, near_b, 0)
    one.start()
    early.pass_all()
    pack_b[shared : shared + rank] = raise_sum[:, :columns].astype(BF16)
    pack_b[shared + rank :] = raise_sum[:, columns:].astype(BF16)
    one.wait()
    half_b[...] = (lower_sum[:, pl.ds(keep, columns)] + near_b[...].astype(F32)).astype(BF16)
    two = send(half_b, far_b, e_sent.at[1], e_got.at[1], across(2))
    two.start()
    for c in range(chunks // 2, chunks):
        far[c].start()
    for r in range(2):
        to_near[0, r * half : (r + 1) * half] = through(1, r).astype(BF16)
        pair[0][r].start()
    two.wait()
    pack_b[:shared] = (half_b[...].astype(F32) + far_b[...].astype(F32)).astype(BF16)
    stays[1].start()
    spread.start()
    for r in range(2):
        ours[r * half : (r + 1) * half] = through(0, r)
    for r in range(2):
        here = slice(r * half, (r + 1) * half)
        pair[0][r].wait()
        ours[here] = ours[here] + from_near[0, here].astype(F32)
    load["x"].wait()
    load["gm"].wait()

    def conclude(c):
        here = slice(c * step, (c + 1) * step)
        far[c].wait()
        x = x_buf[here].astype(F32)
        factor = lax.rsqrt(jnp.mean(x * x, axis=-1, keepdims=True) + EPS)
        unit = x * factor
        grad_in = ours[here] + from_far[c].astype(F32)
        dot = jnp.mean(grad_in * unit, axis=-1, keepdims=True)
        out_ref[here] = (gm_buf[here] + factor * (grad_in - unit * dot)).astype(BF16)

    stays[0].wait()
    early.finish()
    trade[0].start()
    marked = pltpu.make_async_copy(
        first_ref.at[:, pl.ds(4 * rank, rank), pl.ds(columns - LANES, LANES)], marks, last.at[6]
    )
    marked.start()
    conclude(0)
    conclude(1)
    spread.pass_all()
    marked.wait()
    chosen = jnp.max(marks[...].astype(F32), axis=1).astype(jnp.int32)
    chosen_ref[...] = jnp.broadcast_to(chosen[:, LANES - 1 :], chosen.shape)
    conclude(2)
    stays[1].wait()
    spread.finish()
    trade[1].start()
    conclude(3)
    trade[0].wait()
    trade[1].wait()


def backward_call(dp_count, seg_row, sums, sel, low, rsel, columns, rows_of, lse, pieces, stack, x, gm):
    rows, depth = x.shape
    rank, width = rsel.shape[0] // 3, rsel.shape[1]
    heads = width // HD
    length = seg_row.shape[1]
    total = stack.shape[0]
    chunks = 4
    halves = pltpu.VMEM((3 * rank, depth // 2), BF16)
    lines = pltpu.VMEM((chunks, rows // chunks, depth), BF16)
    col = pltpu.VMEM((width, length), BF16)
    row = pltpu.VMEM((length, heads * LANES), BF16)
    total_t = pltpu.VMEM((width, length), F32)
    pack = (5 * rank, depth // 2)
    exchange = [pltpu.VMEM((3 * rank, depth), BF16), halves, halves, halves, pltpu.VMEM(pack, BF16)]
    return pl.pallas_call(
        functools.partial(backward_kernel, heads, dp_count),
        in_specs=[VMEM] * 5 + [ANY] * 14,
        out_specs=[VMEM, ANY, ANY, ANY, ANY, VMEM],
        scratch_shapes=[
            pltpu.VMEM((length, 8), jnp.int32), col, col, col, col, row, row,
            pltpu.VMEM((heads, 1, length), F32),
            pltpu.VMEM((heads, 1, length), F32),
            total_t, total_t, total_t,
            pltpu.VMEM((4, total, rows), BF16),
            pltpu.VMEM((4, rows, depth), BF16),
            pltpu.VMEM((total, depth), BF16),
            pltpu.VMEM((rows, depth), BF16),
            pltpu.VMEM((rows, depth), F32),
            pltpu.VMEM((rows, depth), F32),
            pltpu.VMEM((2, rows, depth), BF16),
            pltpu.VMEM((2, rows, depth), BF16),
            lines, lines,
            pltpu.VMEM((3 * rank, depth), F32),
            pltpu.VMEM((rank, depth), F32),
            *exchange, *exchange,
            pltpu.VMEM((4, rank, depth), BF16),
            pltpu.VMEM((3, rank, depth), BF16),
            pltpu.VMEM((dp_count, rank, LANES), BF16),
            DMA((6, heads)), DMA((4,)), DMA((4 + chunks,)), DMA((4 + chunks,)), DMA((9,)), DMA((9,)),
            DMA((7,)), *Spread.sems(dp_count), *Spread.sems(dp_count),
        ],
        out_shape=[
            jax.ShapeDtypeStruct((rows, depth), BF16),
            jax.ShapeDtypeStruct((dp_count, *pack), BF16),
            jax.ShapeDtypeStruct((dp_count, 3 * rank, depth // 2), BF16),
            jax.ShapeDtypeStruct((dp_count, *pack), BF16),
            jax.ShapeDtypeStruct((dp_count, 3 * rank, depth // 2), BF16),
            jax.ShapeDtypeStruct((dp_count, LANES), jnp.int32),
        ],
        compiler_params=talking(4),
        name="backward",
    )(seg_row, sums, sel, low, rsel, *columns, *rows_of, lse, *pieces, stack, x, gm)


def sets_kernel(
    chosen, first_hbm, first_other_hbm, second_hbm, second_other_hbm, act_in, grad_in, *rest
):
    outs, rest = rest[:12], rest[12:]
    act_out, grad_out, first, first_other, second, second_other, *rest = rest
    sums, (act, grad, loads, stores) = rest[:12], rest[12:]
    bring = [
        pltpu.make_async_copy(src, dst, loads.at[n])
        for n, (src, dst) in enumerate(
            (
                (first_hbm, first), (first_other_hbm, first_other),
                (act_in, act), (grad_in, grad),
                (second_hbm, second), (second_other_hbm, second_other),
            )
        )
    ]
    for copy in bring:
        copy.start()
    leave = [
        pltpu.make_async_copy(src, dst, stores.at[n])
        for n, (src, dst) in enumerate(
            (*zip(sums, outs), (act, act_out), (grad, grad_out))
        )
    ]
    rank = sums[0].shape[1]
    columns = first.shape[2]
    count = first.shape[0]
    parity = lax.rem(lax.axis_index("tensor"), 2)
    here = pl.ds(pl.multiple_of(parity * columns, columns), columns)
    there = pl.ds(pl.multiple_of((1 - parity) * columns, columns), columns)
    for ref in sums:
        ref[...] = jnp.zeros_like(ref)

    def add(group, pack, other):
        @pl.loop(0, count)
        def _(n):
            which = chosen[n, 0]
            for k in range(3):
                part = slice(k * rank, (k + 1) * rank)
                group[k][which, :, here] += pack[n, part].astype(F32)
                group[k][which, :, there] += other[n, part].astype(F32)
            thin = jnp.concatenate(
                [pack[n, 3 * rank : 4 * rank], pack[n, 4 * rank :]], axis=1
            ).astype(F32)
            for k in range(3):
                width = group[3 + k].shape[2]
                group[3 + k][which] += thin[:, k * SLOT : k * SLOT + width]

    bring[0].wait()
    bring[1].wait()
    add(sums[:6], first, first_other)
    for copy in leave[:6]:
        copy.start()
    for n in (0, 1):
        bring[2 + n].wait()
        leave[12 + n].start()
    bring[4].wait()
    bring[5].wait()
    add(sums[6:], second, second_other)
    for copy in leave[6:12]:
        copy.start()
    for copy in leave:
        copy.wait()


def sets_call(chosen, packs, results, sets, width):
    _, five, columns = packs[0].shape
    rank, depth = five // 5, 2 * columns
    full = jax.ShapeDtypeStruct((sets, rank, depth), F32)
    thin = jax.ShapeDtypeStruct((sets, rank, width), F32)
    shapes = [full, full, full, thin, thin, thin] * 2
    lines = [jax.ShapeDtypeStruct(r.shape, r.dtype) for r in results]
    return pl.pallas_call(
        sets_kernel,
        in_specs=[pl.BlockSpec(memory_space=pltpu.SMEM)] + [ANY] * 6,
        out_specs=[ANY] * 14,
        scratch_shapes=[pltpu.VMEM(p.shape, BF16) for p in packs]
        + [pltpu.VMEM(t.shape, t.dtype) for t in shapes + lines]
        + [DMA((6,)), DMA((14,))],
        out_shape=shapes + lines,
        compiler_params=params(),
        name="set_sums",
    )(chosen, *packs, *results)


def on_device(
    dp_count,
    tokens,
    segment_ids,
    adapter_choice,
    cotangent,
    weight_query,
    weight_key,
    weight_value,
    weight_output,
    weight_upward,
    weight_downward,
    query_lower,
    query_raise,
    key_lower,
    key_raise,
    value_lower,
    value_raise,
    output_lower,
    output_raise,
    upward_lower,
    upward_raise,
    downward_lower,
    downward_raise,
):
    x, g = tokens[0], cotangent[0]
    rows = x.shape[0]
    length = segment_ids.shape[1]
    sets = query_lower.shape[0]
    width = query_raise.shape[2]
    seg_row = segment_ids

    feed = (weight_output.T, weight_upward.T, weight_downward.T)
    (
        qt, kt, k, v, low, stack, own, near, far, cross, sel, rsel, w_near, w_far, w_cross, ot, lse, att,
    ) = front_call(
        dp_count,
        adapter_choice,
        x,
        (query_lower, key_lower, value_lower, output_raise, upward_lower, downward_raise),
        (output_lower, upward_raise, downward_lower, query_raise, key_raise, value_raise),
        (weight_query.T, weight_key.T, weight_value.T),
        feed,
        seg_row,
    )
    pieces = (own, near, far, cross)
    act, gm, grad, sums = middle_call(
        x, g, att, pieces, sel, feed, (w_near, w_far, w_cross), length
    )
    input_grad, first, first_other, second, second_other, chosen = backward_call(
        dp_count, seg_row, sums, sel, low, rsel, (qt, kt, ot, grad), (k, v), lse, pieces, stack, x, gm
    )
    *out, act, input_grad = sets_call(
        chosen, (first, first_other, second, second_other), (act, input_grad), sets, width
    )
    (out_raise_g, up_lower_g, down_raise_g, out_lower_g, up_raise_g, down_lower_g) = out[:6]
    (q_lower_g, k_lower_g, v_lower_g, q_raise_g, k_raise_g, v_raise_g) = out[6:12]
    return (
        act[None],
        input_grad[None],
        q_lower_g,
        q_raise_g,
        k_lower_g,
        k_raise_g,
        v_lower_g,
        v_raise_g,
        out_lower_g,
        out_raise_g,
        up_lower_g,
        up_raise_g,
        down_lower_g,
        down_raise_g,
    )


def solution(mesh):
    split = P(None, None, "tensor")
    rows = P("dp", "tensor", None)
    columns = P(None, "tensor")
    return jax.shard_map(
        functools.partial(on_device, mesh.shape["dp"]),
        mesh=mesh,
        in_specs=(rows, P("dp", None), P("dp"), rows)
        + (columns,) * 6
        + (P(), split) * 3
        + (split, P(), P(), split, split, P()),
        out_specs=(rows, rows)
        + (P(), split) * 3
        + (split, P(), P(), split, split, P()),
        check_vma=False,
    )
```

```python
import functools
import math

import jax
import jax.numpy as jnp
from jax import lax
from jax.experimental import pallas as pl
from jax.experimental.pallas import tpu as pltpu
from jax.sharding import PartitionSpec as P

HD = 80
LANES = 128
EPS = 1e-06
NEG = -1e30
F32 = jnp.float32
BF16 = jnp.bfloat16
VMEM_BYTES = 60 * 2**20
SCORE_SCALE = HD ** (-0.5)
LOG2E = math.log2(math.e)
SLOT = 384
UNIT = 16
MESH = pl.DeviceIdType.MESH

NT = (((1,), (1,)), ((), ()))
TN = (((0,), (0,)), ((), ()))


def nn(left, right):
    return jnp.dot(left, right, preferred_element_type=F32)


def nt(left, right):
    return lax.dot_general(left, right, NT, preferred_element_type=F32)


def tn(left, right):
    return lax.dot_general(left, right, TN, preferred_element_type=F32)


def params(**more):
    return pltpu.CompilerParams(vmem_limit_bytes=VMEM_BYTES, **more)


def talking(number):
    return params(collective_id=number, has_side_effects=True)


def whole(shape):
    return pl.BlockSpec(shape, lambda *_: (0,) * len(shape))


ANY = pl.BlockSpec(memory_space=pl.ANY)
VMEM = pl.BlockSpec(memory_space=pltpu.VMEM)
DMA = pltpu.SemaphoreType.DMA


def across(bit):
    return {"tensor": lax.axis_index("tensor") ^ bit}


def along(step, count):
    return {"dp": lax.rem(lax.axis_index("dp") + step, count)}


def hello(peers):
    for peer in peers:
        pl.semaphore_signal(
            pltpu.get_barrier_semaphore(), inc=1, device_id=peer, device_id_type=MESH
        )


def met(peers):
    pl.semaphore_wait(pltpu.get_barrier_semaphore(), len(peers))


def send(src, dst, send_sem, recv_sem, peer):
    return pltpu.make_async_remote_copy(
        src_ref=src, dst_ref=dst, send_sem=send_sem, recv_sem=recv_sem,
        device_id=peer, device_id_type=MESH,
    )


class Spread:
    def __init__(self, count, source, slot, sems):
        me = lax.axis_index("dp")
        sent, got, x_sent, x_got = sems
        self.ring = [{"dp": lax.rem(me + 2 * n, count)} for n in range(1, count // 2)]
        self.partner = {"dp": me + 1 - 2 * lax.rem(me, 2)}
        self.direct = [
            send(source, slot(me), sent.at[n], got.at[n], peer) for n, peer in enumerate(self.ring)
        ]
        self.own = send(source, slot(me), x_sent.at[0], x_got.at[0], self.partner)
        self.onward = []
        for n in range(1, count // 2):
            block = slot(lax.rem(me + count - 2 * n, count))
            self.onward.append(send(block, block, x_sent.at[n], x_got.at[n], self.partner))

    @staticmethod
    def sems(count):
        half = count // 2
        return [DMA((half - 1,)), DMA((half - 1,)), DMA((half,)), DMA((half,))]

    @property
    def peers(self):
        return [self.partner, *self.ring]

    def start(self):
        for copy in self.direct:
            copy.start()
        self.own.start()

    def pass_on(self, n):
        self.direct[n].wait_recv()
        self.onward[n].start()

    def pass_all(self):
        for n in range(len(self.direct)):
            self.pass_on(n)

    def finish(self):
        self.own.wait()
        for copy in self.onward:
            copy.wait()
        for copy in self.direct:
            copy.wait_send()


def place(bit, rows):
    return pl.multiple_of((lax.axis_index("tensor") ^ bit) * rows, rows)


def column_of(seg_row):
    return jnp.broadcast_to(seg_row[...], (8, seg_row.shape[1])).T


def front_kernel(
    heads, dp_count, choice, x_hbm, ql, kl, vl, orr, ul, dr, ol, ur, dl, qr, kr, vr, wq, wk, wv, wo, wu, wd,
    seg_row,
    qt_out, kt_out, k_out, v_out, low_out, stack_out, own_out, near_out, far_out, cross_out,
    sel_out, rsel_out, w_near, w_far_out, w_cross, ot_out, lse_out, att_out,
    x_buf, wide, thin, mine_0, mine_1, fetched_0, fetched_1, own, near, far, cross, stack, sel, rsel,
    qt, kt, vt, k, v, low, w_far, seg_col, acc, top_of, total_of, ot, lse,
    loads, unit_sems, w_sent, w_got, sent, got, local, a_sent, a_got, a_local, s_sent, s_got, *spread_sems,
):
    width = heads * HD
    rank = rsel.shape[0] // 3
    rows = x_buf.shape[0]
    half = rows // 2
    cuts = ((0, half), (half, rows // 4), (half + rows // 4, rows // 4 + rank))
    mine, fetched = (mine_0, mine_1), (fetched_0, fetched_1)
    shares_of = [ref.shape[0] for ref in fetched]
    begins = (0, dp_count * shares_of[0], dp_count * sum(shares_of))
    length = qt.shape[1]
    middle = length // 2
    me = lax.axis_index("dp")

    def slots(pile):
        return lambda n: w_far.at[
            pl.ds(pl.multiple_of(begins[pile] + n * shares_of[pile], UNIT), shares_of[pile])
        ]

    weights = [
        Spread(dp_count, fetched[pile], slots(pile), spread_sems[4 * pile : 4 * pile + 4])
        for pile in range(2)
    ]
    peers = [across(1), across(2), across(3)] + weights[0].peers
    hello(peers)

    per_weight = wo.shape[0] // UNIT

    pieces = []
    for pile in range(2):
        count = shares_of[pile] // UNIT
        for u in range(count):
            number = lax.rem(begins[pile] // UNIT + me * count + u, 3 * per_weight)
            pieces.append((mine[pile].at[pl.ds(u * UNIT, UNIT)], number, unit_sems.at[len(pieces)]))
    for dst, number, sem in pieces:
        for n, w in enumerate((wo, wu, wd)):

            @pl.when(number // per_weight == n)
            def _(dst=dst, number=number, sem=sem, n=n, w=w):
                at = pl.multiple_of((number - n * per_weight) * UNIT, UNIT)
                pltpu.make_async_copy(w.at[pl.ds(at, UNIT)], dst, sem).start()

    lines = [
        pltpu.make_async_copy(
            x_hbm.at[pl.ds(c * half, half)], x_buf.at[pl.ds(c * half, half)], loads.at[c]
        )
        for c in range(2)
    ]
    for copy in lines:
        copy.start()
    thins = [
        pltpu.make_async_copy(ref, thin.at[n], loads.at[2 + n])
        for n, ref in enumerate((ol, ur, dl, qr, kr, vr))
    ]
    wides = [
        pltpu.make_async_copy(ref, wide.at[n], loads.at[8 + n])
        for n, ref in enumerate((ql, kl, vl, orr, ul, dr))
    ]
    squares = [
        pltpu.make_async_copy(ref, stack.at[pl.ds(n * width, width)], loads.at[14 + n])
        for n, ref in enumerate((wq, wk, wv))
    ]
    for copy in (*thins, *wides, *squares):
        copy.start()

    def part(ref, c):
        return ref.at[pl.ds(*cuts[c])]

    parts = range(len(cuts))
    to_far = [send(part(own, c), part(far, c), sent.at[0, c], got.at[0, c], across(2)) for c in parts]
    to_near = [send(part(own, c), part(near, c), sent.at[1, c], got.at[1, c], across(1)) for c in parts]
    on = [send(part(far, c), part(cross, c), sent.at[2, c], got.at[2, c], across(1)) for c in parts]
    shares = [
        send(mine[n], fetched[n], w_sent.at[n], w_got.at[n], across(2)) for n in range(2)
    ]
    which = choice[0]
    for dst, number, sem in pieces:
        pltpu.make_async_copy(wo.at[pl.ds(0, UNIT)], dst, sem).wait()
    met(peers)
    shares[0].start()
    for c in range(2):
        here = slice(c * half, (c + 1) * half)
        lines[c].wait()
        x = x_buf[here].astype(F32)
        factor = lax.rsqrt(jnp.mean(x * x, axis=-1, keepdims=True) + EPS)
        own[here] = (x * factor).astype(BF16)
        if c == 1:
            own[rows:] = jnp.zeros((rank, own.shape[1]), BF16)
            for copy in thins:
                copy.wait()
            for n in range(3):
                own[rows:, n * SLOT : n * SLOT + width] = thin[n, which]
        for n in (0,) if c == 0 else parts[1:]:
            to_far[n].start()
            to_near[n].start()
    shares[1].start()

    pending = []

    def keep(src, dst):
        copy = pltpu.make_async_copy(src, dst, local.at[len(pending)])
        copy.start()
        pending.append(copy)

    keep(own, own_out)
    for copy in wides:
        copy.wait()
    for n in range(6):
        sel[n * rank : (n + 1) * rank] = wide[n, which]
    mark = jnp.full((rank, sel.shape[1]), which, jnp.int32).astype(F32)
    sel[6 * rank :] = mark.astype(BF16)
    keep(sel, sel_out)
    for n in range(3):
        rsel[n * rank : (n + 1) * rank] = thin[3 + n, which]
    keep(rsel, rsel_out)
    stack[3 * width :] = sel[: 3 * rank]
    for copy in squares:
        copy.wait()
    keep(stack, stack_out)

    def project(ref, bit, c):
        first, size = cuts[c][0], min(cuts[c][1], rows - cuts[c][0])
        block = ref[first : first + size]
        out = nt(stack[...], block)
        down = out[3 * width :].astype(BF16)
        here = pl.ds(pl.multiple_of(place(bit, rows) + first, LANES), size)
        low[:, here] = down
        for n, (col, row) in enumerate(((qt, None), (kt, k), (vt, v))):
            low_n = slice(n * rank, (n + 1) * rank)
            value = out[n * width : (n + 1) * width] + tn(rsel[low_n], down[low_n])
            if n == 0:
                value = value * (SCORE_SCALE * LOG2E)
            value = value.astype(BF16)
            col[:, here] = value
            if row is not None:
                for h in range(heads):
                    row[here, h * LANES : h * LANES + HD] = value[h * HD : (h + 1) * HD].T
        for src, dst in ((qt, qt_out), (kt, kt_out), (low, low_out)):
            keep(src.at[:, here], dst.at[:, here])
        for src, dst in ((k, k_out), (v, v_out)):
            keep(src.at[here], dst.at[here])

    seg_col[...] = column_of(seg_row)
    block = rows

    def of_head(h):
        lines = pl.ds(pl.multiple_of(h * HD, UNIT), HD)
        lanes = pl.ds(pl.multiple_of(h * LANES, LANES), LANES)
        return lines, lanes

    def attend(h, keys, count, queries, masked):
        lines, lanes = of_head(h)
        at, over = pl.ds(queries, block), pl.ds(keys, count)
        s = nn(k[over, lanes][:, :HD], qt[lines, at])
        ok = seg_col[over, :1] == seg_row[:, at]
        if masked:
            key = lax.broadcasted_iota(jnp.int32, (count, block), 0)
            ok = ok & (key <= lax.broadcasted_iota(jnp.int32, (count, block), 1) + (count - block))
        s = jnp.where(ok, s, NEG)
        top = jnp.max(s, axis=0, keepdims=True)
        p = jnp.exp2(s - top)
        return top, jnp.sum(p, axis=0, keepdims=True), nn(vt[lines, over], p.astype(BF16))

    def corner(h, base):
        lines, _ = of_head(h)
        for i in range(middle // block):
            queries = pl.multiple_of(base + i * block, block)
            top, total, out = attend(h, base, (i + 1) * block, queries, True)
            top_of[h, :, pl.ds(queries, block)] = top
            total_of[h, :, pl.ds(queries, block)] = total
            acc[lines, pl.ds(queries, block)] = out

    chip = lax.axis_index("tensor") // 2
    far_base = pl.multiple_of((1 - chip) * middle, middle)
    near_base = pl.multiple_of(chip * middle, middle)

    for c in parts:
        project(own, 0, c)
        if c == 0:
            shares[0].wait_recv()
            weights[0].start()
            keep(fetched[0], slots(0)(me))
    for c in parts:
        to_near[c].wait_recv()
        project(near, 1, c)
    keep(near, near_out)

    @pl.loop(0, heads)
    def _(h):
        corner(h, near_base)

    for c in parts:
        to_far[c].wait_recv()
        on[c].start()
        project(far, 2, c)
        on[c].wait_recv()
        project(cross, 3, c)
        if c == 0:
            weights[0].pass_all()
    shares[1].wait_recv()
    weights[1].start()
    keep(far, far_out)
    keep(cross, cross_out)
    keep(fetched[1], slots(1)(me))

    def piece(bit, head):
        src = ot.at[pl.ds(pl.multiple_of(head * HD, UNIT), HD), pl.ds(place(bit, rows), rows)]
        dst = att_out.at[pl.ds(pl.multiple_of(bit * width + head * HD, UNIT), HD)]
        if bit == 0:
            return pltpu.make_async_copy(src, dst, a_local.at[head])
        return send(src, dst, a_sent.at[bit - 1, head], a_got.at[bit - 1, head], across(bit))

    def region(ref, pile):
        return ref.at[pl.ds(begins[pile], begins[pile + 1] - begins[pile])]

    swaps = [
        send(w, w_near.at[pl.ds(n * width, width)], s_sent.at[n], s_got.at[n], across(1))
        for n, w in enumerate((wo, wu, wd))
    ] + [
        send(region(w_far, n), region(w_cross, n), s_sent.at[3 + n], s_got.at[3 + n], across(1))
        for n in range(2)
    ]
    saved = [
        pltpu.make_async_copy(region(w_far, n), region(w_far_out, n), a_local.at[heads + n])
        for n in range(2)
    ]
    for copy in pending:
        copy.wait()
    settled = len(pending)

    @pl.loop(0, heads)
    def _(h):
        lines, _ = of_head(h)
        corner(h, far_base)
        for i in range(middle // block):
            at = pl.ds(middle + i * block, block)
            top, total, out = attend(h, 0, middle, middle + i * block, False)
            before = top_of[h, :, at]
            high = jnp.maximum(before, top)
            left, right = jnp.exp2(before - high), jnp.exp2(top - high)
            top_of[h, :, at] = high
            total_of[h, :, at] = left * total_of[h, :, at] + right * total
            acc[lines, at] = left * acc[lines, at] + right * out
        ot[lines] = (acc[lines] / total_of[h]).astype(BF16)
        lse[h] = top_of[h] + jnp.log2(total_of[h])
        for bit in (2, 3, 1, 0):
            piece(bit, h).start()

        @pl.when(h == 0)
        def _():
            weights[0].finish()
            for copy in swaps[:4]:
                copy.start()
            saved[0].start()

        @pl.when(h == 1)
        def _():
            weights[1].pass_all()

        @pl.when(h == heads - 1)
        def _():
            weights[1].finish()
            swaps[4].start()
            saved[1].start()

    keep(ot, ot_out)
    keep(lse, lse_out)
    for copy in shares:
        copy.wait_send()
    for copy in (*to_far, *to_near, *on):
        copy.wait_send()
    for copy in (*swaps, *saved):
        copy.wait()

    @pl.loop(0, heads)
    def _(h):
        for bit in range(4):
            piece(bit, h).wait()

    for copy in pending[settled:]:
        copy.wait()


def front_call(dp_count, choice, x, wides, thins, weights, feed, seg_row):
    rows, depth = x.shape
    length = seg_row.shape[1]
    sets, rank, width = thins[0].shape
    heads = width // HD
    total = 3 * (width + rank)
    units = max(2, -(-3 * width // (UNIT * dp_count)))
    later = max(1, units // 4)
    shares = [pltpu.VMEM((n * UNIT, depth), BF16) for n in (units - later, later)]
    fetched = (dp_count * units * UNIT, depth)
    block = (rows + rank, depth)
    col, row, down = (width, length), (length, heads * LANES), (3 * rank, length)
    picked, raised = (7 * rank, depth), (3 * rank, width)

    def of(shape, dtype=BF16):
        return jax.ShapeDtypeStruct(shape, dtype)

    statistic = pltpu.VMEM((heads, 1, length), F32)
    return pl.pallas_call(
        functools.partial(front_kernel, heads, dp_count),
        in_specs=[pl.BlockSpec(memory_space=pltpu.SMEM)] + [ANY] * 19 + [VMEM],
        out_specs=[ANY] * 18,
        out_shape=[of(t) for t in (col, col, row, row, down, (total, depth), block, block, block, block)]
        + [of(t) for t in (picked, raised, (3 * width, depth), fetched, fetched, col)]
        + [of((heads, 1, length), F32), of((4 * width, rows))],
        scratch_shapes=[
            pltpu.VMEM((rows, depth), BF16),
            pltpu.VMEM((6, sets, rank, depth), BF16),
            pltpu.VMEM((6, sets, rank, width), BF16),
            *shares,
            *shares,
        ]
        + [pltpu.VMEM(block, BF16)] * 4
        + [pltpu.VMEM(t, BF16) for t in ((total, depth), picked, raised, col, col, col, row, row, down, fetched)]
        + [
            pltpu.VMEM((length, 8), jnp.int32), pltpu.VMEM(col, F32), statistic, statistic,
            pltpu.VMEM(col, BF16), statistic,
            DMA((17,)), DMA((units,)), DMA((2,)), DMA((2,)), DMA((3, 3)), DMA((3, 3)),
            DMA((4 + 12 * 5 + 3 + 2 + 2,)),
            DMA((3, heads)), DMA((3, heads)), DMA((heads + 2,)), DMA((5,)), DMA((5,)),
        ]
        + Spread.sems(dp_count) * 2,
        compiler_params=talking(0),
        name="front",
    )(choice, x, *wides, *thins, *weights, *feed, seg_row)


def own_half(half):
    parity = lax.rem(lax.axis_index("tensor"), 2)
    return pl.multiple_of(parity * half, half), pl.multiple_of((1 - parity) * half, half)


def middle_kernel(
    x_ref, g_ref, att_ref, s0, s1, s2, s3, sel, wo_own, wu_own, wd_own,
    w_near, w_far, w_cross,
    act_ref, gm_ref, grad_out, e_sum,
    wo, wu, wd, ol, ur, dl, gt,
    w_local, g_sent, g_got, g_local,
):
    width = wo_own.shape[0]
    rank = s0.shape[0]
    rows = x_ref.shape[0]
    half = rows // 2
    me = lax.axis_index("tensor")

    peers = [across(1), across(2), across(3)]
    hello(peers)
    weights = []
    for n, (own, dst) in enumerate(((wo_own, wo), (wu_own, wu), (wd_own, wd))):
        here = pl.ds(n * width, width)
        group = [
            pltpu.make_async_copy(src, dst.at[pl.ds(x * width, width)], w_local.at[n, x])
            for x, src in enumerate((own, w_near.at[here], w_far.at[here], w_cross.at[here]))
        ]
        for copy in group:
            copy.start()
        weights.append(group)

    def arrived(n):
        for copy in weights[n]:
            copy.wait()

    smalls = (s0, s1, s2, s3)
    for x, src in enumerate(smalls):
        for slot, dst in enumerate((ol, ur, dl)):
            dst[:, x * width : (x + 1) * width] = src[:, slot * SLOT : slot * SLOT + width].astype(F32)
    out_lower, up_raise, down_lower = (r[...].astype(BF16) for r in (ol, ur, dl))
    out_raise, up_lower, down_raise = (
        sel[n * rank : (n + 1) * rank] for n in (3, 4, 5)
    )

    back = {}
    for r in range(2):
        here = slice(r * half, (r + 1) * half)
        grad = g_ref[here]
        att = att_ref[:, here].astype(F32).T.astype(BF16)
        low_out = nt(att, out_lower).astype(BF16)
        grad_low_down = nt(grad, down_raise).astype(BF16)
        if r == 0:
            arrived(0)
        middle = x_ref[here].astype(F32) + (nn(att, wo[...]) + nn(low_out, out_raise))
        factor = lax.rsqrt(jnp.mean(middle * middle, axis=-1, keepdims=True) + EPS)
        unit = middle * factor
        normed = unit.astype(BF16)
        low_up = nt(normed, up_lower).astype(BF16)
        if r == 0:
            arrived(1)
        preact = nt(normed, wu[...]) + nn(low_up, up_raise)
        sigma = 1.0 / (1.0 + jnp.exp(-preact))
        active = (preact * sigma).astype(BF16)
        if r == 0:
            arrived(2)
        low_down = nt(active, down_lower).astype(BF16)
        grad_act = nt(grad, wd[...]) + nn(grad_low_down, down_lower)
        grad_pre = (grad_act * (sigma * (1.0 + preact * (1.0 - sigma)))).astype(BF16)
        grad_low_up = nt(grad_pre, up_raise).astype(BF16)
        grad_mid = nn(grad_pre, wu[...]) + nn(grad_low_up, up_lower)
        dot = jnp.mean(grad_mid * unit, axis=-1, keepdims=True)
        grad_middle = grad.astype(F32) + factor * (grad_mid - unit * dot)
        gm_ref[here] = grad_middle
        grad_attn = grad_middle.astype(BF16)
        grad_low_out = nt(out_raise, grad_attn).astype(BF16)
        if r == 0:
            met(peers)
        for x in (2, 3, 1, 0):
            value = nt(wo[x * width : (x + 1) * width], grad_attn)
            value = value + tn(smalls[x][:, :width], grad_low_out)
            gt[x, :, here] = value.astype(BF16)
            src = gt.at[x, :, pl.ds(r * half, half)]
            dst = grad_out.at[:, pl.ds(pl.multiple_of(me * rows + r * half, half), half)]
            if x:
                copy = send(src, dst, g_sent.at[x - 1, r], g_got.at[x - 1, r], across(x))
            else:
                copy = pltpu.make_async_copy(src, dst, g_local.at[r])
            copy.start()
            back[x, r] = copy
        act_ref[here] = (middle + (nn(active, wd[...]) + nn(low_down, down_raise))).astype(BF16)
        parts = [
            tn(low_out, grad_attn), tn(grad_low_up, normed), tn(low_down, grad),
            nn(grad_low_out, att), tn(low_up, grad_pre), tn(grad_low_down, active),
        ]
        for n, part in enumerate(parts):
            block = slice(n * rank, (n + 1) * rank)
            e_sum[block] = e_sum[block] + part if r else part

    for copy in back.values():
        copy.wait()


def middle_call(x, g, att, pieces, sel, weights, fetched, length):
    rows, depth = x.shape
    width = weights[0].shape[0]
    rank = sel.shape[0] // 7
    small = pl.BlockSpec((rank, depth), lambda c: (rows // rank, 0))
    square = pltpu.VMEM((4 * width, depth), BF16)
    thin = pltpu.VMEM((rank, depth), F32)
    sums = (6 * rank, depth)
    return pl.pallas_call(
        middle_kernel,
        grid=(1,),
        in_specs=[whole((rows, depth))] * 2 + [whole((4 * width, rows))] + [small] * 4
        + [whole(sel.shape)] + [ANY] * 6,
        out_specs=[whole((rows, depth))] * 2 + [ANY, whole(sums)],
        scratch_shapes=[
            square, square, square, thin, thin, thin,
            pltpu.VMEM((4, width, rows), BF16),
            DMA((3, 4)), DMA((3, 2)), DMA((3, 2)), DMA((2,)),
        ],
        out_shape=[
            jax.ShapeDtypeStruct((rows, depth), BF16),
            jax.ShapeDtypeStruct((rows, depth), F32),
            jax.ShapeDtypeStruct((width, length), BF16),
            jax.ShapeDtypeStruct(sums, F32),
        ],
        compiler_params=talking(3),
        name="feed_forward",
    )(x, g, att, *pieces, sel, *weights, *fetched)


def backward_kernel(
    heads, dp_count, seg_row, e_sum, sel, low, rsel,
    qt_hbm, kt_hbm, ot_hbm, grad_hbm, k_hbm, v_hbm, lse_hbm, p0, p1, p2, p3, stack_hbm, x_hbm, gm_hbm,
    out_ref, first_ref, first_other, all_ref, other_ref, chosen_ref,
    seg_col, qt, kt, ot, grad, k, v, lse, row_dot, dq, dk, dv,
    grads, normed, stack, x_buf, gm_buf, ours, to_near, from_near, to_far, from_far,
    lower_sum, raise_sum, whole_a, near_a, half_a, far_a, pack_a, whole_b, near_b, half_b, far_b, pack_b,
    mine_b, theirs_b, marks,
    head_sems, loads, g_sent, g_got, e_sent, e_got, last, *spread_sems,
):
    rank, width = rsel.shape[0] // 3, rsel.shape[1]
    length = qt.shape[1]
    rows = out_ref.shape[0]
    middle = length // 2
    chunks = from_far.shape[0]
    step = rows // chunks
    block = 256
    shared = 3 * rank
    me = lax.axis_index("tensor")
    mine = lax.axis_index("dp")
    early = Spread(dp_count, pack_a, lambda n: first_ref.at[n], spread_sems[:4])
    upper, under = pl.ds(0, shared), pl.ds(shared, 2 * rank)
    spread = Spread(dp_count, pack_b.at[upper], lambda n: all_ref.at[n, upper], spread_sems[4:8])
    ahead = Spread(dp_count, pack_b.at[under], lambda n: all_ref.at[n, under], spread_sems[8:])
    peers = [across(1), across(2), across(3)] + spread.peers
    hello(peers)

    def of_head(h):
        lines = pl.ds(pl.multiple_of(h * HD, UNIT), HD)
        lanes = pl.ds(pl.multiple_of(h * LANES, LANES), LANES)
        return [
            pltpu.make_async_copy(src.at[lines], dst.at[lines], head_sems.at[n, h])
            for n, (src, dst) in enumerate(((qt_hbm, qt), (kt_hbm, kt), (ot_hbm, ot), (grad_hbm, grad)))
        ] + [
            pltpu.make_async_copy(src.at[:, lanes], dst.at[:, lanes], head_sems.at[4 + n, h])
            for n, (src, dst) in enumerate(((k_hbm, k), (v_hbm, v)))
        ]

    load = {"lse": pltpu.make_async_copy(lse_hbm, lse, last.at[4])}
    load["lse"].start()

    for copy in of_head(0):
        copy.start()
    for x in range(4):
        load[x] = pltpu.make_async_copy((p0, p1, p2, p3)[x].at[pl.ds(0, rows)], normed.at[x], loads.at[x])
    load["stack"] = pltpu.make_async_copy(stack_hbm, stack, last.at[0])
    load["x"] = pltpu.make_async_copy(x_hbm, x_buf, last.at[1])
    load["gm"] = pltpu.make_async_copy(gm_hbm, gm_buf, last.at[2])
    seg_col[...] = column_of(seg_row)
    stays = [
        pltpu.make_async_copy(pack_a, first_ref.at[mine], last.at[5]),
        pltpu.make_async_copy(pack_b, all_ref.at[mine], last.at[3]),
    ]
    columns = half_b.shape[1]
    keep, give = own_half(columns)

    def to_pair(src, dst, n):
        return send(src.at[:, pl.ds(give, columns)], dst, e_sent.at[n], e_got.at[n], across(1))

    whole_a[...] = e_sum[:shared].astype(BF16)
    for x in range(4):
        mine_b[x] = jnp.zeros(mine_b.shape[1:], BF16)
        for slot in range(3):
            part = e_sum[(3 + slot) * rank : (4 + slot) * rank, x * width : (x + 1) * width]
            mine_b[x, :, slot * SLOT : slot * SLOT + width] = part.astype(BF16)
    firsts = [to_pair(whole_a, near_a, 4)] + [
        send(mine_b.at[x], theirs_b.at[x - 1], e_sent.at[5 + x], e_got.at[5 + x], across(x))
        for x in (1, 2, 3)
    ]
    second = send(half_a, far_a, e_sent.at[5], e_got.at[5], across(2))
    load["lse"].wait()

    def tile(h, keys, count, queries, masked):
        lines = pl.ds(pl.multiple_of(h * HD, UNIT), HD)
        lanes = pl.ds(pl.multiple_of(h * LANES, LANES), LANES)
        at = pl.ds(queries, block)
        over = pl.ds(keys, count)
        query, given = qt[lines, at], grad[lines, at]
        s = nn(k[over, lanes][:, :HD], query)
        dp = nn(v[over, lanes][:, :HD], given)
        ok = seg_col[over, :1] == seg_row[:, at]
        if masked:
            key = lax.broadcasted_iota(jnp.int32, (count, block), 0)
            place_of = lax.broadcasted_iota(jnp.int32, (count, block), 1) + (count - block)
            ok = ok & (key <= place_of)
        p = jnp.exp2(jnp.where(ok, s, NEG) - lse[h, :, at])
        ds = (p * (dp - row_dot[h, :, at])).astype(BF16)
        return nn(kt[lines, over], ds), nt(query, ds), nt(given, p.astype(BF16))

    def corner(h, base):
        lines = pl.ds(pl.multiple_of(h * HD, UNIT), HD)
        for i in range(middle // block):
            count = (i + 1) * block
            queries = pl.multiple_of(base + i * block, block)
            a, b, c = tile(h, base, count, queries, True)
            dq[lines, pl.ds(queries, block)] += a
            dk[lines, pl.ds(base, count)] += b
            dv[lines, pl.ds(base, count)] += c

    far_base = pl.multiple_of((1 - me // 2) * middle, middle)
    near_base = pl.multiple_of((me // 2) * middle, middle)

    @pl.loop(0, heads)
    def _(h):
        for copy in of_head(h):
            copy.wait()

        @pl.when(h < heads - 1)
        def _():
            for copy in of_head(h + 1):
                copy.start()

        @pl.when(h == heads - 1)
        def _():
            for key in ("stack", 3, 2, 1, 0, "x", "gm"):
                load[key].start()

        lines = pl.ds(pl.multiple_of(h * HD, UNIT), HD)
        row_dot[h] = jnp.sum(grad[lines].astype(F32) * ot[lines].astype(F32), axis=0, keepdims=True)
        nothing = jnp.zeros((HD, middle), F32)
        dq[lines, :middle] = nothing
        dk[lines, middle:] = nothing
        dv[lines, middle:] = nothing
        for i in range(middle // block):
            at = middle + i * block
            a, b, c = tile(h, 0, middle, at, False)
            dq[lines, at : at + block] = a
            dk[lines, :middle] = dk[lines, :middle] + b if i else b
            dv[lines, :middle] = dv[lines, :middle] + c if i else c
        corner(h, far_base)

        @pl.when(h == 0)
        def _():
            met(peers)
            for copy in firsts:
                copy.start()

    for copy in firsts:
        copy.wait()
    half_a[...] = (e_sum[:shared, pl.ds(keep, columns)] + near_a[...].astype(F32)).astype(BF16)
    second.start()

    def ready(x):
        here = pl.ds(place(x, rows), rows)
        for n, (src, factor) in enumerate(((dq, SCORE_SCALE), (dk, 1.0 / LOG2E), (dv, None))):
            value = src[:, here]
            value = (value if factor is None else value * factor).astype(BF16)
            grads[x, n * width : (n + 1) * width] = value
            grads[x, 3 * width + n * rank : 3 * width + (n + 1) * rank] = nn(
                rsel[n * rank : (n + 1) * rank], value
            ).astype(BF16)

    def adapters(x, starts=False):
        load[x].wait()
        here = pl.ds(place(x, rows), rows)
        for n in range(3):
            value = grads[x, n * width : (n + 1) * width]
            part = nt(low[n * rank : (n + 1) * rank, here], value)
            at = slice(n * SLOT, n * SLOT + width)
            raise_sum[:, at] = part if starts else raise_sum[:, at] + part
        part = nn(grads[x, 3 * width :], normed[x])
        lower_sum[...] = part if starts else lower_sum[...] + part

    half = rows // 2

    def through(x, r):
        return tn(grads[x, :, r * half : (r + 1) * half], stack[...])

    pair = [
        [
            send(
                to_near.at[n, pl.ds(r * half, half)], from_near.at[n, pl.ds(r * half, half)],
                g_sent.at[2 * n + r], g_got.at[2 * n + r], across(1),
            )
            for r in range(2)
        ]
        for n in range(2)
    ]
    far = [
        send(to_far.at[c], from_far.at[c], g_sent.at[4 + c], g_got.at[4 + c], across(2))
        for c in range(chunks)
    ]
    before = chunks // 2
    raise_sum[...] = jnp.zeros_like(raise_sum)
    ready(3)
    load["stack"].wait()
    for r in range(2):
        to_near[1, r * half : (r + 1) * half] = through(3, r).astype(BF16)
        pair[1][r].start()
    ready(2)
    for r in range(2):
        total = through(2, r)
        pair[1][r].wait()
        for c in range(r * chunks // 2, (r + 1) * chunks // 2):
            here = slice(c * step - r * half, (c + 1) * step - r * half)
            there = slice(c * step, (c + 1) * step)
            to_far[c] = (total[here] + from_near[1, there].astype(F32)).astype(BF16)
            if c < before:
                far[c].start()
    sums = (mine_b[0].astype(F32) + theirs_b[0].astype(F32)) + (
        theirs_b[1].astype(F32) + theirs_b[2].astype(F32)
    )
    mark = sel[6 * rank :, : SLOT - width].astype(F32)
    sums = jnp.concatenate([sums[:, : sums.shape[1] - mark.shape[1]], mark], axis=1)
    pack_a[shared : shared + rank] = sums[:, :columns].astype(BF16)
    pack_a[shared + rank :] = sums[:, columns:].astype(BF16)
    second.wait()
    pack_a[:shared] = (half_a[...].astype(F32) + far_a[...].astype(F32)).astype(BF16)
    stays[0].start()
    early.start()
    adapters(3, True)
    adapters(2)

    @pl.loop(0, heads)
    def _(h):
        corner(h, near_base)

    trade = [
        send(src.at[:, pl.ds(0, shared)], dst, e_sent.at[2 + n], e_got.at[2 + n], across(1))
        for n, (src, dst) in enumerate(((first_ref, first_other), (all_ref, other_ref)))
    ]
    ready(1)
    adapters(1)
    ready(0)
    adapters(0)

    whole_b[...] = lower_sum[...].astype(BF16)
    one = to_pair(whole_b, near_b, 0)
    one.start()
    pack_b[shared : shared + rank] = raise_sum[:, :columns].astype(BF16)
    pack_b[shared + rank :] = raise_sum[:, columns:].astype(BF16)
    ahead.start()
    early.pass_all()
    one.wait()
    half_b[...] = (lower_sum[:, pl.ds(keep, columns)] + near_b[...].astype(F32)).astype(BF16)
    two = send(half_b, far_b, e_sent.at[1], e_got.at[1], across(2))
    two.start()
    for c in range(before, chunks):
        far[c].start()
    for r in range(2):
        to_near[0, r * half : (r + 1) * half] = through(1, r).astype(BF16)
        pair[0][r].start()
    two.wait()
    pack_b[:shared] = (half_b[...].astype(F32) + far_b[...].astype(F32)).astype(BF16)
    stays[1].start()
    spread.start()
    ahead.pass_all()
    for r in range(2):
        ours[r * half : (r + 1) * half] = through(0, r)
    for r in range(2):
        here = slice(r * half, (r + 1) * half)
        pair[0][r].wait()
        ours[here] = ours[here] + from_near[0, here].astype(F32)
    load["x"].wait()
    load["gm"].wait()

    def conclude(c):
        here = slice(c * step, (c + 1) * step)
        far[c].wait()
        x = x_buf[here].astype(F32)
        factor = lax.rsqrt(jnp.mean(x * x, axis=-1, keepdims=True) + EPS)
        unit = x * factor
        grad_in = ours[here] + from_far[c].astype(F32)
        dot = jnp.mean(grad_in * unit, axis=-1, keepdims=True)
        out_ref[here] = (gm_buf[here] + factor * (grad_in - unit * dot)).astype(BF16)

    stays[0].wait()
    early.finish()
    trade[0].start()
    marked = pltpu.make_async_copy(
        first_ref.at[:, pl.ds(4 * rank, rank), pl.ds(columns - LANES, LANES)], marks, last.at[6]
    )
    marked.start()
    for c in range(chunks // 2):
        conclude(c)
    spread.pass_all()
    marked.wait()
    chosen = jnp.max(marks[...].astype(F32), axis=1).astype(jnp.int32)
    chosen_ref[...] = jnp.broadcast_to(chosen[:, LANES - 1 :], chosen.shape)
    conclude(chunks // 2)
    stays[1].wait()
    ahead.finish()
    spread.finish()
    trade[1].start()
    for c in range(chunks // 2 + 1, chunks):
        conclude(c)
    trade[0].wait()
    trade[1].wait()


def backward_call(dp_count, seg_row, sums, sel, low, rsel, columns, rows_of, lse, pieces, stack, x, gm):
    rows, depth = x.shape
    rank, width = rsel.shape[0] // 3, rsel.shape[1]
    heads = width // HD
    length = seg_row.shape[1]
    total = stack.shape[0]
    chunks = 8
    halves = pltpu.VMEM((3 * rank, depth // 2), BF16)
    lines = pltpu.VMEM((chunks, rows // chunks, depth), BF16)
    col = pltpu.VMEM((width, length), BF16)
    row = pltpu.VMEM((length, heads * LANES), BF16)
    total_t = pltpu.VMEM((width, length), F32)
    pack = (5 * rank, depth // 2)
    exchange = [pltpu.VMEM((3 * rank, depth), BF16), halves, halves, halves, pltpu.VMEM(pack, BF16)]
    return pl.pallas_call(
        functools.partial(backward_kernel, heads, dp_count),
        in_specs=[VMEM] * 5 + [ANY] * 14,
        out_specs=[VMEM, ANY, ANY, ANY, ANY, VMEM],
        scratch_shapes=[
            pltpu.VMEM((length, 8), jnp.int32), col, col, col, col, row, row,
            pltpu.VMEM((heads, 1, length), F32),
            pltpu.VMEM((heads, 1, length), F32),
            total_t, total_t, total_t,
            pltpu.VMEM((4, total, rows), BF16),
            pltpu.VMEM((4, rows, depth), BF16),
            pltpu.VMEM((total, depth), BF16),
            pltpu.VMEM((rows, depth), BF16),
            pltpu.VMEM((rows, depth), F32),
            pltpu.VMEM((rows, depth), F32),
            pltpu.VMEM((2, rows, depth), BF16),
            pltpu.VMEM((2, rows, depth), BF16),
            lines, lines,
            pltpu.VMEM((3 * rank, depth), F32),
            pltpu.VMEM((rank, depth), F32),
            *exchange, *exchange,
            pltpu.VMEM((4, rank, depth), BF16),
            pltpu.VMEM((3, rank, depth), BF16),
            pltpu.VMEM((dp_count, rank, LANES), BF16),
            DMA((6, heads)), DMA((4,)), DMA((4 + chunks,)), DMA((4 + chunks,)), DMA((9,)), DMA((9,)),
            DMA((7,)), *(Spread.sems(dp_count) * 3),
        ],
        out_shape=[
            jax.ShapeDtypeStruct((rows, depth), BF16),
            jax.ShapeDtypeStruct((dp_count, *pack), BF16),
            jax.ShapeDtypeStruct((dp_count, 3 * rank, depth // 2), BF16),
            jax.ShapeDtypeStruct((dp_count, *pack), BF16),
            jax.ShapeDtypeStruct((dp_count, 3 * rank, depth // 2), BF16),
            jax.ShapeDtypeStruct((dp_count, LANES), jnp.int32),
        ],
        compiler_params=talking(4),
        name="backward",
    )(seg_row, sums, sel, low, rsel, *columns, *rows_of, lse, *pieces, stack, x, gm)


def sets_kernel(
    chosen, first_hbm, first_other_hbm, second_hbm, second_other_hbm, act_in, grad_in, *rest
):
    outs, rest = rest[:12], rest[12:]
    act_out, grad_out, first, first_other, second, second_other, *rest = rest
    sums, (act, grad, loads, stores) = rest[:12], rest[12:]
    bring = [
        pltpu.make_async_copy(src, dst, loads.at[n])
        for n, (src, dst) in enumerate(
            (
                (first_hbm, first), (first_other_hbm, first_other),
                (act_in, act), (grad_in, grad),
                (second_hbm, second), (second_other_hbm, second_other),
            )
        )
    ]
    for copy in bring:
        copy.start()
    leave = [
        pltpu.make_async_copy(src, dst, stores.at[n])
        for n, (src, dst) in enumerate(
            (*zip(sums, outs), (act, act_out), (grad, grad_out))
        )
    ]
    rank = sums[0].shape[1]
    columns = first.shape[2]
    count = first.shape[0]
    parity = lax.rem(lax.axis_index("tensor"), 2)
    here = pl.ds(pl.multiple_of(parity * columns, columns), columns)
    there = pl.ds(pl.multiple_of((1 - parity) * columns, columns), columns)
    for ref in sums:
        ref[...] = jnp.zeros_like(ref)

    def add(group, pack, other):
        @pl.loop(0, count)
        def _(n):
            which = chosen[n, 0]
            for k in range(3):
                part = slice(k * rank, (k + 1) * rank)
                group[k][which, :, here] += pack[n, part].astype(F32)
                group[k][which, :, there] += other[n, part].astype(F32)
            thin = jnp.concatenate(
                [pack[n, 3 * rank : 4 * rank], pack[n, 4 * rank :]], axis=1
            ).astype(F32)
            for k in range(3):
                width = group[3 + k].shape[2]
                group[3 + k][which] += thin[:, k * SLOT : k * SLOT + width]

    bring[0].wait()
    bring[1].wait()
    add(sums[:6], first, first_other)
    for copy in leave[:6]:
        copy.start()
    for n in (0, 1):
        bring[2 + n].wait()
        leave[12 + n].start()
    bring[4].wait()
    bring[5].wait()
    add(sums[6:], second, second_other)
    for copy in leave[6:12]:
        copy.start()
    for copy in leave:
        copy.wait()


def sets_call(chosen, packs, results, sets, width):
    _, five, columns = packs[0].shape
    rank, depth = five // 5, 2 * columns
    full = jax.ShapeDtypeStruct((sets, rank, depth), F32)
    thin = jax.ShapeDtypeStruct((sets, rank, width), F32)
    shapes = [full, full, full, thin, thin, thin] * 2
    lines = [jax.ShapeDtypeStruct(r.shape, r.dtype) for r in results]
    return pl.pallas_call(
        sets_kernel,
        in_specs=[pl.BlockSpec(memory_space=pltpu.SMEM)] + [ANY] * 6,
        out_specs=[ANY] * 14,
        scratch_shapes=[pltpu.VMEM(p.shape, BF16) for p in packs]
        + [pltpu.VMEM(t.shape, t.dtype) for t in shapes + lines]
        + [DMA((6,)), DMA((14,))],
        out_shape=shapes + lines,
        compiler_params=params(),
        name="set_sums",
    )(chosen, *packs, *results)


def on_device(
    dp_count,
    tokens,
    segment_ids,
    adapter_choice,
    cotangent,
    weight_query,
    weight_key,
    weight_value,
    weight_output,
    weight_upward,
    weight_downward,
    query_lower,
    query_raise,
    key_lower,
    key_raise,
    value_lower,
    value_raise,
    output_lower,
    output_raise,
    upward_lower,
    upward_raise,
    downward_lower,
    downward_raise,
):
    x, g = tokens[0], cotangent[0]
    rows = x.shape[0]
    length = segment_ids.shape[1]
    sets = query_lower.shape[0]
    width = query_raise.shape[2]
    seg_row = segment_ids

    feed = (weight_output.T, weight_upward.T, weight_downward.T)
    (
        qt, kt, k, v, low, stack, own, near, far, cross, sel, rsel, w_near, w_far, w_cross, ot, lse, att,
    ) = front_call(
        dp_count,
        adapter_choice,
        x,
        (query_lower, key_lower, value_lower, output_raise, upward_lower, downward_raise),
        (output_lower, upward_raise, downward_lower, query_raise, key_raise, value_raise),
        (weight_query.T, weight_key.T, weight_value.T),
        feed,
        seg_row,
    )
    pieces = (own, near, far, cross)
    act, gm, grad, sums = middle_call(
        x, g, att, pieces, sel, feed, (w_near, w_far, w_cross), length
    )
    input_grad, first, first_other, second, second_other, chosen = backward_call(
        dp_count, seg_row, sums, sel, low, rsel, (qt, kt, ot, grad), (k, v), lse, pieces, stack, x, gm
    )
    *out, act, input_grad = sets_call(
        chosen, (first, first_other, second, second_other), (act, input_grad), sets, width
    )
    (out_raise_g, up_lower_g, down_raise_g, out_lower_g, up_raise_g, down_lower_g) = out[:6]
    (q_lower_g, k_lower_g, v_lower_g, q_raise_g, k_raise_g, v_raise_g) = out[6:12]
    return (
        act[None],
        input_grad[None],
        q_lower_g,
        q_raise_g,
        k_lower_g,
        k_raise_g,
        v_lower_g,
        v_raise_g,
        out_lower_g,
        out_raise_g,
        up_lower_g,
        up_raise_g,
        down_lower_g,
        down_raise_g,
    )


def solution(mesh):
    split = P(None, None, "tensor")
    rows = P("dp", "tensor", None)
    columns = P(None, "tensor")
    return jax.shard_map(
        functools.partial(on_device, mesh.shape["dp"]),
        mesh=mesh,
        in_specs=(rows, P("dp", None), P("dp"), rows)
        + (columns,) * 6
        + (P(), split) * 3
        + (split, P(), P(), split, split, P()),
        out_specs=(rows, rows)
        + (P(), split) * 3
        + (split, P(), P(), split, split, P()),
        check_vma=False,
    )
```

```python
import functools
import math

import jax
import jax.numpy as jnp
from jax import lax
from jax.experimental import pallas as pl
from jax.experimental.pallas import tpu as pltpu
from jax.sharding import PartitionSpec as P

HD = 80
LANES = 128
EPS = 1e-06
NEG = -1e30
F32 = jnp.float32
BF16 = jnp.bfloat16
VMEM_BYTES = 60 * 2**20
SCORE_SCALE = HD ** (-0.5)
LOG2E = math.log2(math.e)
SLOT = 384
UNIT = 16
MESH = pl.DeviceIdType.MESH

NT = (((1,), (1,)), ((), ()))
TN = (((0,), (0,)), ((), ()))


def nn(left, right):
    return jnp.dot(left, right, preferred_element_type=F32)


def nt(left, right):
    return lax.dot_general(left, right, NT, preferred_element_type=F32)


def tn(left, right):
    return lax.dot_general(left, right, TN, preferred_element_type=F32)


def params(**more):
    return pltpu.CompilerParams(vmem_limit_bytes=VMEM_BYTES, **more)


def talking(number):
    return params(collective_id=number, has_side_effects=True)


def whole(shape):
    return pl.BlockSpec(shape, lambda *_: (0,) * len(shape))


ANY = pl.BlockSpec(memory_space=pl.ANY)
VMEM = pl.BlockSpec(memory_space=pltpu.VMEM)
DMA = pltpu.SemaphoreType.DMA


def across(bit):
    return {"tensor": lax.axis_index("tensor") ^ bit}


def along(step, count):
    return {"dp": lax.rem(lax.axis_index("dp") + step, count)}


def hello(peers):
    for peer in peers:
        pl.semaphore_signal(
            pltpu.get_barrier_semaphore(), inc=1, device_id=peer, device_id_type=MESH
        )


def met(peers):
    pl.semaphore_wait(pltpu.get_barrier_semaphore(), len(peers))


def send(src, dst, send_sem, recv_sem, peer):
    return pltpu.make_async_remote_copy(
        src_ref=src, dst_ref=dst, send_sem=send_sem, recv_sem=recv_sem,
        device_id=peer, device_id_type=MESH,
    )


class Spread:
    def __init__(self, count, source, slot, sems):
        me = lax.axis_index("dp")
        sent, got, x_sent, x_got = sems
        self.ring = [{"dp": lax.rem(me + 2 * n, count)} for n in range(1, count // 2)]
        self.partner = {"dp": me + 1 - 2 * lax.rem(me, 2)}
        self.direct = [
            send(source, slot(me), sent.at[n], got.at[n], peer) for n, peer in enumerate(self.ring)
        ]
        self.own = send(source, slot(me), x_sent.at[0], x_got.at[0], self.partner)
        self.onward = []
        for n in range(1, count // 2):
            block = slot(lax.rem(me + count - 2 * n, count))
            self.onward.append(send(block, block, x_sent.at[n], x_got.at[n], self.partner))

    @staticmethod
    def sems(count):
        half = count // 2
        return [DMA((half - 1,)), DMA((half - 1,)), DMA((half,)), DMA((half,))]

    @property
    def peers(self):
        return [self.partner, *self.ring]

    def start(self):
        for copy in self.direct:
            copy.start()
        self.own.start()

    def pass_on(self, n):
        self.direct[n].wait_recv()
        self.onward[n].start()

    def pass_all(self):
        for n in range(len(self.direct)):
            self.pass_on(n)

    def finish(self):
        self.own.wait()
        for copy in self.onward:
            copy.wait()
        for copy in self.direct:
            copy.wait_send()


def place(bit, rows):
    return pl.multiple_of((lax.axis_index("tensor") ^ bit) * rows, rows)


def column_of(seg_row):
    return jnp.broadcast_to(seg_row[...], (8, seg_row.shape[1])).T


def front_kernel(
    heads, dp_count, choice, x_hbm, ql, kl, vl, orr, ul, dr, ol, ur, dl, qr, kr, vr, wq, wk, wv, wo, wu, wd,
    seg_row,
    qt_out, kt_out, k_out, v_out, low_out, stack_out, own_out, near_out, far_out, cross_out,
    sel_out, rsel_out, w_near, w_far_out, w_cross, ot_out, lse_out, att_out,
    x_buf, wide, thin, mine_0, mine_1, fetched_0, fetched_1, own, near, far, cross, stack, sel, rsel,
    qt, kt, vt, k, v, low, w_far, seg_col, acc, top_of, total_of, ot, lse,
    loads, unit_sems, w_sent, w_got, sent, got, local, a_sent, a_got, a_local, s_sent, s_got, *spread_sems,
):
    width = heads * HD
    rank = rsel.shape[0] // 3
    rows = x_buf.shape[0]
    half = rows // 2
    cuts = ((0, half), (half, rows // 4), (half + rows // 4, rows // 4 + rank))
    mine, fetched = (mine_0, mine_1), (fetched_0, fetched_1)
    shares_of = [ref.shape[0] for ref in fetched]
    begins = (0, dp_count * shares_of[0], dp_count * sum(shares_of))
    length = qt.shape[1]
    middle = length // 2
    me = lax.axis_index("dp")

    def slots(pile):
        return lambda n: w_far.at[
            pl.ds(pl.multiple_of(begins[pile] + n * shares_of[pile], UNIT), shares_of[pile])
        ]

    weights = [
        Spread(dp_count, fetched[pile], slots(pile), spread_sems[4 * pile : 4 * pile + 4])
        for pile in range(2)
    ]
    peers = [across(1), across(2), across(3)] + weights[0].peers
    hello(peers)

    per_weight = wo.shape[0] // UNIT

    pieces = []
    for pile in range(2):
        count = shares_of[pile] // UNIT
        for u in range(count):
            number = lax.rem(begins[pile] // UNIT + me * count + u, 3 * per_weight)
            pieces.append((mine[pile].at[pl.ds(u * UNIT, UNIT)], number, unit_sems.at[len(pieces)]))
    for dst, number, sem in pieces:
        for n, w in enumerate((wo, wu, wd)):

            @pl.when(number // per_weight == n)
            def _(dst=dst, number=number, sem=sem, n=n, w=w):
                at = pl.multiple_of((number - n * per_weight) * UNIT, UNIT)
                pltpu.make_async_copy(w.at[pl.ds(at, UNIT)], dst, sem).start()

    lines = [
        pltpu.make_async_copy(
            x_hbm.at[pl.ds(c * half, half)], x_buf.at[pl.ds(c * half, half)], loads.at[c]
        )
        for c in range(2)
    ]
    for copy in lines:
        copy.start()
    thins = [
        pltpu.make_async_copy(ref, thin.at[n], loads.at[2 + n])
        for n, ref in enumerate((ol, ur, dl, qr, kr, vr))
    ]
    wides = [
        pltpu.make_async_copy(ref, wide.at[n], loads.at[8 + n])
        for n, ref in enumerate((ql, kl, vl, orr, ul, dr))
    ]
    squares = [
        pltpu.make_async_copy(ref, stack.at[pl.ds(n * width, width)], loads.at[14 + n])
        for n, ref in enumerate((wq, wk, wv))
    ]
    for copy in (*thins, *wides, *squares):
        copy.start()

    def part(ref, c):
        return ref.at[pl.ds(*cuts[c])]

    parts = range(len(cuts))
    to_far = [send(part(own, c), part(far, c), sent.at[0, c], got.at[0, c], across(2)) for c in parts]
    to_near = [send(part(own, c), part(near, c), sent.at[1, c], got.at[1, c], across(1)) for c in parts]
    on = [send(part(far, c), part(cross, c), sent.at[2, c], got.at[2, c], across(1)) for c in parts]
    shares = [
        send(mine[n], fetched[n], w_sent.at[n], w_got.at[n], across(2)) for n in range(2)
    ]
    which = choice[0]
    for dst, number, sem in pieces:
        pltpu.make_async_copy(wo.at[pl.ds(0, UNIT)], dst, sem).wait()
    met(peers)
    shares[0].start()
    for c in range(2):
        here = slice(c * half, (c + 1) * half)
        lines[c].wait()
        x = x_buf[here].astype(F32)
        factor = lax.rsqrt(jnp.mean(x * x, axis=-1, keepdims=True) + EPS)
        own[here] = (x * factor).astype(BF16)
        if c == 1:
            own[rows:] = jnp.zeros((rank, own.shape[1]), BF16)
            for copy in thins:
                copy.wait()
            for n in range(3):
                own[rows:, n * SLOT : n * SLOT + width] = thin[n, which]
        for n in (0,) if c == 0 else parts[1:]:
            to_far[n].start()
            to_near[n].start()
    shares[1].start()

    pending = []

    def keep(src, dst):
        copy = pltpu.make_async_copy(src, dst, local.at[len(pending)])
        copy.start()
        pending.append(copy)

    keep(own, own_out)
    for copy in wides:
        copy.wait()
    for n in range(6):
        sel[n * rank : (n + 1) * rank] = wide[n, which]
    mark = jnp.full((rank, sel.shape[1]), which, jnp.int32).astype(F32)
    sel[6 * rank :] = mark.astype(BF16)
    keep(sel, sel_out)
    for n in range(3):
        rsel[n * rank : (n + 1) * rank] = thin[3 + n, which]
    keep(rsel, rsel_out)
    stack[3 * width :] = sel[: 3 * rank]
    for copy in squares:
        copy.wait()
    keep(stack, stack_out)

    def project(ref, bit, c):
        first, size = cuts[c][0], min(cuts[c][1], rows - cuts[c][0])
        block = ref[first : first + size]
        out = nt(stack[...], block)
        down = out[3 * width :].astype(BF16)
        here = pl.ds(pl.multiple_of(place(bit, rows) + first, LANES), size)
        low[:, here] = down
        for n, (col, row) in enumerate(((qt, None), (kt, k), (vt, v))):
            low_n = slice(n * rank, (n + 1) * rank)
            value = out[n * width : (n + 1) * width] + tn(rsel[low_n], down[low_n])
            if n == 0:
                value = value * (SCORE_SCALE * LOG2E)
            value = value.astype(BF16)
            col[:, here] = value
            if row is not None:
                for h in range(heads):
                    row[here, h * LANES : h * LANES + HD] = value[h * HD : (h + 1) * HD].T
        for src, dst in ((qt, qt_out), (kt, kt_out), (low, low_out)):
            keep(src.at[:, here], dst.at[:, here])
        for src, dst in ((k, k_out), (v, v_out)):
            keep(src.at[here], dst.at[here])

    seg_col[...] = column_of(seg_row)
    block = rows

    def of_head(h):
        lines = pl.ds(pl.multiple_of(h * HD, UNIT), HD)
        lanes = pl.ds(pl.multiple_of(h * LANES, LANES), LANES)
        return lines, lanes

    def attend(h, keys, count, queries, masked):
        lines, lanes = of_head(h)
        at, over = pl.ds(queries, block), pl.ds(keys, count)
        s = nn(k[over, lanes][:, :HD], qt[lines, at])
        ok = seg_col[over, :1] == seg_row[:, at]
        if masked:
            key = lax.broadcasted_iota(jnp.int32, (count, block), 0)
            ok = ok & (key <= lax.broadcasted_iota(jnp.int32, (count, block), 1) + (count - block))
        s = jnp.where(ok, s, NEG)
        top = jnp.max(s, axis=0, keepdims=True)
        p = jnp.exp2(s - top)
        return top, jnp.sum(p, axis=0, keepdims=True), nn(vt[lines, over], p.astype(BF16))

    def corner(h, base):
        lines, _ = of_head(h)
        for i in range(middle // block):
            queries = pl.multiple_of(base + i * block, block)
            top, total, out = attend(h, base, (i + 1) * block, queries, True)
            top_of[h, :, pl.ds(queries, block)] = top
            total_of[h, :, pl.ds(queries, block)] = total
            acc[lines, pl.ds(queries, block)] = out

    chip = lax.axis_index("tensor") // 2
    far_base = pl.multiple_of((1 - chip) * middle, middle)
    near_base = pl.multiple_of(chip * middle, middle)

    for c in parts:
        project(own, 0, c)
        if c == 0:
            shares[0].wait_recv()
            weights[0].start()
            keep(fetched[0], slots(0)(me))
    for c in parts:
        to_near[c].wait_recv()
        project(near, 1, c)
    keep(near, near_out)

    @pl.loop(0, heads)
    def _(h):
        corner(h, near_base)

    for c in parts:
        to_far[c].wait_recv()
        on[c].start()
        project(far, 2, c)
        on[c].wait_recv()
        project(cross, 3, c)
        if c == 0:
            weights[0].pass_all()
    shares[1].wait_recv()
    weights[1].start()
    keep(far, far_out)
    keep(cross, cross_out)
    keep(fetched[1], slots(1)(me))

    def piece(bit, head):
        src = ot.at[pl.ds(pl.multiple_of(head * HD, UNIT), HD), pl.ds(place(bit, rows), rows)]
        dst = att_out.at[pl.ds(pl.multiple_of(bit * width + head * HD, UNIT), HD)]
        if bit == 0:
            return pltpu.make_async_copy(src, dst, a_local.at[head])
        return send(src, dst, a_sent.at[bit - 1, head], a_got.at[bit - 1, head], across(bit))

    def region(ref, pile):
        return ref.at[pl.ds(begins[pile], begins[pile + 1] - begins[pile])]

    swaps = [
        send(w, w_near.at[pl.ds(n * width, width)], s_sent.at[n], s_got.at[n], across(1))
        for n, w in enumerate((wo, wu, wd))
    ] + [
        send(region(w_far, n), region(w_cross, n), s_sent.at[3 + n], s_got.at[3 + n], across(1))
        for n in range(2)
    ]
    saved = [
        pltpu.make_async_copy(region(w_far, n), region(w_far_out, n), a_local.at[heads + n])
        for n in range(2)
    ]
    for copy in pending:
        copy.wait()
    settled = len(pending)

    @pl.loop(0, heads)
    def _(h):
        lines, _ = of_head(h)
        corner(h, far_base)
        for i in range(middle // block):
            at = pl.ds(middle + i * block, block)
            top, total, out = attend(h, 0, middle, middle + i * block, False)
            before = top_of[h, :, at]
            high = jnp.maximum(before, top)
            left, right = jnp.exp2(before - high), jnp.exp2(top - high)
            top_of[h, :, at] = high
            total_of[h, :, at] = left * total_of[h, :, at] + right * total
            acc[lines, at] = left * acc[lines, at] + right * out
        ot[lines] = (acc[lines] / total_of[h]).astype(BF16)
        lse[h] = top_of[h] + jnp.log2(total_of[h])
        for bit in (2, 3, 1, 0):
            piece(bit, h).start()

        @pl.when(h == 0)
        def _():
            weights[0].finish()
            for copy in swaps[:4]:
                copy.start()
            saved[0].start()

        @pl.when(h == 1)
        def _():
            weights[1].pass_all()

        @pl.when(h == heads - 1)
        def _():
            weights[1].finish()
            swaps[4].start()
            saved[1].start()

    keep(ot, ot_out)
    keep(lse, lse_out)
    for copy in shares:
        copy.wait_send()
    for copy in (*to_far, *to_near, *on):
        copy.wait_send()
    for copy in (*swaps, *saved):
        copy.wait()

    @pl.loop(0, heads)
    def _(h):
        for bit in range(4):
            piece(bit, h).wait()

    for copy in pending[settled:]:
        copy.wait()


def front_call(dp_count, choice, x, wides, thins, weights, feed, seg_row):
    rows, depth = x.shape
    length = seg_row.shape[1]
    sets, rank, width = thins[0].shape
    heads = width // HD
    total = 3 * (width + rank)
    units = max(2, -(-3 * width // (UNIT * dp_count)))
    later = max(1, units // 4)
    shares = [pltpu.VMEM((n * UNIT, depth), BF16) for n in (units - later, later)]
    fetched = (dp_count * units * UNIT, depth)
    block = (rows + rank, depth)
    col, row, down = (width, length), (length, heads * LANES), (3 * rank, length)
    picked, raised = (7 * rank, depth), (3 * rank, width)

    def of(shape, dtype=BF16):
        return jax.ShapeDtypeStruct(shape, dtype)

    statistic = pltpu.VMEM((heads, 1, length), F32)
    return pl.pallas_call(
        functools.partial(front_kernel, heads, dp_count),
        in_specs=[pl.BlockSpec(memory_space=pltpu.SMEM)] + [ANY] * 19 + [VMEM],
        out_specs=[ANY] * 18,
        out_shape=[of(t) for t in (col, col, row, row, down, (total, depth), block, block, block, block)]
        + [of(t) for t in (picked, raised, (3 * width, depth), fetched, fetched, col)]
        + [of((heads, 1, length), F32), of((4 * width, rows))],
        scratch_shapes=[
            pltpu.VMEM((rows, depth), BF16),
            pltpu.VMEM((6, sets, rank, depth), BF16),
            pltpu.VMEM((6, sets, rank, width), BF16),
            *shares,
            *shares,
        ]
        + [pltpu.VMEM(block, BF16)] * 4
        + [pltpu.VMEM(t, BF16) for t in ((total, depth), picked, raised, col, col, col, row, row, down, fetched)]
        + [
            pltpu.VMEM((length, 8), jnp.int32), pltpu.VMEM(col, F32), statistic, statistic,
            pltpu.VMEM(col, BF16), statistic,
            DMA((17,)), DMA((units,)), DMA((2,)), DMA((2,)), DMA((3, 3)), DMA((3, 3)),
            DMA((4 + 12 * 5 + 3 + 2 + 2,)),
            DMA((3, heads)), DMA((3, heads)), DMA((heads + 2,)), DMA((5,)), DMA((5,)),
        ]
        + Spread.sems(dp_count) * 2,
        compiler_params=talking(0),
        name="front",
    )(choice, x, *wides, *thins, *weights, *feed, seg_row)


def own_half(half):
    parity = lax.rem(lax.axis_index("tensor"), 2)
    return pl.multiple_of(parity * half, half), pl.multiple_of((1 - parity) * half, half)


def middle_kernel(
    x_ref, g_ref, att_ref, s0, s1, s2, s3, sel, wo_own, wu_own, wd_own,
    w_near, w_far, w_cross,
    act_ref, gm_ref, grad_out, e_sum,
    wo, wu, wd, ol, ur, dl, gt,
    w_local, g_sent, g_got, g_local,
):
    width = wo_own.shape[0]
    rank = s0.shape[0]
    rows = x_ref.shape[0]
    half = rows // 2
    me = lax.axis_index("tensor")

    peers = [across(1), across(2), across(3)]
    hello(peers)
    weights = []
    for n, (own, dst) in enumerate(((wo_own, wo), (wu_own, wu), (wd_own, wd))):
        here = pl.ds(n * width, width)
        group = [
            pltpu.make_async_copy(src, dst.at[pl.ds(x * width, width)], w_local.at[n, x])
            for x, src in enumerate((own, w_near.at[here], w_far.at[here], w_cross.at[here]))
        ]
        for copy in group:
            copy.start()
        weights.append(group)

    def arrived(n):
        for copy in weights[n]:
            copy.wait()

    smalls = (s0, s1, s2, s3)
    for x, src in enumerate(smalls):
        for slot, dst in enumerate((ol, ur, dl)):
            dst[:, x * width : (x + 1) * width] = src[:, slot * SLOT : slot * SLOT + width].astype(F32)
    out_lower, up_raise, down_lower = (r[...].astype(BF16) for r in (ol, ur, dl))
    out_raise, up_lower, down_raise = (
        sel[n * rank : (n + 1) * rank] for n in (3, 4, 5)
    )

    back = {}
    for r in range(2):
        here = slice(r * half, (r + 1) * half)
        grad = g_ref[here]
        att = att_ref[:, here].astype(F32).T.astype(BF16)
        low_out = nt(att, out_lower).astype(BF16)
        grad_low_down = nt(grad, down_raise).astype(BF16)
        if r == 0:
            arrived(0)
        middle = x_ref[here].astype(F32) + (nn(att, wo[...]) + nn(low_out, out_raise))
        factor = lax.rsqrt(jnp.mean(middle * middle, axis=-1, keepdims=True) + EPS)
        unit = middle * factor
        normed = unit.astype(BF16)
        low_up = nt(normed, up_lower).astype(BF16)
        if r == 0:
            arrived(1)
        preact = nt(normed, wu[...]) + nn(low_up, up_raise)
        sigma = 1.0 / (1.0 + jnp.exp(-preact))
        active = (preact * sigma).astype(BF16)
        if r == 0:
            arrived(2)
        low_down = nt(active, down_lower).astype(BF16)
        grad_act = nt(grad, wd[...]) + nn(grad_low_down, down_lower)
        grad_pre = (grad_act * (sigma * (1.0 + preact * (1.0 - sigma)))).astype(BF16)
        grad_low_up = nt(grad_pre, up_raise).astype(BF16)
        grad_mid = nn(grad_pre, wu[...]) + nn(grad_low_up, up_lower)
        dot = jnp.mean(grad_mid * unit, axis=-1, keepdims=True)
        grad_middle = grad.astype(F32) + factor * (grad_mid - unit * dot)
        gm_ref[here] = grad_middle
        grad_attn = grad_middle.astype(BF16)
        grad_low_out = nt(out_raise, grad_attn).astype(BF16)
        if r == 0:
            met(peers)
        for x in (2, 3, 1, 0):
            value = nt(wo[x * width : (x + 1) * width], grad_attn)
            value = value + tn(smalls[x][:, :width], grad_low_out)
            gt[x, :, here] = value.astype(BF16)
            src = gt.at[x, :, pl.ds(r * half, half)]
            dst = grad_out.at[:, pl.ds(pl.multiple_of(me * rows + r * half, half), half)]
            if x:
                copy = send(src, dst, g_sent.at[x - 1, r], g_got.at[x - 1, r], across(x))
            else:
                copy = pltpu.make_async_copy(src, dst, g_local.at[r])
            copy.start()
            back[x, r] = copy
        act_ref[here] = (middle + (nn(active, wd[...]) + nn(low_down, down_raise))).astype(BF16)
        parts = [
            tn(low_out, grad_attn), tn(grad_low_up, normed), tn(low_down, grad),
            nn(grad_low_out, att), tn(low_up, grad_pre), tn(grad_low_down, active),
        ]
        for n, part in enumerate(parts):
            block = slice(n * rank, (n + 1) * rank)
            e_sum[block] = e_sum[block] + part if r else part

    for copy in back.values():
        copy.wait()


def middle_call(x, g, att, pieces, sel, weights, fetched, length):
    rows, depth = x.shape
    width = weights[0].shape[0]
    rank = sel.shape[0] // 7
    small = pl.BlockSpec((rank, depth), lambda c: (rows // rank, 0))
    square = pltpu.VMEM((4 * width, depth), BF16)
    thin = pltpu.VMEM((rank, depth), F32)
    sums = (6 * rank, depth)
    return pl.pallas_call(
        middle_kernel,
        grid=(1,),
        in_specs=[whole((rows, depth))] * 2 + [whole((4 * width, rows))] + [small] * 4
        + [whole(sel.shape)] + [ANY] * 6,
        out_specs=[whole((rows, depth))] * 2 + [ANY, whole(sums)],
        scratch_shapes=[
            square, square, square, thin, thin, thin,
            pltpu.VMEM((4, width, rows), BF16),
            DMA((3, 4)), DMA((3, 2)), DMA((3, 2)), DMA((2,)),
        ],
        out_shape=[
            jax.ShapeDtypeStruct((rows, depth), BF16),
            jax.ShapeDtypeStruct((rows, depth), F32),
            jax.ShapeDtypeStruct((width, length), BF16),
            jax.ShapeDtypeStruct(sums, F32),
        ],
        compiler_params=talking(3),
        name="feed_forward",
    )(x, g, att, *pieces, sel, *weights, *fetched)


def backward_kernel(
    heads, dp_count, seg_row, e_sum, sel, low, rsel,
    qt_hbm, kt_hbm, ot_hbm, grad_hbm, k_hbm, v_hbm, lse_hbm, p0, p1, p2, p3, stack_hbm, x_hbm, gm_hbm,
    out_ref, first_ref, first_other, all_ref, other_ref, chosen_ref,
    seg_col, qt, kt, ot, grad, k, v, lse, row_dot, dq, dk, dv,
    grads, normed, stack, x_buf, gm_buf, ours, to_near, from_near, to_far, from_far,
    lower_sum, raise_sum, whole_a, near_a, half_a, far_a, pack_a, whole_b, near_b, half_b, far_b, pack_b,
    mine_b, theirs_b, marks,
    head_sems, loads, g_sent, g_got, e_sent, e_got, last, *spread_sems,
):
    rank, width = rsel.shape[0] // 3, rsel.shape[1]
    length = qt.shape[1]
    rows = out_ref.shape[0]
    middle = length // 2
    chunks = from_far.shape[0]
    step = rows // chunks
    block = 256
    shared = 3 * rank
    me = lax.axis_index("tensor")
    mine = lax.axis_index("dp")
    early = Spread(dp_count, pack_a, lambda n: first_ref.at[n], spread_sems[:4])
    upper, under = pl.ds(0, shared), pl.ds(shared, 2 * rank)
    spread = Spread(dp_count, pack_b.at[upper], lambda n: all_ref.at[n, upper], spread_sems[4:8])
    ahead = Spread(dp_count, pack_b.at[under], lambda n: all_ref.at[n, under], spread_sems[8:])
    peers = [across(1), across(2), across(3)] + spread.peers
    hello(peers)

    def of_head(h):
        lines = pl.ds(pl.multiple_of(h * HD, UNIT), HD)
        lanes = pl.ds(pl.multiple_of(h * LANES, LANES), LANES)
        return [
            pltpu.make_async_copy(src.at[lines], dst.at[lines], head_sems.at[n, h])
            for n, (src, dst) in enumerate(((qt_hbm, qt), (kt_hbm, kt), (ot_hbm, ot), (grad_hbm, grad)))
        ] + [
            pltpu.make_async_copy(src.at[:, lanes], dst.at[:, lanes], head_sems.at[4 + n, h])
            for n, (src, dst) in enumerate(((k_hbm, k), (v_hbm, v)))
        ]

    load = {"lse": pltpu.make_async_copy(lse_hbm, lse, last.at[4])}
    load["lse"].start()

    for copy in of_head(0):
        copy.start()
    for x in range(4):
        load[x] = pltpu.make_async_copy((p0, p1, p2, p3)[x].at[pl.ds(0, rows)], normed.at[x], loads.at[x])
    load["stack"] = pltpu.make_async_copy(stack_hbm, stack, last.at[0])
    load["x"] = pltpu.make_async_copy(x_hbm, x_buf, last.at[1])
    load["gm"] = pltpu.make_async_copy(gm_hbm, gm_buf, last.at[2])
    seg_col[...] = column_of(seg_row)
    stays = [
        pltpu.make_async_copy(pack_a, first_ref.at[mine], last.at[5]),
        pltpu.make_async_copy(pack_b, all_ref.at[mine], last.at[3]),
    ]
    columns = half_b.shape[1]
    keep, give = own_half(columns)

    def to_pair(src, dst, n):
        return send(src.at[:, pl.ds(give, columns)], dst, e_sent.at[n], e_got.at[n], across(1))

    whole_a[...] = e_sum[:shared].astype(BF16)
    for x in range(4):
        mine_b[x] = jnp.zeros(mine_b.shape[1:], BF16)
        for slot in range(3):
            part = e_sum[(3 + slot) * rank : (4 + slot) * rank, x * width : (x + 1) * width]
            mine_b[x, :, slot * SLOT : slot * SLOT + width] = part.astype(BF16)
    firsts = [to_pair(whole_a, near_a, 4)] + [
        send(mine_b.at[x], theirs_b.at[x - 1], e_sent.at[5 + x], e_got.at[5 + x], across(x))
        for x in (1, 2, 3)
    ]
    second = send(half_a, far_a, e_sent.at[5], e_got.at[5], across(2))
    load["lse"].wait()

    def tile(h, keys, count, queries, masked):
        lines = pl.ds(pl.multiple_of(h * HD, UNIT), HD)
        lanes = pl.ds(pl.multiple_of(h * LANES, LANES), LANES)
        at = pl.ds(queries, block)
        over = pl.ds(keys, count)
        query, given = qt[lines, at], grad[lines, at]
        s = nn(k[over, lanes][:, :HD], query)
        dp = nn(v[over, lanes][:, :HD], given)
        ok = seg_col[over, :1] == seg_row[:, at]
        if masked:
            key = lax.broadcasted_iota(jnp.int32, (count, block), 0)
            place_of = lax.broadcasted_iota(jnp.int32, (count, block), 1) + (count - block)
            ok = ok & (key <= place_of)
        p = jnp.exp2(jnp.where(ok, s, NEG) - lse[h, :, at])
        ds = (p * (dp - row_dot[h, :, at])).astype(BF16)
        return nn(kt[lines, over], ds), nt(query, ds), nt(given, p.astype(BF16))

    def corner(h, base):
        lines = pl.ds(pl.multiple_of(h * HD, UNIT), HD)
        for i in range(middle // block):
            count = (i + 1) * block
            queries = pl.multiple_of(base + i * block, block)
            a, b, c = tile(h, base, count, queries, True)
            dq[lines, pl.ds(queries, block)] += a
            dk[lines, pl.ds(base, count)] += b
            dv[lines, pl.ds(base, count)] += c

    far_base = pl.multiple_of((1 - me // 2) * middle, middle)
    near_base = pl.multiple_of((me // 2) * middle, middle)

    @pl.loop(0, heads)
    def _(h):
        for copy in of_head(h):
            copy.wait()

        @pl.when(h < heads - 1)
        def _():
            for copy in of_head(h + 1):
                copy.start()

        @pl.when(h == heads - 1)
        def _():
            for key in ("stack", 3, 2, 1, 0, "x", "gm"):
                load[key].start()

        lines = pl.ds(pl.multiple_of(h * HD, UNIT), HD)
        row_dot[h] = jnp.sum(grad[lines].astype(F32) * ot[lines].astype(F32), axis=0, keepdims=True)
        nothing = jnp.zeros((HD, middle), F32)
        dq[lines, :middle] = nothing
        dk[lines, middle:] = nothing
        dv[lines, middle:] = nothing
        for i in range(middle // block):
            at = middle + i * block
            a, b, c = tile(h, 0, middle, at, False)
            dq[lines, at : at + block] = a
            dk[lines, :middle] = dk[lines, :middle] + b if i else b
            dv[lines, :middle] = dv[lines, :middle] + c if i else c
        corner(h, far_base)

        @pl.when(h == 0)
        def _():
            met(peers)
            for copy in firsts:
                copy.start()

    for copy in firsts:
        copy.wait()
    half_a[...] = (e_sum[:shared, pl.ds(keep, columns)] + near_a[...].astype(F32)).astype(BF16)
    second.start()

    def ready(x):
        here = pl.ds(place(x, rows), rows)
        for n, (src, factor) in enumerate(((dq, SCORE_SCALE), (dk, 1.0 / LOG2E), (dv, None))):
            value = src[:, here]
            value = (value if factor is None else value * factor).astype(BF16)
            grads[x, n * width : (n + 1) * width] = value
            grads[x, 3 * width + n * rank : 3 * width + (n + 1) * rank] = nn(
                rsel[n * rank : (n + 1) * rank], value
            ).astype(BF16)

    def adapters(x, starts=False):
        load[x].wait()
        here = pl.ds(place(x, rows), rows)
        for n in range(3):
            value = grads[x, n * width : (n + 1) * width]
            part = nt(low[n * rank : (n + 1) * rank, here], value)
            at = slice(n * SLOT, n * SLOT + width)
            raise_sum[:, at] = part if starts else raise_sum[:, at] + part
        part = nn(grads[x, 3 * width :], normed[x])
        lower_sum[...] = part if starts else lower_sum[...] + part

    half = rows // 2

    def through(x, r):
        return tn(grads[x, :, r * half : (r + 1) * half], stack[...])

    pair = [
        [
            send(
                to_near.at[n, pl.ds(r * half, half)], from_near.at[n, pl.ds(r * half, half)],
                g_sent.at[2 * n + r], g_got.at[2 * n + r], across(1),
            )
            for r in range(2)
        ]
        for n in range(2)
    ]
    far = [
        send(to_far.at[c], from_far.at[c], g_sent.at[4 + c], g_got.at[4 + c], across(2))
        for c in range(chunks)
    ]
    before = chunks // 2 - 1
    raise_sum[...] = jnp.zeros_like(raise_sum)
    ready(3)
    load["stack"].wait()
    for r in range(2):
        to_near[1, r * half : (r + 1) * half] = through(3, r).astype(BF16)
        pair[1][r].start()
    ready(2)
    for r in range(2):
        total = through(2, r)
        pair[1][r].wait()
        for c in range(r * chunks // 2, (r + 1) * chunks // 2):
            here = slice(c * step - r * half, (c + 1) * step - r * half)
            there = slice(c * step, (c + 1) * step)
            to_far[c] = (total[here] + from_near[1, there].astype(F32)).astype(BF16)
            if c < before:
                far[c].start()
    sums = (mine_b[0].astype(F32) + theirs_b[0].astype(F32)) + (
        theirs_b[1].astype(F32) + theirs_b[2].astype(F32)
    )
    mark = sel[6 * rank :, : SLOT - width].astype(F32)
    sums = jnp.concatenate([sums[:, : sums.shape[1] - mark.shape[1]], mark], axis=1)
    pack_a[shared : shared + rank] = sums[:, :columns].astype(BF16)
    pack_a[shared + rank :] = sums[:, columns:].astype(BF16)
    second.wait()
    pack_a[:shared] = (half_a[...].astype(F32) + far_a[...].astype(F32)).astype(BF16)
    stays[0].start()
    early.start()
    adapters(3, True)
    adapters(2)

    @pl.loop(0, heads)
    def _(h):
        corner(h, near_base)

    trade = [
        send(src.at[:, pl.ds(0, shared)], dst, e_sent.at[2 + n], e_got.at[2 + n], across(1))
        for n, (src, dst) in enumerate(((first_ref, first_other), (all_ref, other_ref)))
    ]
    ready(1)
    adapters(1)
    ready(0)
    adapters(0)

    whole_b[...] = lower_sum[...].astype(BF16)
    one = to_pair(whole_b, near_b, 0)
    one.start()
    pack_b[shared : shared + rank] = raise_sum[:, :columns].astype(BF16)
    pack_b[shared + rank :] = raise_sum[:, columns:].astype(BF16)
    ahead.start()
    early.pass_all()
    one.wait()
    half_b[...] = (lower_sum[:, pl.ds(keep, columns)] + near_b[...].astype(F32)).astype(BF16)
    two = send(half_b, far_b, e_sent.at[1], e_got.at[1], across(2))
    two.start()
    for c in range(before, chunks):
        far[c].start()
    for r in range(2):
        to_near[0, r * half : (r + 1) * half] = through(1, r).astype(BF16)
        pair[0][r].start()
    two.wait()
    pack_b[:shared] = (half_b[...].astype(F32) + far_b[...].astype(F32)).astype(BF16)
    stays[1].start()
    spread.start()
    ahead.pass_all()
    for r in range(2):
        ours[r * half : (r + 1) * half] = through(0, r)
    for r in range(2):
        here = slice(r * half, (r + 1) * half)
        pair[0][r].wait()
        ours[here] = ours[here] + from_near[0, here].astype(F32)
    load["x"].wait()
    load["gm"].wait()

    def conclude(c):
        here = slice(c * step, (c + 1) * step)
        far[c].wait()
        x = x_buf[here].astype(F32)
        factor = lax.rsqrt(jnp.mean(x * x, axis=-1, keepdims=True) + EPS)
        unit = x * factor
        grad_in = ours[here] + from_far[c].astype(F32)
        dot = jnp.mean(grad_in * unit, axis=-1, keepdims=True)
        out_ref[here] = (gm_buf[here] + factor * (grad_in - unit * dot)).astype(BF16)

    stays[0].wait()
    early.finish()
    trade[0].start()
    marked = pltpu.make_async_copy(
        first_ref.at[:, pl.ds(4 * rank, rank), pl.ds(columns - LANES, LANES)], marks, last.at[6]
    )
    marked.start()
    for c in range(chunks // 2):
        conclude(c)
    spread.pass_all()
    marked.wait()
    chosen = jnp.max(marks[...].astype(F32), axis=1).astype(jnp.int32)
    chosen_ref[...] = jnp.broadcast_to(chosen[:, LANES - 1 :], chosen.shape)
    conclude(chunks // 2)
    stays[1].wait()
    ahead.finish()
    spread.finish()
    trade[1].start()
    for c in range(chunks // 2 + 1, chunks):
        conclude(c)
    trade[0].wait()
    trade[1].wait()


def backward_call(dp_count, seg_row, sums, sel, low, rsel, columns, rows_of, lse, pieces, stack, x, gm):
    rows, depth = x.shape
    rank, width = rsel.shape[0] // 3, rsel.shape[1]
    heads = width // HD
    length = seg_row.shape[1]
    total = stack.shape[0]
    chunks = 8
    halves = pltpu.VMEM((3 * rank, depth // 2), BF16)
    lines = pltpu.VMEM((chunks, rows // chunks, depth), BF16)
    col = pltpu.VMEM((width, length), BF16)
    row = pltpu.VMEM((length, heads * LANES), BF16)
    total_t = pltpu.VMEM((width, length), F32)
    pack = (5 * rank, depth // 2)
    exchange = [pltpu.VMEM((3 * rank, depth), BF16), halves, halves, halves, pltpu.VMEM(pack, BF16)]
    return pl.pallas_call(
        functools.partial(backward_kernel, heads, dp_count),
        in_specs=[VMEM] * 5 + [ANY] * 14,
        out_specs=[VMEM, ANY, ANY, ANY, ANY, VMEM],
        scratch_shapes=[
            pltpu.VMEM((length, 8), jnp.int32), col, col, col, col, row, row,
            pltpu.VMEM((heads, 1, length), F32),
            pltpu.VMEM((heads, 1, length), F32),
            total_t, total_t, total_t,
            pltpu.VMEM((4, total, rows), BF16),
            pltpu.VMEM((4, rows, depth), BF16),
            pltpu.VMEM((total, depth), BF16),
            pltpu.VMEM((rows, depth), BF16),
            pltpu.VMEM((rows, depth), F32),
            pltpu.VMEM((rows, depth), F32),
            pltpu.VMEM((2, rows, depth), BF16),
            pltpu.VMEM((2, rows, depth), BF16),
            lines, lines,
            pltpu.VMEM((3 * rank, depth), F32),
            pltpu.VMEM((rank, depth), F32),
            *exchange, *exchange,
            pltpu.VMEM((4, rank, depth), BF16),
            pltpu.VMEM((3, rank, depth), BF16),
            pltpu.VMEM((dp_count, rank, LANES), BF16),
            DMA((6, heads)), DMA((4,)), DMA((4 + chunks,)), DMA((4 + chunks,)), DMA((9,)), DMA((9,)),
            DMA((7,)), *(Spread.sems(dp_count) * 3),
        ],
        out_shape=[
            jax.ShapeDtypeStruct((rows, depth), BF16),
            jax.ShapeDtypeStruct((dp_count, *pack), BF16),
            jax.ShapeDtypeStruct((dp_count, 3 * rank, depth // 2), BF16),
            jax.ShapeDtypeStruct((dp_count, *pack), BF16),
            jax.ShapeDtypeStruct((dp_count, 3 * rank, depth // 2), BF16),
            jax.ShapeDtypeStruct((dp_count, LANES), jnp.int32),
        ],
        compiler_params=talking(4),
        name="backward",
    )(seg_row, sums, sel, low, rsel, *columns, *rows_of, lse, *pieces, stack, x, gm)


def sets_kernel(
    chosen, first_hbm, first_other_hbm, second_hbm, second_other_hbm, act_in, grad_in, *rest
):
    outs, rest = rest[:12], rest[12:]
    act_out, grad_out, first, first_other, second, second_other, *rest = rest
    sums, (act, grad, loads, stores) = rest[:12], rest[12:]
    bring = [
        pltpu.make_async_copy(src, dst, loads.at[n])
        for n, (src, dst) in enumerate(
            (
                (first_hbm, first), (first_other_hbm, first_other),
                (act_in, act), (grad_in, grad),
                (second_hbm, second), (second_other_hbm, second_other),
            )
        )
    ]
    for copy in bring:
        copy.start()
    leave = [
        pltpu.make_async_copy(src, dst, stores.at[n])
        for n, (src, dst) in enumerate(
            (*zip(sums, outs), (act, act_out), (grad, grad_out))
        )
    ]
    rank = sums[0].shape[1]
    columns = first.shape[2]
    count = first.shape[0]
    parity = lax.rem(lax.axis_index("tensor"), 2)
    here = pl.ds(pl.multiple_of(parity * columns, columns), columns)
    there = pl.ds(pl.multiple_of((1 - parity) * columns, columns), columns)
    for ref in sums:
        ref[...] = jnp.zeros_like(ref)

    def add(group, pack, other):
        @pl.loop(0, count)
        def _(n):
            which = chosen[n, 0]
            for k in range(3):
                part = slice(k * rank, (k + 1) * rank)
                group[k][which, :, here] += pack[n, part].astype(F32)
                group[k][which, :, there] += other[n, part].astype(F32)
            thin = jnp.concatenate(
                [pack[n, 3 * rank : 4 * rank], pack[n, 4 * rank :]], axis=1
            ).astype(F32)
            for k in range(3):
                width = group[3 + k].shape[2]
                group[3 + k][which] += thin[:, k * SLOT : k * SLOT + width]

    bring[0].wait()
    bring[1].wait()
    add(sums[:6], first, first_other)
    for copy in leave[:6]:
        copy.start()
    for n in (0, 1):
        bring[2 + n].wait()
        leave[12 + n].start()
    bring[4].wait()
    bring[5].wait()
    add(sums[6:], second, second_other)
    for copy in leave[6:12]:
        copy.start()
    for copy in leave:
        copy.wait()


def sets_call(chosen, packs, results, sets, width):
    _, five, columns = packs[0].shape
    rank, depth = five // 5, 2 * columns
    full = jax.ShapeDtypeStruct((sets, rank, depth), F32)
    thin = jax.ShapeDtypeStruct((sets, rank, width), F32)
    shapes = [full, full, full, thin, thin, thin] * 2
    lines = [jax.ShapeDtypeStruct(r.shape, r.dtype) for r in results]
    return pl.pallas_call(
        sets_kernel,
        in_specs=[pl.BlockSpec(memory_space=pltpu.SMEM)] + [ANY] * 6,
        out_specs=[ANY] * 14,
        scratch_shapes=[pltpu.VMEM(p.shape, BF16) for p in packs]
        + [pltpu.VMEM(t.shape, t.dtype) for t in shapes + lines]
        + [DMA((6,)), DMA((14,))],
        out_shape=shapes + lines,
        compiler_params=params(),
        name="set_sums",
    )(chosen, *packs, *results)


def on_device(
    dp_count,
    tokens,
    segment_ids,
    adapter_choice,
    cotangent,
    weight_query,
    weight_key,
    weight_value,
    weight_output,
    weight_upward,
    weight_downward,
    query_lower,
    query_raise,
    key_lower,
    key_raise,
    value_lower,
    value_raise,
    output_lower,
    output_raise,
    upward_lower,
    upward_raise,
    downward_lower,
    downward_raise,
):
    x, g = tokens[0], cotangent[0]
    rows = x.shape[0]
    length = segment_ids.shape[1]
    sets = query_lower.shape[0]
    width = query_raise.shape[2]
    seg_row = segment_ids

    feed = (weight_output.T, weight_upward.T, weight_downward.T)
    (
        qt, kt, k, v, low, stack, own, near, far, cross, sel, rsel, w_near, w_far, w_cross, ot, lse, att,
    ) = front_call(
        dp_count,
        adapter_choice,
        x,
        (query_lower, key_lower, value_lower, output_raise, upward_lower, downward_raise),
        (output_lower, upward_raise, downward_lower, query_raise, key_raise, value_raise),
        (weight_query.T, weight_key.T, weight_value.T),
        feed,
        seg_row,
    )
    pieces = (own, near, far, cross)
    act, gm, grad, sums = middle_call(
        x, g, att, pieces, sel, feed, (w_near, w_far, w_cross), length
    )
    input_grad, first, first_other, second, second_other, chosen = backward_call(
        dp_count, seg_row, sums, sel, low, rsel, (qt, kt, ot, grad), (k, v), lse, pieces, stack, x, gm
    )
    *out, act, input_grad = sets_call(
        chosen, (first, first_other, second, second_other), (act, input_grad), sets, width
    )
    (out_raise_g, up_lower_g, down_raise_g, out_lower_g, up_raise_g, down_lower_g) = out[:6]
    (q_lower_g, k_lower_g, v_lower_g, q_raise_g, k_raise_g, v_raise_g) = out[6:12]
    return (
        act[None],
        input_grad[None],
        q_lower_g,
        q_raise_g,
        k_lower_g,
        k_raise_g,
        v_lower_g,
        v_raise_g,
        out_lower_g,
        out_raise_g,
        up_lower_g,
        up_raise_g,
        down_lower_g,
        down_raise_g,
    )


def solution(mesh):
    split = P(None, None, "tensor")
    rows = P("dp", "tensor", None)
    columns = P(None, "tensor")
    return jax.shard_map(
        functools.partial(on_device, mesh.shape["dp"]),
        mesh=mesh,
        in_specs=(rows, P("dp", None), P("dp"), rows)
        + (columns,) * 6
        + (P(), split) * 3
        + (split, P(), P(), split, split, P()),
        out_specs=(rows, rows)
        + (P(), split) * 3
        + (split, P(), P(), split, split, P()),
        check_vma=False,
    )
```
